128 devices in a mesh: section: 2 (over z_lo), dp: 8 (over x, z_hi), head: 8 (over y, core).
Axes of the slice: x: 4, y: 4, z: 4 (z_hi: 2, z_lo: 2; z = z_hi * 2 + z_lo), core: 2. Of those that a mesh axis runs over, the one named last changes fastest.
Arguments:
- images: bfloat16 [16, 1024, 1024], P('dp', 'head'), may hold values from -6 to 6
- key_mask: int32 [16, 1024], P('dp'), may hold values from 0 to 1, as said below
- image_order: int32 [16], P('dp'), may hold values from 0 to 15, as said below
- attn_norm_gain: bfloat16 [2, 1024], P('section', ('dp', 'head')), may hold values from 0.5 to 1.5
- attn_norm_bias: bfloat16 [2, 1024], P('section', ('dp', 'head')), may hold values from -0.625 to 0.625
- qkv_weight: bfloat16 [2, 1024, 3072], P('section', ('dp', 'head')), may hold values from -0.1875 to 0.1875
- query_bias: bfloat16 [2, 1024], P('section', ('dp', 'head')), may hold values from -0.625 to 0.625
- value_bias: bfloat16 [2, 1024], P('section', ('dp', 'head')), may hold values from -0.625 to 0.625
- proj_weight: bfloat16 [2, 1024, 1024], P('section', ('dp', 'head')), may hold values from -3.5 to 3.5
- proj_bias: bfloat16 [2, 1024], P('section', ('dp', 'head')), may hold values from -0.625 to 0.625
- attn_scale: bfloat16 [2, 1024], P('section', ('dp', 'head')), may hold values from 0.3984375 to 1.1953125
- mlp_norm_gain: bfloat16 [2, 1024], P('section', ('dp', 'head')), may hold values from 0.5 to 1.5
- mlp_norm_bias: bfloat16 [2, 1024], P('section', ('dp', 'head')), may hold values from -0.625 to 0.625
- fc1_weight: bfloat16 [2, 1024, 4096], P('section', ('dp', 'head')), may hold values from -0.1875 to 0.1875
- fc1_bias: bfloat16 [2, 4096], P('section', ('dp', 'head')), may hold values from -0.625 to 0.625
- fc2_weight: bfloat16 [2, 4096, 1024], P('section', ('dp', 'head')), may hold values from -0.09375 to 0.09375
- fc2_bias: bfloat16 [2, 1024], P('section', ('dp', 'head')), may hold values from -0.625 to 0.625
- mlp_scale: bfloat16 [2, 1024], P('section', ('dp', 'head')), may hold values from 0.3984375 to 1.1953125
- cotangent: bfloat16 [16, 1024, 1024], P('dp', 'head'), may hold values from -6 to 6
Outputs:
- layer_out: bfloat16 [2, 16, 1024, 1024], P('section', 'dp', 'head')
- input_grad: bfloat16 [2, 16, 1024, 1024], P('section', 'dp', 'head')
- grad_attn_norm_gain: float32 [2, 1024], P('section', ('dp', 'head'))
- grad_attn_norm_bias: float32 [2, 1024], P('section', ('dp', 'head'))
- grad_qkv_weight: float32 [2, 1024, 3072], P('section', ('dp', 'head'))
- grad_query_bias: float32 [2, 1024], P('section', ('dp', 'head'))
- grad_value_bias: float32 [2, 1024], P('section', ('dp', 'head'))
- grad_proj_weight: float32 [2, 1024, 1024], P('section', ('dp', 'head'))
- grad_proj_bias: float32 [2, 1024], P('section', ('dp', 'head'))
- grad_attn_scale: float32 [2, 1024], P('section', ('dp', 'head'))
- grad_mlp_norm_gain: float32 [2, 1024], P('section', ('dp', 'head'))
- grad_mlp_norm_bias: float32 [2, 1024], P('section', ('dp', 'head'))
- grad_fc1_weight: float32 [2, 1024, 4096], P('section', ('dp', 'head'))
- grad_fc1_bias: float32 [2, 4096], P('section', ('dp', 'head'))
- grad_fc2_weight: float32 [2, 4096, 1024], P('section', ('dp', 'head'))
- grad_fc2_bias: float32 [2, 1024], P('section', ('dp', 'head'))
- grad_mlp_scale: float32 [2, 1024], P('section', ('dp', 'head'))
The draws below stay inside these ranges and needn't reach their ends.
Inputs may be any that keep to these rules, and one draw needn't show every extreme that they name: `key_mask`: the ones of each image form a prefix of its 1024 tokens, its first token among them, and its zeros the rest. `image_order`: each aligned block of 2 entries, the images of one index of dp, is a permutation of that block's own positions; micro-batch k of that index takes the block's entries k * 1 to (k + 1) - 1.
All inputs are finite; a program needn't handle non-finite values.
Results may differ from the reference program's by a relative error of at most 0.022.
Values may be sent and summed in bfloat16 or wider, within the bound.
No kernel may reach another device: no remote copies, remote signals or barrier semaphores. Data moves between devices by JAX's collectives and lax.ppermute only.
A program may use at most 512 MiB of HBM per device.

```python
import math
import jax
import jax.numpy as jnp
from jax import lax

D = 1024
DH = 64
FF = 4096
SEQ = 1024
MICRO = 2
IMG = 1
SECTIONS = 2
BATCH = 16


def draw_key_mask(key, part):
    key = jax.random.fold_in(key, 11)
    padding = jax.random.randint(key, (BATCH, 1), 1, max(2, SEQ // 128) + 1)
    position = jnp.arange(SEQ, dtype=jnp.int32)[None, :]
    return (position < SEQ - padding).astype(jnp.int32)


def draw_image_order(key, part):
    key = jax.random.fold_in(key, 12)
    group_size = MICRO * IMG
    groups = BATCH // group_size
    keys_all = jax.random.split(key, groups)
    shuffled = jax.vmap(lambda one_key: jax.random.permutation(one_key, group_size))(keys_all)
    block_start = (jnp.arange(groups, dtype=jnp.int32) * group_size)[:, None]
    return (shuffled.astype(jnp.int32) + block_start).reshape(BATCH).astype(jnp.int32)


def block_scale(rng, dims, shards, smallest, largest):
    gain = 1.0
    for axis_at, parts in shards:
        heights = jax.random.uniform(jax.random.fold_in(jax.random.fold_in(rng, 6), axis_at), (parts,), jnp.float32, smallest / len(shards), largest / len(shards))
        gain = gain * jnp.repeat(jnp.exp(heights), dims[axis_at] // parts).reshape((-1,) + (1,) * (len(dims) - 1 - axis_at))
    return gain


def normal_values(rng, extent, width, limit, cuts=(), held_as=jnp.bfloat16):
    array = jax.random.normal(rng, extent, jnp.float32) * width
    if len(cuts) > 0:
        array = block_scale(rng, extent, cuts, -0.22, 0.18) * array
    return jnp.clip(array, min=-limit, max=limit).astype(held_as)


def setup_inputs(seed: int = 0) -> dict:
    arg_keys = jax.random.split(jax.random.key(seed), 20)
    images = normal_values(arg_keys[0], (BATCH, SEQ, D), 1.0, 6.0, ((0, 8), (1, 8)))
    key_mask = draw_key_mask(jax.random.fold_in(arg_keys[19], 71), 0)
    image_order = draw_image_order(jax.random.fold_in(arg_keys[19], 71), 0)
    attn_norm_gain = jnp.clip(1.0 + 0.1 * jax.random.normal(arg_keys[3], (SECTIONS, D), jnp.float32), 0.5, 1.5).astype(jnp.bfloat16)
    attn_norm_bias = normal_values(arg_keys[4], (SECTIONS, D), 0.1, 0.625, ((0, 2), (1, 64)))
    qkv_weight = normal_values(arg_keys[5], (SECTIONS, D, 3 * D), D ** -0.5, 0.1875, ((0, 2), (1, 64)))
    query_bias = normal_values(arg_keys[6], (SECTIONS, D), 0.1, 0.625, ((0, 2), (1, 64)))
    value_bias = normal_values(arg_keys[7], (SECTIONS, D), 0.1, 0.625, ((0, 2), (1, 64)))
    proj_weight = normal_values(arg_keys[8], (SECTIONS, D, D), (max(1, 3 * D // SEQ)) ** -0.5, 3.5, ((0, 2), (1, 64)))
    proj_bias = normal_values(arg_keys[9], (SECTIONS, D), 0.1, 0.625, ((0, 2), (1, 64)))
    attn_scale = jnp.clip(jnp.exp(math.log(1.1953125) - 1.0986123 * jax.random.uniform(arg_keys[10], (SECTIONS, D), jnp.float32) ** block_scale(arg_keys[10], (SECTIONS, D), ((0, 2), (1, 64)), -0.2, 0.2)), 0.3984375, 1.1953125).astype(jnp.bfloat16)
    mlp_norm_gain = jnp.clip(1.0 + 0.1 * jax.random.normal(arg_keys[11], (SECTIONS, D), jnp.float32), 0.5, 1.5).astype(jnp.bfloat16)
    mlp_norm_bias = normal_values(arg_keys[12], (SECTIONS, D), 0.1, 0.625, ((0, 2), (1, 64)))
    fc1_weight = normal_values(arg_keys[13], (SECTIONS, D, FF), D ** -0.5, 0.1875, ((0, 2), (1, 64)))
    fc1_bias = normal_values(arg_keys[14], (SECTIONS, FF), 0.1, 0.625, ((0, 2), (1, 64)))
    fc2_weight = normal_values(arg_keys[15], (SECTIONS, FF, D), FF ** -0.5, 0.09375, ((0, 2), (1, 64)))
    fc2_bias = normal_values(arg_keys[16], (SECTIONS, D), 0.1, 0.625, ((0, 2), (1, 64)))
    mlp_scale = jnp.clip(jnp.exp(math.log(1.1953125) - 1.0986123 * jax.random.uniform(arg_keys[17], (SECTIONS, D), jnp.float32) ** block_scale(arg_keys[17], (SECTIONS, D), ((0, 2), (1, 64)), -0.2, 0.2)), 0.3984375, 1.1953125).astype(jnp.bfloat16)
    cotangent = normal_values(arg_keys[18], (BATCH, SEQ, D), 1.0, 6.0, ((0, 8), (1, 8)))
    return {"images": images, "key_mask": key_mask, "image_order": image_order, "attn_norm_gain": attn_norm_gain, "attn_norm_bias": attn_norm_bias, "qkv_weight": qkv_weight, "query_bias": query_bias, "value_bias": value_bias, "proj_weight": proj_weight, "proj_bias": proj_bias, "attn_scale": attn_scale, "mlp_norm_gain": mlp_norm_gain, "mlp_norm_bias": mlp_norm_bias, "fc1_weight": fc1_weight, "fc1_bias": fc1_bias, "fc2_weight": fc2_weight, "fc2_bias": fc2_bias, "mlp_scale": mlp_scale, "cotangent": cotangent}


@jax.custom_vjp
def low(v):
    return lax.optimization_barrier(v.astype(jnp.bfloat16)).astype(jnp.float32)

@jax.custom_vjp
def low_back(v):
    return v

def low_keep(v):
    return (low(v), None)

def low_pass(kept, grad):
    return (grad,)

def back_keep(v):
    return (v, None)

def back_low(kept, grad):
    return (low(grad),)
low.defvjp(low_keep, low_pass)
low_back.defvjp(back_keep, back_low)
MASKED_SCORE = -1e+30
NORM_EPSILON = 1e-06
EXACT_PRODUCT = lax.Precision.HIGHEST

def layer_norm(tokens_in, norm_gain, norm_shift):
    centre = tokens_in - lax.optimization_barrier(jnp.mean(tokens_in, axis=-1, keepdims=True))
    scaled = centre * lax.rsqrt(lax.optimization_barrier(jnp.mean(centre * centre, axis=-1, keepdims=True)) + NORM_EPSILON)
    return scaled * norm_gain + norm_shift

def one_layer(tokens_in, valid_keys, weights):
    attn_gain, attn_shift, qkv_full, query_add, value_add, proj_full, proj_add, attn_layer, mlp_gain, mlp_shift, fc1_full, fc1_add, fc2_full, fc2_add, mlp_layer = weights
    seq_len, features = tokens_in.shape
    head_count = features // DH
    normed = low(layer_norm(tokens_in, attn_gain, attn_shift))
    qkv_add = jnp.concatenate([query_add, jnp.zeros_like(query_add), value_add])
    mixed_qkv = low_back(low(jnp.dot(normed, qkv_full, precision=EXACT_PRODUCT) + qkv_add))
    split_qkv = mixed_qkv.reshape(seq_len, 3, head_count, DH)
    scores = low_back(jnp.einsum('qhd,khd->hqk', split_qkv[:, 0], split_qkv[:, 1], precision=EXACT_PRODUCT) * DH ** (-0.5))
    scores = jnp.where(valid_keys[None, None, :] > 0, scores, MASKED_SCORE)
    attention = low(jnp.exp(scores - jax.nn.logsumexp(scores, axis=-1, keepdims=True)))
    mixed_heads = jnp.einsum('hqk,khd->qhd', attention, split_qkv[:, 2], precision=EXACT_PRODUCT).reshape(seq_len, features)
    mixed_heads = low_back(low(mixed_heads))
    branch = low_back(jnp.dot(mixed_heads, proj_full, precision=EXACT_PRODUCT)) + proj_add
    middle = tokens_in + attn_layer * branch
    normed_mid = low(layer_norm(middle, mlp_gain, mlp_shift))
    hidden = low_back(jnp.dot(normed_mid, fc1_full, precision=EXACT_PRODUCT)) + fc1_add
    active_units = low(jax.nn.gelu(hidden, approximate=False))
    mlp_out = low_back(jnp.dot(active_units, fc2_full, precision=EXACT_PRODUCT)) + fc2_add
    return middle + mlp_layer * mlp_out

def reference(images, key_mask, image_order, attn_norm_gain, attn_norm_bias, qkv_weight, query_bias, value_bias, proj_weight, proj_bias, attn_scale, mlp_norm_gain, mlp_norm_bias, fc1_weight, fc1_bias, fc2_weight, fc2_bias, mlp_scale, cotangent):
    weights = tuple((member.astype(jnp.float32) for member in (attn_norm_gain, attn_norm_bias, qkv_weight, query_bias, value_bias, proj_weight, proj_bias, attn_scale, mlp_norm_gain, mlp_norm_bias, fc1_weight, fc1_bias, fc2_weight, fc2_bias, mlp_scale)))
    inputs = images.astype(jnp.float32)
    probes = jnp.zeros(inputs.shape, jnp.float32)

    def forward(layer_inputs, layer_weights, probe_all):
        ordered = jnp.take(layer_inputs, image_order, axis=0)
        mask_rows = jnp.take(key_mask, image_order, axis=0)
        first_layer = tuple((member[0] for member in layer_weights))
        second_layer = tuple((member[1] for member in layer_weights))

        def per_image(item_group):
            tokens_in, valid_keys, probe_rows = item_group
            between = low_back(low(one_layer(tokens_in, valid_keys, first_layer))) + probe_rows
            return (one_layer(between, valid_keys, second_layer), between)
        return lax.map(jax.checkpoint(per_image), (ordered, mask_rows, probe_all))
    outputs, pullback = jax.vjp(forward, inputs, weights, probes)
    grad_inputs, grad_weights, grad_between = pullback((cotangent.astype(jnp.float32), jnp.zeros_like(outputs[1])))
    layer_out = jnp.stack([outputs[1], outputs[0]]).astype(jnp.bfloat16)
    input_grad = jnp.stack([grad_inputs, grad_between]).astype(jnp.bfloat16)
    return (layer_out, input_grad, grad_weights[0], grad_weights[1], grad_weights[2], grad_weights[3], grad_weights[4], grad_weights[5], grad_weights[6], grad_weights[7], grad_weights[8], grad_weights[9], grad_weights[10], grad_weights[11], grad_weights[12], grad_weights[13], grad_weights[14])
```

```python
import functools

import jax
import jax.numpy as jnp
from jax import lax
from jax.experimental import pallas as pl
from jax.experimental.pallas import tpu as pltpu
from jax.sharding import PartitionSpec as P

DH = 64
MASKED_SCORE = -1e30
NORM_EPSILON = 1e-06
ROOT_HALF = 0.7071067811865476
DENSITY_SCALE = 0.3989422804014327
SCORE_SCALE = DH ** (-0.5)
SLAB = 16
QUERY_ROWS = 256
VMEM_LIMIT = 60 * 1024 * 1024

(
    ATTN_GAIN,
    ATTN_SHIFT,
    QUERY_ADD,
    VALUE_ADD,
    PROJ_ADD,
    ATTN_LAYER,
    MLP_GAIN,
    MLP_SHIFT,
    FC2_ADD,
    MLP_LAYER,
) = range(10)
HIDDEN_ROW = 10
TABLE_ROWS = 16


def hop(block, axis, places):
    size = lax.axis_size(axis)
    return lax.ppermute(block, axis, [(i, (i + 2 * places) % size) for i in range(size)])


def swap(block, axis):
    size = lax.axis_size(axis)
    return lax.ppermute(block, axis, [(i, i ^ 1) for i in range(size)])


def coordinates():
    dp_index, head_index = lax.axis_index("dp"), lax.axis_index("head")
    return dp_index // 2, dp_index % 2, head_index // 2, head_index % 2


def spread(shard, last_axis):
    x_me, z_me, y_me, core_me = coordinates()
    x_size, y_size = lax.axis_size("dp") // 2, lax.axis_size("head") // 2
    across = swap(shard, "dp")
    pair = jnp.where(z_me == 0, jnp.stack([shard, across]), jnp.stack([across, shard]))
    zeros = (0,) * shard.ndim
    if last_axis == "dp":
        first_axis, first_me, first_size = "head", y_me, y_size
        last_me, last_size = x_me, x_size
        lane = jnp.zeros((2, y_size) + shard.shape, shard.dtype)
    else:
        first_axis, first_me, first_size = "dp", x_me, x_size
        last_me, last_size = y_me, y_size
        lane = jnp.zeros((x_size, 2) + shard.shape, shard.dtype)
    for places in range(first_size):
        came = pair if places == 0 else hop(pair, first_axis, places)
        source = (first_me - places) % first_size
        if last_axis == "dp":
            lane = lax.dynamic_update_slice(lane, came[:, None], (0, source) + zeros)
        else:
            lane = lax.dynamic_update_slice(lane, came[None], (source, 0) + zeros)
    whole = jnp.zeros((x_size, 2, y_size, 2) + shard.shape, shard.dtype)
    arrived = [
        lane if places == 0 else hop(lane, last_axis, places) for places in range(last_size)
    ]
    for places, came in enumerate(arrived):
        source = (last_me - places) % last_size
        for core, block in ((core_me, came), (1 - core_me, swap(came, "head"))):
            if last_axis == "dp":
                whole = lax.dynamic_update_slice(
                    whole, block[None, :, :, None], (source, 0, 0, core) + zeros
                )
            else:
                whole = lax.dynamic_update_slice(
                    whole, block[:, :, None, None], (0, 0, source, core) + zeros
                )
    return whole.reshape((x_size * 2 * y_size * 2,) + shard.shape)


def ring_sum(terms, axis, dim, me, size):
    own = lax.dynamic_index_in_dim(terms, me, dim, keepdims=False).astype(jnp.float32)
    for places in range(1, size):
        block = lax.dynamic_index_in_dim(terms, (me + places) % size, dim, keepdims=False)
        own = own + hop(block, axis, places).astype(jnp.float32)
    return own


def collect(mine, other, first_axis):
    x_me, z_me, y_me, core_me = coordinates()
    x_size, y_size = lax.axis_size("dp") // 2, lax.axis_size("head") // 2
    chip_sum = mine.astype(jnp.float32) + swap(other, "head").astype(jnp.float32)
    terms = chip_sum.astype(jnp.bfloat16).reshape((x_size, 2, y_size) + mine.shape[1:])
    if first_axis == "dp":
        terms = ring_sum(terms, "dp", 0, x_me, x_size).astype(jnp.bfloat16)
        terms = ring_sum(terms, "head", 1, y_me, y_size)
    else:
        terms = ring_sum(terms, "head", 2, y_me, y_size).astype(jnp.bfloat16)
        terms = ring_sum(terms, "dp", 0, x_me, x_size)
    away = lax.dynamic_index_in_dim(terms, 1 - z_me, 0, keepdims=False).astype(jnp.bfloat16)
    own = lax.dynamic_index_in_dim(terms, z_me, 0, keepdims=False)
    return own + swap(away, "dp").astype(jnp.float32)


def to_peers(blocks):
    return lax.all_to_all(blocks, "head", split_axis=0, concat_axis=0, tiled=True)


def shifted(block, distance):
    size = lax.axis_size("section")
    route = [(i, i + distance) for i in range(size) if 0 <= i + distance < size]
    return lax.ppermute(block, "section", route)


def norm_stats(rows):
    centre = rows - jnp.mean(rows, axis=-1, keepdims=True)
    inverse = lax.rsqrt(jnp.mean(centre * centre, axis=-1, keepdims=True) + NORM_EPSILON)
    return centre * inverse, inverse


def norm_back(grad_norm, scaled, inverse):
    first_mean = jnp.mean(grad_norm, axis=-1, keepdims=True)
    second_mean = jnp.mean(grad_norm * scaled, axis=-1, keepdims=True)
    return inverse * (grad_norm - first_mean - scaled * second_mean)


def product(left, right):
    return jnp.dot(left, right, preferred_element_type=jnp.float32)


def product_nt(left, right):
    return lax.dot_general(
        left, right, (((1,), (1,)), ((), ())), preferred_element_type=jnp.float32
    )


def product_tn(left, right):
    return lax.dot_general(
        left, right, (((0,), (0,)), ((), ())), preferred_element_type=jnp.float32
    )


def flat(block):
    return block.reshape(-1, block.shape[-1])


def column_sum(rows):
    return jnp.sum(rows, axis=0, keepdims=True)


def vector(table_ref, row):
    return table_ref[row : row + 1, :]


def side_by_side(blocks_ref, start=0):
    return jnp.concatenate(
        [blocks_ref[peer, :, start : start + 128] for peer in range(blocks_ref.shape[0])], axis=1
    )


def put_side_by_side(blocks_ref, rows, start=0):
    for peer in range(blocks_ref.shape[0]):
        blocks_ref[peer, :, start : start + 128] = rows[:, peer * 128 : (peer + 1) * 128].astype(
            blocks_ref.dtype
        )


def attn_normed(rows, table_ref):
    scaled, inverse = norm_stats(rows)
    normed = (scaled * vector(table_ref, ATTN_GAIN) + vector(table_ref, ATTN_SHIFT)).astype(
        jnp.bfloat16
    )
    return normed, scaled, inverse


def mlp_normed(middle, table_ref):
    scaled, inverse = norm_stats(middle)
    normed = (scaled * vector(table_ref, MLP_GAIN) + vector(table_ref, MLP_SHIFT)).astype(
        jnp.bfloat16
    )
    return normed, scaled, inverse


def cumulative(hidden):
    return 0.5 * (1.0 + lax.erf(hidden * ROOT_HALF))


def front_kernel(x_ref, table_ref, qk_ref, v_ref, out_ref):
    normed, _, _ = attn_normed(x_ref[...].astype(jnp.float32), table_ref)
    queries = product(normed, flat(qk_ref[:, :SLAB])) + vector(table_ref, QUERY_ADD)
    put_side_by_side(out_ref, queries, 0)
    put_side_by_side(out_ref, product(normed, flat(qk_ref[:, SLAB:])), 128)
    values = product(normed, flat(v_ref[...])) + vector(table_ref, VALUE_ADD)
    put_side_by_side(out_ref, values, 256)


def valid_rows(count, like):
    return lax.broadcasted_iota(jnp.int32, like.shape, 0) < count


def attend_kernel(count_ref, heads_ref, out_ref, lse_ref):
    count = count_ref[pl.program_id(0)]
    block = flat(heads_ref[:, 0])
    seq_len = block.shape[0]
    for start in range(0, seq_len, QUERY_ROWS):
        outs = []
        for head in range(2):
            low = head * DH
            keys = block[:, 128 + low : 128 + low + DH]
            values = block[:, 256 + low : 256 + low + DH]
            queries = block[start : start + QUERY_ROWS, low : low + DH]
            scores = product_nt(keys, queries)
            scores = jnp.where(valid_rows(count, scores), scores * SCORE_SCALE, MASKED_SCORE)
            largest = jnp.max(scores, axis=0, keepdims=True)
            weights = jnp.exp(scores - largest)
            total = jnp.sum(weights, axis=0, keepdims=True)
            mixed = product_tn(values, weights.astype(jnp.bfloat16)) / total
            outs.append(mixed.T)
            lse_ref[0, head : head + 1, start : start + QUERY_ROWS] = largest + jnp.log(total)
        rows = jnp.concatenate(outs, axis=1).astype(jnp.bfloat16)
        peers = QUERY_ROWS // 128
        out_ref[start // 128 : start // 128 + peers, 0] = rows.reshape(peers, 128, 128)


def attend_back_kernel(count_ref, grad_ref, heads_ref, lse_ref, out_ref):
    count = count_ref[pl.program_id(0)]
    block = flat(heads_ref[:, 0])
    grads = flat(grad_ref[:, 0])
    seq_len = block.shape[0]
    peers = QUERY_ROWS // 128
    key_sums = [jnp.zeros((seq_len, DH), jnp.float32) for _ in range(2)]
    value_sums = [jnp.zeros((seq_len, DH), jnp.float32) for _ in range(2)]
    for start in range(0, seq_len, QUERY_ROWS):
        outs = []
        for head in range(2):
            low = head * DH
            keys = block[:, 128 + low : 128 + low + DH]
            values = block[:, 256 + low : 256 + low + DH]
            queries = block[start : start + QUERY_ROWS, low : low + DH]
            grad_rows = grads[start : start + QUERY_ROWS, low : low + DH]
            lse = lse_ref[0, head : head + 1, start : start + QUERY_ROWS]
            scores = product_nt(keys, queries)
            scores = jnp.where(valid_rows(count, scores), scores * SCORE_SCALE, MASKED_SCORE)
            weights = jnp.exp(scores - lse)
            grad_weights = product_nt(values, grad_rows)
            dots = jnp.sum(weights * grad_weights, axis=0, keepdims=True)
            grad_scores = (weights * (grad_weights - dots)).astype(jnp.bfloat16)
            value_sums[head] += product(weights.astype(jnp.bfloat16), grad_rows)
            key_sums[head] += product(grad_scores, queries)
            outs.append((product_tn(keys, grad_scores) * SCORE_SCALE).T)
        rows = jnp.concatenate(outs, axis=1).astype(jnp.bfloat16)
        out_ref[start // 128 : start // 128 + peers, 0, :, :128] = rows.reshape(peers, 128, 128)
    key_rows = (jnp.concatenate(key_sums, axis=1) * SCORE_SCALE).astype(jnp.bfloat16)
    value_rows = jnp.concatenate(value_sums, axis=1).astype(jnp.bfloat16)
    out_ref[:, 0, :, 128:256] = key_rows.reshape(-1, 128, 128)
    out_ref[:, 0, :, 256:] = value_rows.reshape(-1, 128, 128)


def rear_kernel(keep, x_ref, attn_ref, table_ref, proj_ref, fc1_ref, fc2_ref, *rest):
    if keep:
        result_ref, branch_ref, hidden_ref, mlp_ref, normed, middle, total = rest
    else:
        result_ref, normed, middle, total = rest
    step = pl.program_id(0)

    @pl.when(step == 0)
    def _():
        branch = product(side_by_side(attn_ref), flat(proj_ref[...])) + vector(table_ref, PROJ_ADD)
        if keep:
            branch_ref[...] = branch
        middle[...] = x_ref[...].astype(jnp.float32) + vector(table_ref, ATTN_LAYER) * branch
        normed[...] = mlp_normed(middle[...], table_ref)[0]
        total[...] = jnp.broadcast_to(vector(table_ref, FC2_ADD), total.shape)

    hidden = product(normed[...], flat(fc1_ref[...])) + table_ref[pl.ds(HIDDEN_ROW + step, 1), :]
    if keep:
        hidden_ref[...] = hidden
    active = (hidden * cumulative(hidden)).astype(jnp.bfloat16)
    total[...] += product(active, flat(fc2_ref[...]))

    @pl.when(step == pl.num_programs(0) - 1)
    def _():
        if keep:
            mlp_ref[...] = total[...]
        result = middle[...] + vector(table_ref, MLP_LAYER) * total[...]
        result_ref[...] = result.astype(jnp.bfloat16)


def rear_back_kernel(
    keep,
    grad_ref,
    x_ref,
    branch_ref,
    hidden_ref,
    mlp_ref,
    table_ref,
    proj_ref,
    fc1_ref,
    fc2_ref,
    attn_grad_ref,
    middle_grad_ref,
    *rest,
):
    if keep:
        mlp_low_ref, hidden_low_ref, active_ref, normed_ref, branch_low_ref, sums_ref = rest[:6]
    mlp_low, total = rest[-2:]
    step = pl.program_id(0)

    @pl.when(step == 0)
    def _():
        grad_mlp = vector(table_ref, MLP_LAYER) * grad_ref[...].astype(jnp.float32)
        mlp_low[...] = grad_mlp.astype(jnp.bfloat16)
        total[...] = jnp.zeros_like(total)
        if keep:
            sums_ref[...] = jnp.zeros_like(sums_ref)
            sums_ref[FC2_ADD : FC2_ADD + 1, :] = column_sum(grad_mlp)
            mlp_low_ref[...] = mlp_low[...]

    hidden = hidden_ref[...]
    below = cumulative(hidden)
    slope = below + hidden * (jnp.exp(-0.5 * hidden * hidden) * DENSITY_SCALE)
    grad_hidden = product_nt(mlp_low[...], flat(fc2_ref[...])) * slope
    hidden_low = grad_hidden.astype(jnp.bfloat16)
    total[...] += product_nt(hidden_low, flat(fc1_ref[...]))
    if keep:
        sums_ref[pl.ds(HIDDEN_ROW + step, 1), :] = column_sum(grad_hidden)
        hidden_low_ref[...] = hidden_low
        active_ref[...] = (hidden * below).astype(jnp.bfloat16)

    @pl.when(step == pl.num_programs(0) - 1)
    def _():
        grad_rows = grad_ref[...].astype(jnp.float32)
        branch = branch_ref[...]
        middle = x_ref[...].astype(jnp.float32) + vector(table_ref, ATTN_LAYER) * branch
        normed, scaled, inverse = mlp_normed(middle, table_ref)
        grad_normed = total[...]
        grad_middle = grad_rows + norm_back(
            grad_normed * vector(table_ref, MLP_GAIN), scaled, inverse
        )
        middle_grad_ref[...] = grad_middle
        grad_branch = vector(table_ref, ATTN_LAYER) * grad_middle
        branch_low = grad_branch.astype(jnp.bfloat16)
        put_side_by_side(attn_grad_ref, product_nt(branch_low, flat(proj_ref[...])))
        if keep:
            normed_ref[...] = normed
            branch_low_ref[...] = branch_low
            for row, rows in (
                (MLP_LAYER, grad_rows * mlp_ref[...]),
                (MLP_GAIN, grad_normed * scaled),
                (MLP_SHIFT, grad_normed),
                (ATTN_LAYER, grad_middle * branch),
                (PROJ_ADD, grad_branch),
            ):
                sums_ref[row : row + 1, :] = column_sum(rows)


def front_back_kernel(keep, grad_ref, middle_grad_ref, x_ref, table_ref, qk_ref, v_ref, *rest):
    if keep:
        out_ref, sums_ref = rest
    else:
        (out_ref,) = rest
    queries, keys, values = (side_by_side(grad_ref, start) for start in (0, 128, 256))
    grad_normed = product_nt(queries, flat(qk_ref[:, :SLAB]))
    grad_normed += product_nt(keys, flat(qk_ref[:, SLAB:]))
    grad_normed += product_nt(values, flat(v_ref[...]))
    _, scaled, inverse = attn_normed(x_ref[...].astype(jnp.float32), table_ref)
    grad_input = middle_grad_ref[...] + norm_back(
        grad_normed * vector(table_ref, ATTN_GAIN), scaled, inverse
    )
    out_ref[...] = grad_input.astype(jnp.bfloat16)
    if keep:
        sums_ref[...] = jnp.zeros_like(sums_ref)
        for row, rows in (
            (ATTN_GAIN, grad_normed * scaled),
            (ATTN_SHIFT, grad_normed),
            (QUERY_ADD, queries.astype(jnp.float32)),
            (VALUE_ADD, values.astype(jnp.float32)),
        ):
            sums_ref[row : row + 1, :] = column_sum(rows)


def put_by_core(core, mine_ref, other_ref, rows, start, count):
    pairs = rows.astype(jnp.bfloat16).reshape(-1, 2, count, rows.shape[-1])
    first, second = pairs[:, 0], pairs[:, 1]
    here = core == 0
    mine_ref[:, start : start + count] = jnp.where(here, first, second)
    other_ref[:, start : start + count] = jnp.where(here, second, first)


def mlp_weights_kernel(
    core_ref,
    normed_ref,
    hidden_low_ref,
    active_ref,
    mlp_low_ref,
    fc1_mine_ref,
    fc1_other_ref,
    fc2_mine_ref,
    fc2_other_ref,
):
    core = core_ref[0]
    fc2_grad = product_tn(active_ref[...], mlp_low_ref[...])
    put_by_core(core, fc2_mine_ref, fc2_other_ref, fc2_grad, 0, fc2_mine_ref.shape[1])
    fc1_grad = product_tn(normed_ref[...], hidden_low_ref[...])
    put_by_core(core, fc1_mine_ref, fc1_other_ref, fc1_grad, 0, SLAB)


def attn_weights_kernel(
    core_ref,
    x_ref,
    table_ref,
    grad_ref,
    attn_ref,
    branch_low_ref,
    small_ref,
    first_mine_ref,
    first_other_ref,
    second_mine_ref,
    second_other_ref,
):
    core = core_ref[0]
    normed, _, _ = attn_normed(x_ref[...].astype(jnp.float32), table_ref)
    for at in range(2):
        grad = product_tn(normed, side_by_side(grad_ref, at * 128))
        put_by_core(core, first_mine_ref, first_other_ref, grad, at * SLAB, SLAB)
    grad = product_tn(normed, side_by_side(grad_ref, 256))
    put_by_core(core, second_mine_ref, second_other_ref, grad, 0, SLAB)
    grad = product_tn(side_by_side(attn_ref), branch_low_ref[...])
    put_by_core(core, second_mine_ref, second_other_ref, grad, SLAB, SLAB)
    put_by_core(core, second_mine_ref, second_other_ref, flat(small_ref[...]), 2 * SLAB, SLAB)


def like(*shape, dtype=jnp.bfloat16):
    return jax.ShapeDtypeStruct(shape, dtype)


def whole_block(array):
    ndim = len(array.shape)
    return pl.BlockSpec(array.shape, lambda *_: (0,) * ndim)


def params():
    return pltpu.CompilerParams(vmem_limit_bytes=VMEM_LIMIT)


SCALARS = pl.BlockSpec(memory_space=pltpu.SMEM)


def call_front(x, table, early):
    rows, width = x.shape
    devices = early[0].shape[0]
    return pl.pallas_call(
        front_kernel,
        grid=(1,),
        in_specs=[
            whole_block(x),
            whole_block(table),
            whole_block(early[0]),
            pl.BlockSpec((devices, SLAB, width), lambda i: (0, 0, 0)),
        ],
        out_specs=pl.BlockSpec((8, rows, 384), lambda i: (0, 0, 0)),
        out_shape=like(8, rows, 384),
        compiler_params=params(),
    )(x, table, *early)


def call_attend(counts, heads):
    images = counts.shape[0]
    heads = heads.reshape(8, images, -1, 384)
    tokens = heads.shape[2]
    out, lse = pl.pallas_call(
        attend_kernel,
        grid=(images,),
        in_specs=[SCALARS, pl.BlockSpec((8, 1, tokens, 384), lambda i: (0, i, 0, 0))],
        out_specs=[
            pl.BlockSpec((8, 1, tokens, 128), lambda i: (0, i, 0, 0)),
            pl.BlockSpec((1, 2, 8 * tokens), lambda i: (i, 0, 0)),
        ],
        out_shape=[
            like(8, images, tokens, 128),
            like(images, 2, 8 * tokens, dtype=jnp.float32),
        ],
        compiler_params=params(),
    )(counts, heads)
    return out.reshape(8, images * tokens, 128), lse


def call_attend_back(counts, grads, heads, lse):
    images = counts.shape[0]
    heads = heads.reshape(8, images, -1, 384)
    tokens = heads.shape[2]
    out = pl.pallas_call(
        attend_back_kernel,
        grid=(images,),
        in_specs=[
            SCALARS,
            pl.BlockSpec((8, 1, tokens, 128), lambda i: (0, i, 0, 0)),
            pl.BlockSpec((8, 1, tokens, 384), lambda i: (0, i, 0, 0)),
            pl.BlockSpec((1, 2, 8 * tokens), lambda i: (i, 0, 0)),
        ],
        out_specs=pl.BlockSpec((8, 1, tokens, 384), lambda i: (0, i, 0, 0)),
        out_shape=like(*heads.shape),
        compiler_params=params(),
    )(counts, grads.reshape(8, images, tokens, 128), heads, lse)
    return out.reshape(8, images * tokens, 384)


def rear_weight_specs(late):
    fc1, fc2_proj = late
    devices, _, width = fc1.shape
    fc2_rows = fc2_proj.shape[1] - SLAB
    steps = fc1.shape[1] // SLAB
    return steps, [
        pl.BlockSpec((devices, SLAB, width), lambda j: (0, fc2_rows // SLAB, 0)),
        pl.BlockSpec((devices, SLAB, width), lambda j: (0, j, 0)),
        pl.BlockSpec((devices // steps, fc2_rows, width), lambda j: (j, 0, 0)),
    ]


def call_rear(keep, x, attn, table, late):
    rows, width = x.shape
    steps, weight_specs = rear_weight_specs(late)
    full = like(rows, width, dtype=jnp.float32)
    column = pl.BlockSpec((rows, width), lambda j: (0, j))
    out_shape, out_specs = [like(rows, width)], [whole_block(x)]
    if keep:
        out_shape += [full, like(rows, steps * width, dtype=jnp.float32), full]
        out_specs += [whole_block(x), column, whole_block(x)]
    return pl.pallas_call(
        functools.partial(rear_kernel, keep),
        grid=(steps,),
        in_specs=[whole_block(x), whole_block(attn), whole_block(table)] + weight_specs,
        out_specs=out_specs,
        out_shape=out_shape,
        scratch_shapes=[
            pltpu.VMEM((rows, width), jnp.bfloat16),
            pltpu.VMEM((rows, width), jnp.float32),
            pltpu.VMEM((rows, width), jnp.float32),
        ],
        compiler_params=params(),
    )(x, attn, table, late[1], late[0], late[1])


def call_rear_back(keep, grad, x, branch, hidden, mlp, table, late):
    rows, width = x.shape
    steps, weight_specs = rear_weight_specs(late)
    column = pl.BlockSpec((rows, width), lambda j: (0, j))
    out_shape = [like(8, rows, 128), like(rows, width, dtype=jnp.float32)]
    out_specs = [pl.BlockSpec((8, rows, 128), lambda j: (0, 0, 0)), whole_block(x)]
    if keep:
        wide = like(rows, steps * width)
        out_shape += [like(rows, width), wide, wide, like(rows, width), like(rows, width)]
        out_specs += [whole_block(x), column, column, whole_block(x), whole_block(x)]
        out_shape += [like(*table.shape, dtype=jnp.float32)]
        out_specs += [whole_block(table)]
    return pl.pallas_call(
        functools.partial(rear_back_kernel, keep),
        grid=(steps,),
        in_specs=[
            whole_block(grad),
            whole_block(x),
            whole_block(branch),
            column,
            whole_block(mlp),
            whole_block(table),
        ]
        + weight_specs,
        out_specs=out_specs,
        out_shape=out_shape,
        scratch_shapes=[
            pltpu.VMEM((rows, width), jnp.bfloat16),
            pltpu.VMEM((rows, width), jnp.float32),
        ],
        compiler_params=params(),
    )(grad, x, branch, hidden, mlp, table, late[1], late[0], late[1])


def call_front_back(keep, grad_qkv, grad_middle, x, table, early):
    rows, width = x.shape
    devices = early[0].shape[0]
    out_shape, out_specs = [like(rows, width)], [whole_block(x)]
    if keep:
        out_shape += [like(*table.shape, dtype=jnp.float32)]
        out_specs += [whole_block(table)]
    return pl.pallas_call(
        functools.partial(front_back_kernel, keep),
        grid=(1,),
        in_specs=[
            whole_block(grad_qkv),
            whole_block(grad_middle),
            whole_block(x),
            whole_block(table),
            whole_block(early[0]),
            pl.BlockSpec((devices, SLAB, width), lambda i: (0, 0, 0)),
        ],
        out_specs=out_specs,
        out_shape=out_shape,
        compiler_params=params(),
    )(grad_qkv, grad_middle, x, table, *early)


def call_mlp_weights(core, normed, hidden_low, active, mlp_low, late):
    rows, width = normed.shape
    chips = late[0].shape[0] // 2
    steps = late[0].shape[1] // SLAB
    owned = late[0].shape[1]
    column = pl.BlockSpec((rows, width), lambda j: (0, j))
    fc1_spec = pl.BlockSpec((chips, SLAB, width), lambda j: (0, j, 0))
    fc2_spec = pl.BlockSpec((chips // steps, owned, width), lambda j: (j, 0, 0))
    return pl.pallas_call(
        mlp_weights_kernel,
        grid=(steps,),
        in_specs=[SCALARS, whole_block(normed), column, column, whole_block(mlp_low)],
        out_specs=[fc1_spec, fc1_spec, fc2_spec, fc2_spec],
        out_shape=[like(chips, owned, width)] * 4,
        compiler_params=params(),
    )(core, normed, hidden_low, active, mlp_low)


def call_attn_weights(core, x, table, grad_qkv, attn, branch_low, small):
    width = x.shape[1]
    chips = small.shape[0] // 2
    first, second = like(chips, 2 * SLAB, width), like(chips, 3 * SLAB, width)
    operands = (x, table, grad_qkv, attn, branch_low, small)
    return pl.pallas_call(
        attn_weights_kernel,
        grid=(1,),
        in_specs=[SCALARS] + [whole_block(operand) for operand in operands],
        out_specs=[whole_block(shape) for shape in (first, first, second, second)],
        out_shape=[first, first, second, second],
        compiler_params=params(),
    )(core, *operands)


def small_slab(vectors, hidden_vector):
    lead = vectors.shape[:-2]
    row = jnp.concatenate([vectors.reshape(lead + (-1,)), hidden_vector], axis=-1)
    return jnp.pad(
        row[..., None, :], [(0, 0)] * len(lead) + [(0, SLAB - 1), (0, 1024 - row.shape[-1])]
    )


def table_of(slabs):
    row = slabs[:, 0, :].astype(jnp.float32)
    vectors = row[:, : HIDDEN_ROW * SLAB].reshape(-1, HIDDEN_ROW, SLAB)
    vectors = vectors.transpose(1, 0, 2).reshape(HIDDEN_ROW, -1)
    start = HIDDEN_ROW * SLAB
    hidden = row[:, start : start + 64].reshape(-1, vectors.shape[1])
    return jnp.pad(
        jnp.concatenate([vectors, hidden]),
        [(0, TABLE_ROWS - HIDDEN_ROW - hidden.shape[0]), (0, 0)],
    )


def slabs_of(sums, devices):
    vectors = sums[:HIDDEN_ROW].reshape(HIDDEN_ROW, devices, SLAB).transpose(1, 0, 2)
    hidden = sums[HIDDEN_ROW : HIDDEN_ROW + 4].reshape(devices, -1)
    return small_slab(vectors, hidden).astype(jnp.bfloat16)


def column_slabs(rows):
    count = rows.shape[1] // 1024
    return rows.reshape(SLAB, count, 1024).transpose(1, 0, 2).reshape(count * SLAB, 1024)


def from_column_slabs(rows):
    count = rows.shape[0] // SLAB
    return rows.reshape(count, SLAB, 1024).transpose(1, 0, 2).reshape(SLAB, count * 1024)


def on_device(
    images,
    key_mask,
    image_order,
    attn_norm_gain,
    attn_norm_bias,
    qkv_weight,
    query_bias,
    value_bias,
    proj_weight,
    proj_bias,
    attn_scale,
    mlp_norm_gain,
    mlp_norm_bias,
    fc1_weight,
    fc1_bias,
    fc2_weight,
    fc2_bias,
    mlp_scale,
    cotangent,
):
    section_index = lax.axis_index("section")
    local_images, tokens_here, features = images.shape
    rows = local_images * tokens_here
    reversed_order = image_order[0] > image_order[1]
    core = (lax.axis_index("head") % 2).astype(jnp.int32).reshape(1)

    vectors = jnp.concatenate(
        [
            attn_norm_gain,
            attn_norm_bias,
            query_bias,
            value_bias,
            proj_bias,
            attn_scale,
            mlp_norm_gain,
            mlp_norm_bias,
            fc2_bias,
            mlp_scale,
        ]
    )
    qkv_slabs = column_slabs(qkv_weight[0])
    early = (
        spread(qkv_slabs[: 2 * SLAB], "dp"),
        spread(
            jnp.concatenate([qkv_slabs[2 * SLAB :], small_slab(vectors, fc1_bias[0])]), "head"
        ),
    )
    late = (
        spread(column_slabs(fc1_weight[0]), "dp"),
        spread(jnp.concatenate([fc2_weight[0], proj_weight[0]]), "head"),
    )
    table = table_of(early[1][:, SLAB:])
    devices = early[0].shape[0]

    own_images = jnp.where(reversed_order, images[::-1], images).reshape(rows, features)
    counts = jnp.sum(key_mask, axis=1, dtype=jnp.int32)
    counts = jnp.where(reversed_order, counts[::-1], counts)

    def forward(x, keep):
        heads = to_peers(call_front(x, table, early))
        attn_heads, lse = call_attend(counts, heads)
        attn = to_peers(attn_heads)
        return (heads, lse, attn), call_rear(keep, x, attn, table, late)

    def backward(grad, x, attn_state, rear_state, keep):
        heads, lse, _ = attn_state
        _, branch, hidden, mlp = rear_state
        rear = call_rear_back(keep, grad, x, branch, hidden, mlp, table, late)
        grad_heads = to_peers(rear[0])
        grad_qkv = to_peers(call_attend_back(counts, grad_heads, heads, lse))
        front = call_front_back(keep, grad_qkv, rear[1], x, table, early)
        return rear, grad_qkv, front

    _, (passed,) = forward(own_images, False)
    x = jnp.where(section_index == 0, own_images, shifted(passed, 1))
    attn_state, rear_state = forward(x, True)

    own_grad = cotangent.reshape(rows, features)
    _, _, (passed_back,) = backward(own_grad, x, attn_state, rear_state, False)
    grad = jnp.where(section_index == 0, shifted(passed_back, -1), own_grad)
    rear, grad_qkv, (input_grad, front_sums) = backward(grad, x, attn_state, rear_state, True)
    _, _, mlp_low, hidden_low, active, normed, branch_low, rear_sums = rear

    fc1_mine, fc1_other, fc2_mine, fc2_other = call_mlp_weights(
        core, normed, hidden_low, active, mlp_low, late
    )
    fc1_grad = collect(fc1_mine, fc1_other, "dp")
    fc2_grad = collect(fc2_mine, fc2_other, "head")
    small = slabs_of(rear_sums + front_sums, devices)
    first_mine, first_other, second_mine, second_other = call_attn_weights(
        core, x, table, grad_qkv, attn_state[2], branch_low, small
    )
    first_grad = collect(first_mine, first_other, "dp")
    second_grad = collect(second_mine, second_other, "head")
    qkv_grad = from_column_slabs(jnp.concatenate([first_grad, second_grad[:SLAB]]))
    proj_grad = second_grad[SLAB : 2 * SLAB]
    row = second_grad[2 * SLAB]
    small_grads = row[: HIDDEN_ROW * SLAB].reshape(HIDDEN_ROW, SLAB)
    fc1_bias_grad = row[HIDDEN_ROW * SLAB : HIDDEN_ROW * SLAB + 64]

    layer_out = rear_state[0].reshape(images.shape)
    input_grad = input_grad.reshape(images.shape)
    input_grad = jnp.where(
        (section_index == 0) & reversed_order, input_grad[::-1], input_grad
    )
    outs = (
        layer_out,
        input_grad,
        small_grads[ATTN_GAIN],
        small_grads[ATTN_SHIFT],
        qkv_grad,
        small_grads[QUERY_ADD],
        small_grads[VALUE_ADD],
        proj_grad,
        small_grads[PROJ_ADD],
        small_grads[ATTN_LAYER],
        small_grads[MLP_GAIN],
        small_grads[MLP_SHIFT],
        from_column_slabs(fc1_grad),
        fc1_bias_grad,
        fc2_grad,
        small_grads[FC2_ADD],
        small_grads[MLP_LAYER],
    )
    return tuple(member[None] for member in outs)


def solution(mesh):
    tokens = P("dp", "head", None)
    vec = P("section", ("dp", "head"))
    mat = P("section", ("dp", "head"), None)
    in_specs = (
        (tokens, P("dp", None), P("dp"), vec, vec, mat, vec, vec, mat, vec, vec, vec, vec)
        + (mat, vec, mat, vec, vec, tokens)
    )
    out_tokens = P("section", "dp", "head", None)
    out_specs = (
        (out_tokens, out_tokens, vec, vec, mat, vec, vec, mat, vec, vec, vec, vec, mat, vec)
        + (mat, vec, vec)
    )
    return jax.shard_map(
        on_device, mesh=mesh, in_specs=in_specs, out_specs=out_specs, check_vma=False
    )
```

```python
import functools

import jax
import jax.numpy as jnp
from jax import lax
from jax.experimental import pallas as pl
from jax.experimental.pallas import tpu as pltpu
from jax.sharding import PartitionSpec as P

DH = 64
MASKED_SCORE = -1e30
NORM_EPSILON = 1e-06
ROOT_HALF = 0.7071067811865476
DENSITY_SCALE = 0.3989422804014327
SCORE_SCALE = DH ** (-0.5)
SLAB = 16
SMALL_WIDTH = 512
QUERY_ROWS = 256
VMEM_LIMIT = 60 * 1024 * 1024

(
    ATTN_GAIN,
    ATTN_SHIFT,
    QUERY_ADD,
    VALUE_ADD,
    PROJ_ADD,
    ATTN_LAYER,
    MLP_GAIN,
    MLP_SHIFT,
    FC2_ADD,
    MLP_LAYER,
) = range(10)
HIDDEN_ROW = 10
TABLE_ROWS = 16


def hop(block, axis, places):
    size = lax.axis_size(axis)
    return lax.ppermute(block, axis, [(i, (i + 2 * places) % size) for i in range(size)])


def swap(block, axis):
    size = lax.axis_size(axis)
    return lax.ppermute(block, axis, [(i, i ^ 1) for i in range(size)])


def coordinates():
    dp_index, head_index = lax.axis_index("dp"), lax.axis_index("head")
    return dp_index // 2, dp_index % 2, head_index // 2, head_index % 2


def after(value, *others):
    return lax.optimization_barrier((value,) + others)[0]


def blank(shape, given):
    def kernel(given_ref, out_ref):
        pass

    anywhere = pl.BlockSpec(memory_space=pl.ANY)
    return pl.pallas_call(
        kernel,
        in_specs=[anywhere],
        out_specs=anywhere,
        out_shape=jax.ShapeDtypeStruct(shape, given.dtype),
    )(given)


def by_core(core, mine, other, axis):
    return jnp.where(
        core == 0,
        jnp.concatenate([mine, other], axis=axis),
        jnp.concatenate([other, mine], axis=axis),
    )


def spread_chip(shard):
    _, z_me, _, core_me = coordinates()
    half = shard.shape[1] // 2
    first, second = shard[:, :half], shard[:, half:]
    mine = jnp.where(core_me == 0, first, second)[None]
    cores = by_core(core_me, mine, swap(jnp.where(core_me == 0, second, first), "head")[None], 0)
    return by_core(z_me, cores[None], swap(cores, "dp")[None], 0)


def spread_lane(pair, last_axis):
    x_me, _, y_me, _ = coordinates()
    x_size, y_size = lax.axis_size("dp") // 2, lax.axis_size("head") // 2
    shape = pair.shape[1:]
    zeros = (0,) * len(shape)
    along_y = last_axis == "dp"
    axis, me, size = ("head", y_me, y_size) if along_y else ("dp", x_me, x_size)
    lane = blank(((2, size) if along_y else (size, 2)) + shape, pair)
    for places in range(size):
        came = pair if places == 0 else hop(pair, axis, places)
        source = (me - places) % size
        if along_y:
            lane = lax.dynamic_update_slice(lane, came[:, None], (0, source) + zeros)
        else:
            lane = lax.dynamic_update_slice(lane, came[None], (source, 0) + zeros)
    return lane


def spread_ends(lane, last_axis):
    return hop(lane, last_axis, 1), hop(lane, last_axis, -1)


def spread_rest(lane, ends, last_axis):
    x_me, _, y_me, _ = coordinates()
    x_size, y_size = lax.axis_size("dp") // 2, lax.axis_size("head") // 2
    along_x = last_axis == "dp"
    me, size = (x_me, x_size) if along_x else (y_me, y_size)
    low, high = ends
    half = lane.shape[0] // 2
    far = (hop(low[:half], last_axis, 1), hop(high[half:], last_axis, -1))
    shape = lane.shape[2:]
    zeros = (0,) * len(shape)
    near = blank((x_size, 2, y_size) + shape, lane)
    for places, at, block in (
        (0, 0, lane),
        (1, 0, low),
        (-1, 0, high),
        (2, 0, far[0]),
        (2, half, far[1]),
    ):
        source = (me - places) % size
        if along_x:
            near = lax.dynamic_update_slice(near, block[None], (source, at, 0) + zeros)
        else:
            near = lax.dynamic_update_slice(near, block[:, :, None], (at, 0, source) + zeros)
    near = near.reshape((-1,) + shape[1:])
    return near, swap(near, "head")


def piece(terms, at, dim):
    return lax.dynamic_index_in_dim(terms, at, dim, keepdims=False)


def core_sum(mine, other):
    x_size, y_size = lax.axis_size("dp") // 2, lax.axis_size("head") // 2
    total = mine.astype(jnp.float32) + swap(other, "head").astype(jnp.float32)
    return total.astype(jnp.bfloat16).reshape((x_size, 2, y_size, 2) + mine.shape[1:])


def ring_halves(terms, axis):
    x_me, _, y_me, _ = coordinates()
    dim, me, size = (0, x_me, 4) if axis == "dp" else (2, y_me, 4)
    far = piece(terms, (me + 2) % size, dim)
    half = far.shape[0] // 2
    return hop(far[:half], axis, 1), hop(far[half:], axis, -1)


def ring_rest(terms, halves, axis):
    x_me, _, y_me, _ = coordinates()
    dim, me, size = (0, x_me, 4) if axis == "dp" else (2, y_me, 4)
    low, high = (part.astype(jnp.float32) for part in halves)
    up = piece(terms, (me + 1) % size, dim).astype(jnp.float32)
    down = piece(terms, (me - 1) % size, dim).astype(jnp.float32)
    half = up.shape[0] // 2
    up = jnp.concatenate([up[:half] + low, up[half:]]).astype(jnp.bfloat16)
    down = jnp.concatenate([down[:half], down[half:] + high]).astype(jnp.bfloat16)
    total = piece(terms, me, dim).astype(jnp.float32)
    total = total + hop(up, axis, 1).astype(jnp.float32)
    return total + hop(down, axis, -1).astype(jnp.float32)


def ring_direct(terms, axis, dim, me):
    own = piece(terms, me, dim).astype(jnp.float32)
    for places in (1, 2, 3):
        own = own + hop(piece(terms, (me + places) % 4, dim), axis, places).astype(jnp.float32)
    return own


def second_ring(terms, first_axis):
    x_me, _, y_me, _ = coordinates()
    terms = terms.astype(jnp.bfloat16)
    if first_axis == "dp":
        return ring_direct(terms, "head", 1, y_me)
    return ring_direct(terms, "dp", 0, x_me)


def collect_rest(terms):
    _, z_me, _, core_me = coordinates()
    away = piece(terms, 1 - z_me, 0).astype(jnp.bfloat16)
    cores = piece(terms, z_me, 0) + swap(away, "dp").astype(jnp.float32)
    got = swap(piece(cores, 1 - core_me, 0).astype(jnp.bfloat16), "head").astype(jnp.float32)
    return by_core(core_me, piece(cores, core_me, 0), got, 1)


def to_peers(blocks):
    return lax.all_to_all(blocks, "head", split_axis=0, concat_axis=0, tiled=True)


def shifted(block, distance):
    size = lax.axis_size("section")
    route = [(i, i + distance) for i in range(size) if 0 <= i + distance < size]
    return lax.ppermute(block, "section", route)


def norm_stats(rows):
    centre = rows - jnp.mean(rows, axis=-1, keepdims=True)
    inverse = lax.rsqrt(jnp.mean(centre * centre, axis=-1, keepdims=True) + NORM_EPSILON)
    return centre * inverse, inverse


def norm_back(grad_norm, scaled, inverse):
    first_mean = jnp.mean(grad_norm, axis=-1, keepdims=True)
    second_mean = jnp.mean(grad_norm * scaled, axis=-1, keepdims=True)
    return inverse * (grad_norm - first_mean - scaled * second_mean)


def product(left, right):
    return jnp.dot(left, right, preferred_element_type=jnp.float32)


def product_nt(left, right):
    return lax.dot_general(
        left, right, (((1,), (1,)), ((), ())), preferred_element_type=jnp.float32
    )


def product_tn(left, right):
    return lax.dot_general(
        left, right, (((0,), (0,)), ((), ())), preferred_element_type=jnp.float32
    )


def flat(block):
    return block.reshape(-1, block.shape[-1])


def column_sum(rows):
    return jnp.sum(rows, axis=0, keepdims=True)


def vector(table_ref, row):
    return table_ref[row : row + 1, :]


def side_by_side(blocks_ref, start=0, first=0, count=8):
    return jnp.concatenate(
        [blocks_ref[first + peer, :, start : start + 128] for peer in range(count)], axis=1
    )


def put_side_by_side(blocks_ref, rows, start=0, first=0):
    for peer in range(rows.shape[1] // 128):
        blocks_ref[first + peer, :, start : start + 128] = rows[
            :, peer * 128 : (peer + 1) * 128
        ].astype(blocks_ref.dtype)


def halves(core, rows):
    half = rows.shape[1] // 2
    first, second = rows[:, :half], rows[:, half:]
    return jnp.where(core == 0, first, second), jnp.where(core == 0, second, first)


def attn_normed(rows, table_ref):
    scaled, inverse = norm_stats(rows)
    normed = (scaled * vector(table_ref, ATTN_GAIN) + vector(table_ref, ATTN_SHIFT)).astype(
        jnp.bfloat16
    )
    return normed, scaled, inverse


def mlp_normed(middle, table_ref):
    scaled, inverse = norm_stats(middle)
    normed = (scaled * vector(table_ref, MLP_GAIN) + vector(table_ref, MLP_SHIFT)).astype(
        jnp.bfloat16
    )
    return normed, scaled, inverse


def cumulative(hidden):
    return 0.5 * (1.0 + lax.erf(hidden * ROOT_HALF))


def front_kernel(
    core_ref, x_ref, table_ref, qk_mine_ref, v_mine_ref, qk_other_ref, v_other_ref, out_ref
):
    core = core_ref[0]
    normed, _, _ = attn_normed(x_ref[...].astype(jnp.float32), table_ref)
    query_adds = halves(core, vector(table_ref, QUERY_ADD))
    value_adds = halves(core, vector(table_ref, VALUE_ADD))
    for at, (qk_ref, v_ref) in enumerate(
        ((qk_mine_ref, v_mine_ref), (qk_other_ref, v_other_ref))
    ):
        first = (core if at == 0 else 1 - core) * 4
        queries = product(normed, flat(qk_ref[:, :SLAB])) + query_adds[at]
        put_side_by_side(out_ref, queries, 0, first)
        put_side_by_side(out_ref, product(normed, flat(qk_ref[:, SLAB:])), 128, first)
        values = product(normed, flat(v_ref[...])) + value_adds[at]
        put_side_by_side(out_ref, values, 256, first)


def valid_rows(count, like):
    return lax.broadcasted_iota(jnp.int32, like.shape, 0) < count


def attend_kernel(count_ref, heads_ref, out_ref, lse_ref):
    count = count_ref[pl.program_id(0)]
    block = flat(heads_ref[:, 0])
    seq_len = block.shape[0]
    for start in range(0, seq_len, QUERY_ROWS):
        outs = []
        for head in range(2):
            low = head * DH
            keys = block[:, 128 + low : 128 + low + DH]
            values = block[:, 256 + low : 256 + low + DH]
            queries = block[start : start + QUERY_ROWS, low : low + DH]
            scores = product_nt(keys, queries)
            scores = jnp.where(valid_rows(count, scores), scores * SCORE_SCALE, MASKED_SCORE)
            largest = jnp.max(scores, axis=0, keepdims=True)
            weights = jnp.exp(scores - largest)
            total = jnp.sum(weights, axis=0, keepdims=True)
            mixed = product_tn(values, weights.astype(jnp.bfloat16)) / total
            outs.append(mixed.T)
            lse_ref[0, head : head + 1, start : start + QUERY_ROWS] = largest + jnp.log(total)
        rows = jnp.concatenate(outs, axis=1).astype(jnp.bfloat16)
        peers = QUERY_ROWS // 128
        out_ref[start // 128 : start // 128 + peers, 0] = rows.reshape(peers, 128, 128)


def attend_back_kernel(count_ref, grad_ref, heads_ref, lse_ref, out_ref):
    count = count_ref[pl.program_id(0)]
    block = flat(heads_ref[:, 0])
    grads = flat(grad_ref[:, 0])
    seq_len = block.shape[0]
    peers = QUERY_ROWS // 128
    key_sums = [jnp.zeros((seq_len, DH), jnp.float32) for _ in range(2)]
    value_sums = [jnp.zeros((seq_len, DH), jnp.float32) for _ in range(2)]
    for start in range(0, seq_len, QUERY_ROWS):
        outs = []
        for head in range(2):
            low = head * DH
            keys = block[:, 128 + low : 128 + low + DH]
            values = block[:, 256 + low : 256 + low + DH]
            queries = block[start : start + QUERY_ROWS, low : low + DH]
            grad_rows = grads[start : start + QUERY_ROWS, low : low + DH]
            lse = lse_ref[0, head : head + 1, start : start + QUERY_ROWS]
            scores = product_nt(keys, queries)
            scores = jnp.where(valid_rows(count, scores), scores * SCORE_SCALE, MASKED_SCORE)
            weights = jnp.exp(scores - lse)
            grad_weights = product_nt(values, grad_rows)
            dots = jnp.sum(weights * grad_weights, axis=0, keepdims=True)
            grad_scores = (weights * (grad_weights - dots)).astype(jnp.bfloat16)
            value_sums[head] += product(weights.astype(jnp.bfloat16), grad_rows)
            key_sums[head] += product(grad_scores, queries)
            outs.append((product_tn(keys, grad_scores) * SCORE_SCALE).T)
        rows = jnp.concatenate(outs, axis=1).astype(jnp.bfloat16)
        out_ref[start // 128 : start // 128 + peers, 0, :, :128] = rows.reshape(peers, 128, 128)
    key_rows = (jnp.concatenate(key_sums, axis=1) * SCORE_SCALE).astype(jnp.bfloat16)
    value_rows = jnp.concatenate(value_sums, axis=1).astype(jnp.bfloat16)
    out_ref[:, 0, :, 128:256] = key_rows.reshape(-1, 128, 128)
    out_ref[:, 0, :, 256:] = value_rows.reshape(-1, 128, 128)


def rear_kernel(keep, x_ref, attn_ref, table_ref, proj_ref, fc1_ref, fc2_ref, *rest):
    if keep:
        result_ref, branch_ref, hidden_ref, mlp_ref, normed, middle, total = rest
    else:
        result_ref, normed, middle, total = rest
    step = pl.program_id(0)

    @pl.when(step == 0)
    def _():
        branch = product(side_by_side(attn_ref), flat(proj_ref[...])) + vector(table_ref, PROJ_ADD)
        if keep:
            branch_ref[...] = branch
        middle[...] = x_ref[...].astype(jnp.float32) + vector(table_ref, ATTN_LAYER) * branch
        normed[...] = mlp_normed(middle[...], table_ref)[0]
        total[...] = jnp.broadcast_to(vector(table_ref, FC2_ADD), total.shape)

    hidden = product(normed[...], flat(fc1_ref[...])) + table_ref[pl.ds(HIDDEN_ROW + step, 1), :]
    if keep:
        hidden_ref[...] = hidden
    active = (hidden * cumulative(hidden)).astype(jnp.bfloat16)
    total[...] += product(active, flat(fc2_ref[...]))

    @pl.when(step == pl.num_programs(0) - 1)
    def _():
        if keep:
            mlp_ref[...] = total[...]
        result = middle[...] + vector(table_ref, MLP_LAYER) * total[...]
        result_ref[...] = result.astype(jnp.bfloat16)


def rear_back_kernel(
    keep,
    grad_ref,
    x_ref,
    branch_ref,
    hidden_ref,
    mlp_ref,
    table_ref,
    proj_ref,
    fc1_ref,
    fc2_ref,
    attn_grad_ref,
    middle_grad_ref,
    *rest,
):
    if keep:
        mlp_low_ref, hidden_low_ref, active_ref, normed_ref, branch_low_ref, sums_ref = rest[:6]
    mlp_low, total = rest[-2:]
    step = pl.program_id(0)

    @pl.when(step == 0)
    def _():
        grad_mlp = vector(table_ref, MLP_LAYER) * grad_ref[...].astype(jnp.float32)
        mlp_low[...] = grad_mlp.astype(jnp.bfloat16)
        total[...] = jnp.zeros_like(total)
        if keep:
            sums_ref[...] = jnp.zeros_like(sums_ref)
            sums_ref[FC2_ADD : FC2_ADD + 1, :] = column_sum(grad_mlp)
            mlp_low_ref[...] = mlp_low[...]

    hidden = hidden_ref[...]
    below = cumulative(hidden)
    slope = below + hidden * (jnp.exp(-0.5 * hidden * hidden) * DENSITY_SCALE)
    grad_hidden = product_nt(mlp_low[...], flat(fc2_ref[...])) * slope
    hidden_low = grad_hidden.astype(jnp.bfloat16)
    total[...] += product_nt(hidden_low, flat(fc1_ref[...]))
    if keep:
        sums_ref[pl.ds(HIDDEN_ROW + step, 1), :] = column_sum(grad_hidden)
        hidden_low_ref[...] = hidden_low
        active_ref[...] = (hidden * below).astype(jnp.bfloat16)

    @pl.when(step == pl.num_programs(0) - 1)
    def _():
        grad_rows = grad_ref[...].astype(jnp.float32)
        branch = branch_ref[...]
        middle = x_ref[...].astype(jnp.float32) + vector(table_ref, ATTN_LAYER) * branch
        normed, scaled, inverse = mlp_normed(middle, table_ref)
        grad_normed = total[...]
        grad_middle = grad_rows + norm_back(
            grad_normed * vector(table_ref, MLP_GAIN), scaled, inverse
        )
        middle_grad_ref[...] = grad_middle
        grad_branch = vector(table_ref, ATTN_LAYER) * grad_middle
        branch_low = grad_branch.astype(jnp.bfloat16)
        put_side_by_side(attn_grad_ref, product_nt(branch_low, flat(proj_ref[...])))
        if keep:
            normed_ref[...] = normed
            branch_low_ref[...] = branch_low
            for row, rows in (
                (MLP_LAYER, grad_rows * mlp_ref[...]),
                (MLP_GAIN, grad_normed * scaled),
                (MLP_SHIFT, grad_normed),
                (ATTN_LAYER, grad_middle * branch),
                (PROJ_ADD, grad_branch),
            ):
                sums_ref[row : row + 1, :] = column_sum(rows)


def front_back_kernel(
    keep,
    core_ref,
    grad_ref,
    middle_grad_ref,
    x_ref,
    table_ref,
    qk_mine_ref,
    v_mine_ref,
    qk_other_ref,
    v_other_ref,
    *rest,
):
    if keep:
        out_ref, sums_ref = rest
    else:
        (out_ref,) = rest
    core = core_ref[0]
    grad_normed = 0.0
    for at, (qk_ref, v_ref) in enumerate(
        ((qk_mine_ref, v_mine_ref), (qk_other_ref, v_other_ref))
    ):
        first = (core if at == 0 else 1 - core) * 4
        queries, keys, values = (
            side_by_side(grad_ref, start, first, 4) for start in (0, 128, 256)
        )
        grad_normed += product_nt(queries, flat(qk_ref[:, :SLAB]))
        grad_normed += product_nt(keys, flat(qk_ref[:, SLAB:]))
        grad_normed += product_nt(values, flat(v_ref[...]))
    _, scaled, inverse = attn_normed(x_ref[...].astype(jnp.float32), table_ref)
    grad_input = middle_grad_ref[...] + norm_back(
        grad_normed * vector(table_ref, ATTN_GAIN), scaled, inverse
    )
    out_ref[...] = grad_input.astype(jnp.bfloat16)
    if keep:
        sums_ref[...] = jnp.zeros_like(sums_ref)
        for row, rows in (
            (ATTN_GAIN, grad_normed * scaled),
            (ATTN_SHIFT, grad_normed),
            (QUERY_ADD, side_by_side(grad_ref, 0).astype(jnp.float32)),
            (VALUE_ADD, side_by_side(grad_ref, 256).astype(jnp.float32)),
        ):
            sums_ref[row : row + 1, :] = column_sum(rows)


def put_products(core, mine_ref, other_ref, left, right, start, count):
    for ref, part in zip((mine_ref, other_ref), halves(core, right)):
        grad = product_tn(left, part).astype(jnp.bfloat16)
        ref[:, start : start + count] = grad.reshape(-1, count, part.shape[1])


def mlp_weights_kernel(
    core_ref,
    normed_ref,
    hidden_low_ref,
    active_ref,
    mlp_low_ref,
    attn_ref,
    branch_low_ref,
    fc1_mine_ref,
    fc1_other_ref,
    fc2_mine_ref,
    fc2_other_ref,
    proj_mine_ref,
    proj_other_ref,
):
    core = core_ref[0]
    owned = fc2_mine_ref.shape[1]
    put_products(core, fc2_mine_ref, fc2_other_ref, active_ref[...], mlp_low_ref[...], 0, owned)
    put_products(core, fc1_mine_ref, fc1_other_ref, normed_ref[...], hidden_low_ref[...], 0, SLAB)

    @pl.when(pl.program_id(0) == 0)
    def _():
        attn = side_by_side(attn_ref)
        put_products(core, proj_mine_ref, proj_other_ref, attn, branch_low_ref[...], 0, SLAB)


def query_key_weights_kernel(core_ref, x_ref, table_ref, grad_ref, mine_ref, other_ref):
    normed, _, _ = attn_normed(x_ref[...].astype(jnp.float32), table_ref)
    for at in range(2):
        grads = side_by_side(grad_ref, at * 128)
        put_products(core_ref[0], mine_ref, other_ref, normed, grads, at * SLAB, SLAB)


def value_weights_kernel(core_ref, x_ref, table_ref, grad_ref, small_ref, mine_ref, other_ref):
    core = core_ref[0]
    normed, _, _ = attn_normed(x_ref[...].astype(jnp.float32), table_ref)
    put_products(core, mine_ref, other_ref, normed, side_by_side(grad_ref, 256), 0, SLAB)
    small = small_ref[...]
    mine_ref[:, SLAB:] = jnp.where(core == 0, small, jnp.zeros_like(small))
    other_ref[:, SLAB:] = jnp.where(core == 0, jnp.zeros_like(small), small)


def like(*shape, dtype=jnp.bfloat16):
    return jax.ShapeDtypeStruct(shape, dtype)


def whole_block(array):
    ndim = len(array.shape)
    return pl.BlockSpec(array.shape, lambda *_: (0,) * ndim)


def params():
    return pltpu.CompilerParams(vmem_limit_bytes=VMEM_LIMIT)


def takes(microseconds):
    return pl.CostEstimate(
        flops=int(microseconds * 1.15e9), transcendentals=0, bytes_accessed=int(microseconds * 3e6)
    )


SCALARS = pl.BlockSpec(memory_space=pltpu.SMEM)


def early_specs(early):
    devices, _, half = early[0].shape
    values = pl.BlockSpec((devices, SLAB, half), lambda i: (0, 0, 0))
    return [whole_block(early[0]), values, whole_block(early[0]), values]


def call_front(core, x, table, early):
    rows, _ = x.shape
    return pl.pallas_call(
        front_kernel,
        grid=(1,),
        in_specs=[SCALARS, whole_block(x), whole_block(table)] + early_specs(early),
        out_specs=pl.BlockSpec((8, rows, 384), lambda i: (0, 0, 0)),
        out_shape=like(8, rows, 384),
        compiler_params=params(),
        cost_estimate=takes(6.5),
    )(core, x, table, *early)


def call_attend(counts, heads):
    images = counts.shape[0]
    heads = heads.reshape(8, images, -1, 384)
    tokens = heads.shape[2]
    out, lse = pl.pallas_call(
        attend_kernel,
        grid=(images,),
        in_specs=[SCALARS, pl.BlockSpec((8, 1, tokens, 384), lambda i: (0, i, 0, 0))],
        out_specs=[
            pl.BlockSpec((8, 1, tokens, 128), lambda i: (0, i, 0, 0)),
            pl.BlockSpec((1, 2, 8 * tokens), lambda i: (i, 0, 0)),
        ],
        out_shape=[
            like(8, images, tokens, 128),
            like(images, 2, 8 * tokens, dtype=jnp.float32),
        ],
        compiler_params=params(),
        cost_estimate=takes(14.3),
    )(counts, heads)
    return out.reshape(8, images * tokens, 128), lse


def call_attend_back(counts, grads, heads, lse):
    images = counts.shape[0]
    heads = heads.reshape(8, images, -1, 384)
    tokens = heads.shape[2]
    out = pl.pallas_call(
        attend_back_kernel,
        grid=(images,),
        in_specs=[
            SCALARS,
            pl.BlockSpec((8, 1, tokens, 128), lambda i: (0, i, 0, 0)),
            pl.BlockSpec((8, 1, tokens, 384), lambda i: (0, i, 0, 0)),
            pl.BlockSpec((1, 2, 8 * tokens), lambda i: (i, 0, 0)),
        ],
        out_specs=pl.BlockSpec((8, 1, tokens, 384), lambda i: (0, i, 0, 0)),
        out_shape=like(*heads.shape),
        compiler_params=params(),
        cost_estimate=takes(16.5),
    )(counts, grads.reshape(8, images, tokens, 128), heads, lse)
    return out.reshape(8, images * tokens, 384)


def rear_weight_specs(late):
    devices, owned, width = late.shape
    fc2_rows = (owned - SLAB) // 2
    steps = fc2_rows // SLAB
    return steps, [
        pl.BlockSpec((devices, SLAB, width), lambda j: (0, 2 * steps, 0)),
        pl.BlockSpec((devices, SLAB, width), lambda j: (0, steps + j, 0)),
        pl.BlockSpec((devices // steps, fc2_rows, width), lambda j: (j, 0, 0)),
    ]


def call_rear(keep, x, attn, table, late):
    rows, width = x.shape
    steps, weight_specs = rear_weight_specs(late)
    full = like(rows, width, dtype=jnp.float32)
    column = pl.BlockSpec((rows, width), lambda j: (0, j))
    out_shape, out_specs = [like(rows, width)], [whole_block(x)]
    if keep:
        out_shape += [full, like(rows, steps * width, dtype=jnp.float32), full]
        out_specs += [whole_block(x), column, whole_block(x)]
    return pl.pallas_call(
        functools.partial(rear_kernel, keep),
        grid=(steps,),
        in_specs=[whole_block(member) for member in (x, attn, table)] + weight_specs,
        out_specs=out_specs,
        out_shape=out_shape,
        scratch_shapes=[
            pltpu.VMEM((rows, width), jnp.bfloat16),
            pltpu.VMEM((rows, width), jnp.float32),
            pltpu.VMEM((rows, width), jnp.float32),
        ],
        compiler_params=params(),
        cost_estimate=takes(13),
    )(x, attn, table, late, late, late)


def call_rear_back(keep, grad, x, branch, hidden, mlp, table, late):
    rows, width = x.shape
    steps, weight_specs = rear_weight_specs(late)
    column = pl.BlockSpec((rows, width), lambda j: (0, j))
    attn_grad = like(8, rows, 128)
    out_shape = [attn_grad, like(rows, width, dtype=jnp.float32)]
    out_specs = [whole_block(attn_grad), whole_block(x)]
    if keep:
        wide = like(rows, steps * width)
        out_shape += [like(rows, width), wide, wide, like(rows, width), like(rows, width)]
        out_specs += [whole_block(x), column, column, whole_block(x), whole_block(x)]
        out_shape += [like(*table.shape, dtype=jnp.float32)]
        out_specs += [whole_block(table)]
    return pl.pallas_call(
        functools.partial(rear_back_kernel, keep),
        grid=(steps,),
        in_specs=[
            whole_block(grad),
            whole_block(x),
            whole_block(branch),
            column,
            whole_block(mlp),
            whole_block(table),
        ]
        + weight_specs,
        out_specs=out_specs,
        out_shape=out_shape,
        scratch_shapes=[
            pltpu.VMEM((rows, width), jnp.bfloat16),
            pltpu.VMEM((rows, width), jnp.float32),
        ],
        compiler_params=params(),
        cost_estimate=takes(16),
    )(grad, x, branch, hidden, mlp, table, late, late, late)


def call_front_back(keep, core, grad_qkv, grad_middle, x, table, early):
    rows, width = x.shape
    out_shape, out_specs = [like(rows, width)], [whole_block(x)]
    if keep:
        out_shape += [like(*table.shape, dtype=jnp.float32)]
        out_specs += [whole_block(table)]
    return pl.pallas_call(
        functools.partial(front_back_kernel, keep),
        grid=(1,),
        in_specs=[SCALARS]
        + [whole_block(member) for member in (grad_qkv, grad_middle, x, table)]
        + early_specs(early),
        out_specs=out_specs,
        out_shape=out_shape,
        compiler_params=params(),
        cost_estimate=takes(7),
    )(core, grad_qkv, grad_middle, x, table, *early)


def call_mlp_weights(core, normed, hidden_low, active, mlp_low, attn, branch_low, devices, owned):
    rows, width = normed.shape
    steps = owned // SLAB
    half = width // 2
    column = pl.BlockSpec((rows, width), lambda j: (0, j))
    fc1_spec = pl.BlockSpec((devices, SLAB, half), lambda j: (0, j, 0))
    fc2_spec = pl.BlockSpec((devices // steps, owned, half), lambda j: (j, 0, 0))
    proj_spec = pl.BlockSpec((devices, SLAB, half), lambda j: (0, 0, 0))
    return pl.pallas_call(
        mlp_weights_kernel,
        grid=(steps,),
        in_specs=[SCALARS, whole_block(normed), column, column]
        + [whole_block(member) for member in (mlp_low, attn, branch_low)],
        out_specs=[fc1_spec, fc1_spec, fc2_spec, fc2_spec, proj_spec, proj_spec],
        out_shape=[like(devices, owned, half)] * 4 + [like(devices, SLAB, half)] * 2,
        compiler_params=params(),
        cost_estimate=takes(11),
    )(core, normed, hidden_low, active, mlp_low, attn, branch_low)


def call_attn_weights(kernel, core, devices, *operands):
    shape = like(devices, 2 * SLAB, operands[0].shape[1] // 2)
    return pl.pallas_call(
        kernel,
        grid=(1,),
        in_specs=[SCALARS] + [whole_block(operand) for operand in operands],
        out_specs=[whole_block(shape)] * 2,
        out_shape=[shape] * 2,
        compiler_params=params(),
        cost_estimate=takes(4),
    )(core, *operands)


def small_slab(vectors, hidden_vector):
    lead = vectors.shape[:-2]
    row = jnp.concatenate([vectors.reshape(lead + (-1,)), hidden_vector], axis=-1)
    return jnp.pad(
        row[..., None, :], [(0, 0)] * len(lead) + [(0, SLAB - 1), (0, SMALL_WIDTH - row.shape[-1])]
    )


def table_of(slabs):
    row = slabs.astype(jnp.float32)
    vectors = row[:, : HIDDEN_ROW * SLAB].reshape(-1, HIDDEN_ROW, SLAB)
    vectors = vectors.transpose(1, 0, 2).reshape(HIDDEN_ROW, -1)
    start = HIDDEN_ROW * SLAB
    hidden = row[:, start : start + 64].reshape(-1, vectors.shape[1])
    return jnp.pad(
        jnp.concatenate([vectors, hidden]),
        [(0, TABLE_ROWS - HIDDEN_ROW - hidden.shape[0]), (0, 0)],
    )


def slabs_of(sums, devices):
    vectors = sums[:HIDDEN_ROW].reshape(HIDDEN_ROW, devices, SLAB).transpose(1, 0, 2)
    hidden = sums[HIDDEN_ROW : HIDDEN_ROW + 4].reshape(devices, -1)
    return small_slab(vectors, hidden).astype(jnp.bfloat16)


def column_slabs(rows):
    count = rows.shape[1] // 1024
    return rows.reshape(SLAB, count, 1024).transpose(1, 0, 2).reshape(count * SLAB, 1024)


def from_column_slabs(rows):
    count = rows.shape[0] // SLAB
    return rows.reshape(count, SLAB, 1024).transpose(1, 0, 2).reshape(SLAB, count * 1024)


def on_device(
    images,
    key_mask,
    image_order,
    attn_norm_gain,
    attn_norm_bias,
    qkv_weight,
    query_bias,
    value_bias,
    proj_weight,
    proj_bias,
    attn_scale,
    mlp_norm_gain,
    mlp_norm_bias,
    fc1_weight,
    fc1_bias,
    fc2_weight,
    fc2_bias,
    mlp_scale,
    cotangent,
):
    section_index = lax.axis_index("section")
    local_images, tokens_here, features = images.shape
    rows = local_images * tokens_here
    reversed_order = image_order[0] > image_order[1]
    core = (lax.axis_index("head") % 2).astype(jnp.int32).reshape(1)

    vectors = jnp.concatenate(
        [
            attn_norm_gain,
            attn_norm_bias,
            query_bias,
            value_bias,
            proj_bias,
            attn_scale,
            mlp_norm_gain,
            mlp_norm_bias,
            fc2_bias,
            mlp_scale,
        ]
    )
    late_shard = jnp.concatenate([fc2_weight[0], column_slabs(fc1_weight[0]), proj_weight[0]])
    late = lax.all_gather(late_shard, ("dp", "head"), axis=0)
    devices = late.shape[0]
    small_shard = jnp.pad(
        small_slab(vectors, fc1_bias[0]), [(0, 0), (0, features - SMALL_WIDTH)]
    )
    early_shard = jnp.concatenate([column_slabs(qkv_weight[0]), small_shard])
    ways = ("dp", "head")
    chip = spread_chip(early_shard)
    lanes = [
        spread_lane(chip[:, :, : 2 * SLAB], "dp"),
        spread_lane(chip[:, :, 2 * SLAB :], "head"),
    ]
    ends = [spread_ends(lane, way) for lane, way in zip(lanes, ways)]
    spread_parts = [spread_rest(*item) for item in zip(lanes, ends, ways)]
    early = [part[at] for at in range(2) for part in spread_parts]
    table = table_of(jnp.where(core == 0, early[1][:, SLAB], early[3][:, SLAB]))

    own_images = jnp.where(reversed_order, images[::-1], images).reshape(rows, features)
    counts = jnp.sum(key_mask, axis=1, dtype=jnp.int32)
    counts = jnp.where(reversed_order, counts[::-1], counts)

    def attention(x):
        heads = to_peers(call_front(core, x, table, early))
        attn, lse = call_attend(counts, heads)
        return heads, lse, to_peers(attn)

    (passed,) = call_rear(False, own_images, attention(own_images)[2], table, late)
    x = jnp.where(section_index == 0, own_images, shifted(passed, 1))
    heads, lse, attn = attention(x)
    result, *rear_state = call_rear(True, x, attn, table, late)

    own_grad = cotangent.reshape(rows, features)
    rear = call_rear_back(False, own_grad, x, *rear_state, table, late)
    grad_qkv = to_peers(call_attend_back(counts, to_peers(rear[0]), heads, lse))
    (passed_back,) = call_front_back(False, core, grad_qkv, rear[1], x, table, early)
    grad = jnp.where(section_index == 0, shifted(passed_back, -1), own_grad)

    rear = call_rear_back(True, grad, x, *rear_state, table, late)
    grad_attn, grad_middle, mlp_low, hidden_low, active, normed, branch_low, rear_sums = rear
    fc1_mine, fc1_other, fc2_mine, fc2_other, proj_mine, proj_other = call_mlp_weights(
        core, normed, hidden_low, active, mlp_low, attn, branch_low, devices, 4 * SLAB
    )
    grad_heads = after(to_peers(grad_attn), fc1_mine)
    mlp_terms = [
        core_sum(fc1_mine, fc1_other),
        jnp.concatenate(
            [core_sum(fc2_mine, fc2_other), core_sum(proj_mine, proj_other)], axis=4
        ),
    ]
    grad_qkv = to_peers(call_attend_back(counts, grad_heads, heads, lse))
    grad_qkv = after(grad_qkv, *mlp_terms)
    mlp_halves = [ring_halves(terms, way) for terms, way in zip(mlp_terms, ways)]
    mlp_terms = [ring_rest(*item) for item in zip(mlp_terms, mlp_halves, ways)]

    attn_parts = call_attn_weights(query_key_weights_kernel, core, devices, x, table, grad_qkv)
    input_grad, front_sums = call_front_back(
        True, core, after(grad_qkv, attn_parts, mlp_halves), grad_middle, x, table, early
    )
    small = slabs_of(rear_sums + front_sums, devices)
    value_parts = call_attn_weights(
        value_weights_kernel, core, devices, x, table, grad_qkv, small
    )
    attn_terms = [core_sum(*attn_parts), core_sum(*value_parts)]
    attn_terms = [
        ring_rest(terms, ring_halves(terms, way), way) for terms, way in zip(attn_terms, ways)
    ]
    ring_sums = [
        second_ring(terms, way)
        for terms, way in zip(mlp_terms + attn_terms, ways + ways)
    ]
    shard_grad = collect_rest(jnp.concatenate(ring_sums, axis=2))
    fc1_grad, fc2_grad, proj_grad, qkv_grad, small_row = (
        shard_grad[start:stop]
        for start, stop in (
            (0, 4 * SLAB),
            (4 * SLAB, 8 * SLAB),
            (8 * SLAB, 9 * SLAB),
            (9 * SLAB, 12 * SLAB),
            (12 * SLAB, 12 * SLAB + 1),
        )
    )
    qkv_grad = from_column_slabs(qkv_grad)
    row = small_row[0]
    small_grads = row[: HIDDEN_ROW * SLAB].reshape(HIDDEN_ROW, SLAB)
    fc1_bias_grad = row[HIDDEN_ROW * SLAB : HIDDEN_ROW * SLAB + 64]

    layer_out = result.reshape(images.shape)
    input_grad = input_grad.reshape(images.shape)
    input_grad = jnp.where(
        (section_index == 0) & reversed_order, input_grad[::-1], input_grad
    )
    outs = (
        layer_out,
        input_grad,
        small_grads[ATTN_GAIN],
        small_grads[ATTN_SHIFT],
        qkv_grad,
        small_grads[QUERY_ADD],
        small_grads[VALUE_ADD],
        proj_grad,
        small_grads[PROJ_ADD],
        small_grads[ATTN_LAYER],
        small_grads[MLP_GAIN],
        small_grads[MLP_SHIFT],
        from_column_slabs(fc1_grad),
        fc1_bias_grad,
        fc2_grad,
        small_grads[FC2_ADD],
        small_grads[MLP_LAYER],
    )
    return tuple(member[None] for member in outs)


def solution(mesh):
    tokens = P("dp", "head", None)
    vec = P("section", ("dp", "head"))
    mat = P("section", ("dp", "head"), None)
    in_specs = (
        (tokens, P("dp", None), P("dp"), vec, vec, mat, vec, vec, mat, vec, vec, vec, vec)
        + (mat, vec, mat, vec, vec, tokens)
    )
    out_tokens = P("section", "dp", "head", None)
    out_specs = (
        (out_tokens, out_tokens, vec, vec, mat, vec, vec, mat, vec, vec, vec, vec, mat, vec)
        + (mat, vec, vec)
    )
    return jax.shard_map(
        on_device, mesh=mesh, in_specs=in_specs, out_specs=out_specs, check_vma=False
    )
```

```python
import functools

import jax
import jax.numpy as jnp
from jax import lax
from jax.experimental import pallas as pl
from jax.experimental.pallas import tpu as pltpu
from jax.sharding import PartitionSpec as P

DH = 64
MASKED_SCORE = -1e30
NORM_EPSILON = 1e-06
ROOT_HALF = 0.7071067811865476
DENSITY_SCALE = 0.3989422804014327
SCORE_SCALE = DH ** (-0.5)
SLAB = 16
SMALL_WIDTH = 512
QUERY_ROWS = 256
VMEM_LIMIT = 60 * 1024 * 1024

(
    ATTN_GAIN,
    ATTN_SHIFT,
    QUERY_ADD,
    VALUE_ADD,
    PROJ_ADD,
    ATTN_LAYER,
    MLP_GAIN,
    MLP_SHIFT,
    FC2_ADD,
    MLP_LAYER,
) = range(10)
HIDDEN_ROW = 10
TABLE_ROWS = 16

MLP_NORMED, ATTN_NORMED, ATTN_OUT = 4, 5, 6
MLP_GRAD, BRANCH_GRAD = 4, 5


def hop(block, axis, places):
    size = lax.axis_size(axis)
    return lax.ppermute(block, axis, [(i, (i + 2 * places) % size) for i in range(size)])


def swap(block, axis):
    size = lax.axis_size(axis)
    return lax.ppermute(block, axis, [(i, i ^ 1) for i in range(size)])


def coordinates():
    dp_index, head_index = lax.axis_index("dp"), lax.axis_index("head")
    return dp_index // 2, dp_index % 2, head_index // 2, head_index % 2


def after(value, *others):
    return lax.optimization_barrier((value,) + others)[0]


def blank(shape, given):
    def kernel(given_ref, out_ref):
        pass

    anywhere = pl.BlockSpec(memory_space=pl.ANY)
    return pl.pallas_call(
        kernel,
        in_specs=[anywhere],
        out_specs=anywhere,
        out_shape=jax.ShapeDtypeStruct(shape, given.dtype),
    )(given)


def by_core(core, mine, other, axis):
    return jnp.where(
        core == 0,
        jnp.concatenate([mine, other], axis=axis),
        jnp.concatenate([other, mine], axis=axis),
    )


def spread_chip(shard):
    _, z_me, _, core_me = coordinates()
    half = shard.shape[1] // 2
    first, second = shard[:, :half], shard[:, half:]
    mine = jnp.where(core_me == 0, first, second)[None]
    cores = by_core(core_me, mine, swap(jnp.where(core_me == 0, second, first), "head")[None], 0)
    return by_core(z_me, cores[None], swap(cores, "dp")[None], 0)


def spread_lane(pair, last_axis):
    x_me, _, y_me, _ = coordinates()
    x_size, y_size = lax.axis_size("dp") // 2, lax.axis_size("head") // 2
    shape = pair.shape[1:]
    zeros = (0,) * len(shape)
    along_y = last_axis == "dp"
    axis, me, size = ("head", y_me, y_size) if along_y else ("dp", x_me, x_size)
    lane = blank(((2, size) if along_y else (size, 2)) + shape, pair)
    for places in range(size):
        came = pair if places == 0 else hop(pair, axis, places)
        source = (me - places) % size
        if along_y:
            lane = lax.dynamic_update_slice(lane, came[:, None], (0, source) + zeros)
        else:
            lane = lax.dynamic_update_slice(lane, came[None], (source, 0) + zeros)
    return lane


def spread_ends(lane, last_axis):
    return hop(lane, last_axis, 1), hop(lane, last_axis, -1)


def spread_rest(lane, ends, last_axis):
    x_me, _, y_me, _ = coordinates()
    x_size, y_size = lax.axis_size("dp") // 2, lax.axis_size("head") // 2
    along_x = last_axis == "dp"
    me, size = (x_me, x_size) if along_x else (y_me, y_size)
    low, high = ends
    half = lane.shape[0] // 2
    far = (hop(low[:half], last_axis, 1), hop(high[half:], last_axis, -1))
    shape = lane.shape[2:]
    zeros = (0,) * len(shape)
    near = blank((x_size, 2, y_size) + shape, lane)
    for places, at, block in (
        (0, 0, lane),
        (1, 0, low),
        (-1, 0, high),
        (2, 0, far[0]),
        (2, half, far[1]),
    ):
        source = (me - places) % size
        if along_x:
            near = lax.dynamic_update_slice(near, block[None], (source, at, 0) + zeros)
        else:
            near = lax.dynamic_update_slice(near, block[:, :, None], (at, 0, source) + zeros)
    near = near.reshape((-1,) + shape[1:])
    return near, swap(near, "head")


def piece(terms, at, dim):
    return lax.dynamic_index_in_dim(terms, at, dim, keepdims=False)


def by_chip(terms):
    x_size, y_size = lax.axis_size("dp") // 2, lax.axis_size("head") // 2
    return terms.reshape((x_size, 2, y_size, 2) + terms.shape[1:])


def ring_halves(terms, axis):
    x_me, _, y_me, _ = coordinates()
    dim, me, size = (0, x_me, 4) if axis == "dp" else (2, y_me, 4)
    far = piece(terms, (me + 2) % size, dim)
    half = far.shape[0] // 2
    return hop(far[:half], axis, 1), hop(far[half:], axis, -1)


def ring_ends(terms, passed, axis):
    x_me, _, y_me, _ = coordinates()
    dim, me, size = (0, x_me, 4) if axis == "dp" else (2, y_me, 4)
    low, high = (part.astype(jnp.float32) for part in passed)
    up = piece(terms, (me + 1) % size, dim).astype(jnp.float32)
    down = piece(terms, (me - 1) % size, dim).astype(jnp.float32)
    half = up.shape[0] // 2
    up = jnp.concatenate([up[:half] + low, up[half:]]).astype(jnp.bfloat16)
    down = jnp.concatenate([down[:half], down[half:] + high]).astype(jnp.bfloat16)
    return hop(up, axis, 1), hop(down, axis, -1)


def ring_total(terms, ends, axis):
    x_me, _, y_me, _ = coordinates()
    own = piece(terms, x_me, 0) if axis == "dp" else piece(terms, y_me, 2)
    return sum((end.astype(jnp.float32) for end in ends), own.astype(jnp.float32))


def ring_direct(terms, axis, dim, me):
    own = piece(terms, me, dim).astype(jnp.float32)
    for places in (1, 2, 3):
        own = own + hop(piece(terms, (me + places) % 4, dim), axis, places).astype(jnp.float32)
    return own


def second_ring(terms, first_axis):
    x_me, _, y_me, _ = coordinates()
    terms = terms.astype(jnp.bfloat16)
    if first_axis == "dp":
        return ring_direct(terms, "head", 1, y_me)
    return ring_direct(terms, "dp", 0, x_me)


def collect_rest(terms):
    _, z_me, _, core_me = coordinates()
    away = piece(terms, 1 - z_me, 0).astype(jnp.bfloat16)
    cores = piece(terms, z_me, 0) + swap(away, "dp").astype(jnp.float32)
    got = swap(piece(cores, 1 - core_me, 0).astype(jnp.bfloat16), "head").astype(jnp.float32)
    return by_core(core_me, piece(cores, core_me, 0), got, 1)


def to_peers(blocks):
    return lax.all_to_all(blocks, "head", split_axis=0, concat_axis=0, tiled=True)


def shifted(block, distance):
    size = lax.axis_size("section")
    route = [(i, i + distance) for i in range(size) if 0 <= i + distance < size]
    return lax.ppermute(block, "section", route)


def norm_stats(rows):
    centre = rows - jnp.mean(rows, axis=-1, keepdims=True)
    inverse = lax.rsqrt(jnp.mean(centre * centre, axis=-1, keepdims=True) + NORM_EPSILON)
    return centre * inverse, inverse


def norm_back(grad_norm, scaled, inverse):
    first_mean = jnp.mean(grad_norm, axis=-1, keepdims=True)
    second_mean = jnp.mean(grad_norm * scaled, axis=-1, keepdims=True)
    return inverse * (grad_norm - first_mean - scaled * second_mean)


def product(left, right):
    return jnp.dot(left, right, preferred_element_type=jnp.float32)


def product_nt(left, right):
    return lax.dot_general(
        left, right, (((1,), (1,)), ((), ())), preferred_element_type=jnp.float32
    )


def product_tn(left, right):
    return lax.dot_general(
        left, right, (((0,), (0,)), ((), ())), preferred_element_type=jnp.float32
    )


def flat(block):
    return block.reshape(-1, block.shape[-1])


def column_sum(rows):
    return jnp.sum(rows, axis=0, keepdims=True)


def vector(table_ref, row):
    return table_ref[row : row + 1, :]


def side_by_side(blocks_ref, start=0, first=0, count=8):
    return jnp.concatenate(
        [blocks_ref[first + peer, :, start : start + 128] for peer in range(count)], axis=1
    )


def put_side_by_side(blocks_ref, rows, start=0, first=0):
    for peer in range(rows.shape[1] // 128):
        blocks_ref[first + peer, :, start : start + 128] = rows[
            :, peer * 128 : (peer + 1) * 128
        ].astype(blocks_ref.dtype)


def put_column(ref, at, rows):
    width = rows.shape[1]
    start = at * width if isinstance(at, int) else pl.multiple_of(at * width, width)
    ref[:, pl.ds(start, width)] = rows


def halves(core, rows):
    half = rows.shape[1] // 2
    first, second = rows[:, :half], rows[:, half:]
    return jnp.where(core == 0, first, second), jnp.where(core == 0, second, first)


def attn_normed(rows, table_ref):
    scaled, inverse = norm_stats(rows)
    normed = (scaled * vector(table_ref, ATTN_GAIN) + vector(table_ref, ATTN_SHIFT)).astype(
        jnp.bfloat16
    )
    return normed, scaled, inverse


def mlp_normed(middle, table_ref):
    scaled, inverse = norm_stats(middle)
    normed = (scaled * vector(table_ref, MLP_GAIN) + vector(table_ref, MLP_SHIFT)).astype(
        jnp.bfloat16
    )
    return normed, scaled, inverse


def cumulative(hidden):
    return 0.5 * (1.0 + lax.erf(hidden * ROOT_HALF))


def front_kernel(
    core_ref, x_ref, table_ref, qk_mine_ref, v_mine_ref, qk_other_ref, v_other_ref, out_ref
):
    core = core_ref[0]
    normed, _, _ = attn_normed(x_ref[...].astype(jnp.float32), table_ref)
    query_adds = halves(core, vector(table_ref, QUERY_ADD))
    value_adds = halves(core, vector(table_ref, VALUE_ADD))
    for at, (qk_ref, v_ref) in enumerate(
        ((qk_mine_ref, v_mine_ref), (qk_other_ref, v_other_ref))
    ):
        first = (core if at == 0 else 1 - core) * 4
        queries = product(normed, flat(qk_ref[:, :SLAB])) + query_adds[at]
        put_side_by_side(out_ref, queries, 0, first)
        put_side_by_side(out_ref, product(normed, flat(qk_ref[:, SLAB:])), 128, first)
        values = product(normed, flat(v_ref[...])) + value_adds[at]
        put_side_by_side(out_ref, values, 256, first)


def marked(rows, mark):
    first = lax.broadcasted_iota(jnp.int32, rows.shape, 1) == 0
    return jnp.concatenate([rows, jnp.where(first, mark, 0.0).astype(jnp.bfloat16)], axis=1)


def masked_keys(block, count, head):
    keys = block[:, 128 + head * DH : 128 + (head + 1) * DH]
    valid = lax.broadcasted_iota(jnp.int32, keys.shape, 0) < count
    return marked(keys, jnp.where(valid, 0.0, MASKED_SCORE))


def scaled_queries(block, start, head):
    queries = block[start : start + QUERY_ROWS, head * DH : (head + 1) * DH]
    return marked((queries.astype(jnp.float32) * SCORE_SCALE).astype(jnp.bfloat16), 1.0)


def attend_kernel(count_ref, heads_ref, out_ref, lse_ref):
    count = count_ref[pl.program_id(0)]
    block = flat(heads_ref[:, 0])
    seq_len = block.shape[0]
    keys = [masked_keys(block, count, head) for head in range(2)]
    values = [block[:, 256 + head * DH : 256 + (head + 1) * DH] for head in range(2)]
    values = [jnp.concatenate([part, jnp.ones_like(part)], axis=1) for part in values]
    for start in range(0, seq_len, QUERY_ROWS):
        outs = []
        for head in range(2):
            scores = product_nt(keys[head], scaled_queries(block, start, head))
            largest = jnp.max(scores, axis=0, keepdims=True)
            weights = jnp.exp(scores - largest)
            mixed = product_tn(values[head], weights.astype(jnp.bfloat16))
            total = mixed[DH : DH + 1]
            outs.append((mixed[:DH] / total).T)
            lse_ref[0, head : head + 1, start : start + QUERY_ROWS] = largest + jnp.log(total)
        rows = jnp.concatenate(outs, axis=1).astype(jnp.bfloat16)
        peers = QUERY_ROWS // 128
        out_ref[start // 128 : start // 128 + peers, 0] = rows.reshape(peers, 128, 128)


def attend_back_kernel(count_ref, grad_ref, heads_ref, lse_ref, out_ref):
    count = count_ref[pl.program_id(0)]
    block = flat(heads_ref[:, 0])
    grads = flat(grad_ref[:, 0])
    seq_len = block.shape[0]
    peers = QUERY_ROWS // 128
    keys = [masked_keys(block, count, head) for head in range(2)]
    values = [block[:, 256 + head * DH : 256 + (head + 1) * DH] for head in range(2)]
    key_sums = [jnp.zeros((seq_len, DH), jnp.float32) for _ in range(2)]
    value_sums = [jnp.zeros((seq_len, DH), jnp.float32) for _ in range(2)]
    for start in range(0, seq_len, QUERY_ROWS):
        outs = []
        for head in range(2):
            queries = scaled_queries(block, start, head)
            grad_rows = grads[start : start + QUERY_ROWS, head * DH : (head + 1) * DH]
            lse = lse_ref[0, head : head + 1, start : start + QUERY_ROWS]
            weights = jnp.exp(product_nt(keys[head], queries) - lse)
            grad_weights = product_nt(values[head], grad_rows)
            dots = jnp.sum(weights * grad_weights, axis=0, keepdims=True)
            grad_scores = (weights * (grad_weights - dots)).astype(jnp.bfloat16)
            value_sums[head] += product(weights.astype(jnp.bfloat16), grad_rows)
            key_sums[head] += product(grad_scores, queries[:, :DH])
            outs.append((product_tn(keys[head][:, :DH], grad_scores) * SCORE_SCALE).T)
        rows = jnp.concatenate(outs, axis=1).astype(jnp.bfloat16)
        out_ref[start // 128 : start // 128 + peers, 0, :, :128] = rows.reshape(peers, 128, 128)
    key_rows = jnp.concatenate(key_sums, axis=1).astype(jnp.bfloat16)
    value_rows = jnp.concatenate(value_sums, axis=1).astype(jnp.bfloat16)
    out_ref[:, 0, :, 128:256] = key_rows.reshape(-1, 128, 128)
    out_ref[:, 0, :, 256:] = value_rows.reshape(-1, 128, 128)


def hidden_halves(fc1_ref, fc2_ref):
    columns, owners = fc1_ref.shape[2] // 2, fc2_ref.shape[0] // 2
    return [
        (at * columns, (at + 1) * columns, at * owners, (at + 1) * owners) for at in range(2)
    ]


def rear_kernel(keep, x_ref, attn_ref, table_ref, proj_ref, fc1_ref, fc2_ref, *rest):
    if keep:
        result_ref, branch_ref, hidden_ref, mlp_ref, left_ref, normed, middle, total = rest
    else:
        result_ref, normed, middle, total = rest
    step = pl.program_id(0)

    @pl.when(step == 0)
    def _():
        attn = side_by_side(attn_ref)
        branch = product(attn, flat(proj_ref[...])) + vector(table_ref, PROJ_ADD)
        rows = x_ref[...].astype(jnp.float32)
        middle[...] = rows + vector(table_ref, ATTN_LAYER) * branch
        normed[...] = mlp_normed(middle[...], table_ref)[0]
        if keep:
            branch_ref[...] = branch
            put_column(left_ref, MLP_NORMED, normed[...])
            put_column(left_ref, ATTN_NORMED, attn_normed(rows, table_ref)[0])
            put_column(left_ref, ATTN_OUT, attn)
        total[...] = jnp.broadcast_to(vector(table_ref, FC2_ADD), total.shape)

    adds = table_ref[pl.ds(HIDDEN_ROW + step, 1), :]
    actives, mixed = [], 0.0
    for low, high, rows_from, rows_to in hidden_halves(fc1_ref, fc2_ref):
        hidden = product(normed[...], flat(fc1_ref[:, :, low:high])) + adds[:, low:high]
        if keep:
            hidden_ref[:, low:high] = hidden
        actives.append((hidden * cumulative(hidden)).astype(jnp.bfloat16))
        mixed += product(actives[-1], flat(fc2_ref[rows_from:rows_to]))
    if keep:
        put_column(left_ref, step, jnp.concatenate(actives, axis=1))
    total[...] += mixed

    @pl.when(step == pl.num_programs(0) - 1)
    def _():
        if keep:
            mlp_ref[...] = total[...]
        result = middle[...] + vector(table_ref, MLP_LAYER) * total[...]
        result_ref[...] = result.astype(jnp.bfloat16)


def rear_back_kernel(
    keep,
    core_ref,
    grad_ref,
    x_ref,
    branch_ref,
    hidden_ref,
    mlp_ref,
    table_ref,
    proj_ref,
    fc1_ref,
    fc2_ref,
    attn_grad_ref,
    middle_grad_ref,
    *rest,
):
    if keep:
        mine_ref, other_ref, sums_ref = rest[:3]
    mlp_low, total = rest[-2:]
    step = pl.program_id(0)

    def put_right(at, rows):
        mine, other = halves(core_ref[0], rows)
        put_column(mine_ref, at, mine)
        put_column(other_ref, at, other)

    @pl.when(step == 0)
    def _():
        grad_mlp = vector(table_ref, MLP_LAYER) * grad_ref[...].astype(jnp.float32)
        mlp_low[...] = grad_mlp.astype(jnp.bfloat16)
        total[...] = jnp.zeros_like(total)
        if keep:
            sums_ref[...] = jnp.zeros_like(sums_ref)
            sums_ref[FC2_ADD : FC2_ADD + 1, :] = column_sum(grad_mlp)
            put_right(MLP_GRAD, mlp_low[...])

    lows, sums, mixed = [], [], 0.0
    for low, high, rows_from, rows_to in hidden_halves(fc1_ref, fc2_ref):
        hidden = hidden_ref[:, low:high]
        slope = cumulative(hidden) + hidden * (jnp.exp(-0.5 * hidden * hidden) * DENSITY_SCALE)
        grad_hidden = product_nt(mlp_low[...], flat(fc2_ref[rows_from:rows_to])) * slope
        lows.append(grad_hidden.astype(jnp.bfloat16))
        sums.append(column_sum(grad_hidden))
        mixed += product_nt(lows[-1], flat(fc1_ref[:, :, low:high]))
    total[...] += mixed
    if keep:
        sums_ref[pl.ds(HIDDEN_ROW + step, 1), :] = jnp.concatenate(sums, axis=1)
        put_right(step, jnp.concatenate(lows, axis=1))

    @pl.when(step == pl.num_programs(0) - 1)
    def _():
        grad_rows = grad_ref[...].astype(jnp.float32)
        branch = branch_ref[...]
        middle = x_ref[...].astype(jnp.float32) + vector(table_ref, ATTN_LAYER) * branch
        _, scaled, inverse = mlp_normed(middle, table_ref)
        grad_normed = total[...]
        grad_middle = grad_rows + norm_back(
            grad_normed * vector(table_ref, MLP_GAIN), scaled, inverse
        )
        middle_grad_ref[...] = grad_middle
        grad_branch = vector(table_ref, ATTN_LAYER) * grad_middle
        branch_low = grad_branch.astype(jnp.bfloat16)
        put_side_by_side(attn_grad_ref, product_nt(branch_low, flat(proj_ref[...])))
        if keep:
            put_right(BRANCH_GRAD, branch_low)
            for row, rows in (
                (MLP_LAYER, grad_rows * mlp_ref[...]),
                (MLP_GAIN, grad_normed * scaled),
                (MLP_SHIFT, grad_normed),
                (ATTN_LAYER, grad_middle * branch),
                (PROJ_ADD, grad_branch),
            ):
                sums_ref[row : row + 1, :] = column_sum(rows)


def front_back_kernel(
    keep,
    core_ref,
    grad_ref,
    middle_grad_ref,
    x_ref,
    table_ref,
    qk_mine_ref,
    v_mine_ref,
    qk_other_ref,
    v_other_ref,
    *rest,
):
    if keep:
        out_ref, sums_ref = rest
    else:
        (out_ref,) = rest
    core = core_ref[0]
    grad_normed = 0.0
    for at, (qk_ref, v_ref) in enumerate(
        ((qk_mine_ref, v_mine_ref), (qk_other_ref, v_other_ref))
    ):
        first = (core if at == 0 else 1 - core) * 4
        queries, keys, values = (
            side_by_side(grad_ref, start, first, 4) for start in (0, 128, 256)
        )
        grad_normed += product_nt(queries, flat(qk_ref[:, :SLAB]))
        grad_normed += product_nt(keys, flat(qk_ref[:, SLAB:]))
        grad_normed += product_nt(values, flat(v_ref[...]))
    _, scaled, inverse = attn_normed(x_ref[...].astype(jnp.float32), table_ref)
    grad_input = middle_grad_ref[...] + norm_back(
        grad_normed * vector(table_ref, ATTN_GAIN), scaled, inverse
    )
    out_ref[...] = grad_input.astype(jnp.bfloat16)
    if keep:
        sums_ref[...] = jnp.zeros_like(sums_ref)
        for row, rows in (
            (ATTN_GAIN, grad_normed * scaled),
            (ATTN_SHIFT, grad_normed),
            (QUERY_ADD, side_by_side(grad_ref, 0).astype(jnp.float32)),
            (VALUE_ADD, side_by_side(grad_ref, 256).astype(jnp.float32)),
        ):
            sums_ref[row : row + 1, :] = column_sum(rows)


def both_products(left_ref, left_other_ref, right, right_other):
    grad = product_tn(left_ref[...], right) + product_tn(left_other_ref[...], right_other)
    return grad.astype(jnp.bfloat16)


def mlp_weights_kernel(
    active_ref,
    active_other_ref,
    normed_ref,
    normed_other_ref,
    attn_ref,
    attn_other_ref,
    hidden_ref,
    hidden_other_ref,
    mlp_ref,
    mlp_other_ref,
    branch_ref,
    branch_other_ref,
    fc1_proj_ref,
    fc2_ref,
):
    step = pl.program_id(0)
    devices, _, half = fc1_proj_ref.shape
    fc2 = both_products(active_ref, active_other_ref, mlp_ref[...], mlp_other_ref[...])
    fc2_ref[...] = fc2.reshape(fc2_ref.shape)
    fc1 = both_products(normed_ref, normed_other_ref, hidden_ref[...], hidden_other_ref[...])
    start = pl.multiple_of(step * SLAB, SLAB)
    fc1_proj_ref[:, pl.ds(start, SLAB)] = fc1.reshape(devices, SLAB, half)

    @pl.when(step == 0)
    def _():
        proj = both_products(attn_ref, attn_other_ref, branch_ref[...], branch_other_ref[...])
        start = pl.num_programs(0) * SLAB
        fc1_proj_ref[:, start:] = proj.reshape(devices, SLAB, half)


def attn_weights_kernel(parts, core_ref, left_ref, left_other_ref, grad_ref, got_ref, *rest):
    out_ref = rest[-1]
    devices, _, half = out_ref.shape
    for at, part in enumerate(parts):
        right = side_by_side(grad_ref, part * 128, core_ref[0] * 4, 4)
        right_other = side_by_side(got_ref, part * 128, 0, 4)
        grad = both_products(left_ref, left_other_ref, right, right_other)
        out_ref[:, at * SLAB : (at + 1) * SLAB] = grad.reshape(devices, SLAB, half)
    if len(rest) > 1:
        out_ref[:, len(parts) * SLAB :] = rest[0][...]


def like(*shape, dtype=jnp.bfloat16):
    return jax.ShapeDtypeStruct(shape, dtype)


def whole_block(array):
    ndim = len(array.shape)
    return pl.BlockSpec(array.shape, lambda *_: (0,) * ndim)


def params():
    return pltpu.CompilerParams(vmem_limit_bytes=VMEM_LIMIT)


def takes(microseconds):
    return pl.CostEstimate(
        flops=int(microseconds * 1.15e9), transcendentals=0, bytes_accessed=int(microseconds * 3e6)
    )


SCALARS = pl.BlockSpec(memory_space=pltpu.SMEM)


def early_specs(early):
    devices, _, half = early[0].shape
    values = pl.BlockSpec((devices, SLAB, half), lambda i: (0, 0, 0))
    return [whole_block(early[0]), values, whole_block(early[0]), values]


def call_front(core, x, table, early):
    rows, _ = x.shape
    return pl.pallas_call(
        front_kernel,
        grid=(1,),
        in_specs=[SCALARS, whole_block(x), whole_block(table)] + early_specs(early),
        out_specs=pl.BlockSpec((8, rows, 384), lambda i: (0, 0, 0)),
        out_shape=like(8, rows, 384),
        compiler_params=params(),
        cost_estimate=takes(6.5),
    )(core, x, table, *early)


def call_attend(counts, heads):
    images = counts.shape[0]
    heads = heads.reshape(8, images, -1, 384)
    tokens = heads.shape[2]
    out, lse = pl.pallas_call(
        attend_kernel,
        grid=(images,),
        in_specs=[SCALARS, pl.BlockSpec((8, 1, tokens, 384), lambda i: (0, i, 0, 0))],
        out_specs=[
            pl.BlockSpec((8, 1, tokens, 128), lambda i: (0, i, 0, 0)),
            pl.BlockSpec((1, 2, 8 * tokens), lambda i: (i, 0, 0)),
        ],
        out_shape=[
            like(8, images, tokens, 128),
            like(images, 2, 8 * tokens, dtype=jnp.float32),
        ],
        compiler_params=params(),
        cost_estimate=takes(14.3),
    )(counts, heads)
    return out.reshape(8, images * tokens, 128), lse


def call_attend_back(counts, grads, heads, lse):
    images = counts.shape[0]
    heads = heads.reshape(8, images, -1, 384)
    tokens = heads.shape[2]
    out = pl.pallas_call(
        attend_back_kernel,
        grid=(images,),
        in_specs=[
            SCALARS,
            pl.BlockSpec((8, 1, tokens, 128), lambda i: (0, i, 0, 0)),
            pl.BlockSpec((8, 1, tokens, 384), lambda i: (0, i, 0, 0)),
            pl.BlockSpec((1, 2, 8 * tokens), lambda i: (i, 0, 0)),
        ],
        out_specs=pl.BlockSpec((8, 1, tokens, 384), lambda i: (0, i, 0, 0)),
        out_shape=like(*heads.shape),
        compiler_params=params(),
        cost_estimate=takes(16.5),
    )(counts, grads.reshape(8, images, tokens, 128), heads, lse)
    return out.reshape(8, images * tokens, 384)


def rear_weight_specs(late):
    devices, owned, width = late.shape
    fc2_rows = (owned - SLAB) // 2
    steps = fc2_rows // SLAB
    return steps, [
        pl.BlockSpec((devices, SLAB, width), lambda j: (0, 2 * steps, 0)),
        pl.BlockSpec((devices, SLAB, width), lambda j: (0, steps + j, 0)),
        pl.BlockSpec((devices // steps, fc2_rows, width), lambda j: (j, 0, 0)),
    ]


def call_rear(keep, x, attn, table, late):
    rows, width = x.shape
    steps, weight_specs = rear_weight_specs(late)
    full = like(rows, width, dtype=jnp.float32)
    column = pl.BlockSpec((rows, width), lambda j: (0, j))
    out_shape, out_specs = [like(rows, width)], [whole_block(x)]
    if keep:
        left = like(rows, (steps + 3) * width)
        out_shape += [full, like(rows, steps * width, dtype=jnp.float32), full, left]
        out_specs += [whole_block(x), column, whole_block(x), whole_block(left)]
    return pl.pallas_call(
        functools.partial(rear_kernel, keep),
        grid=(steps,),
        in_specs=[whole_block(member) for member in (x, attn, table)] + weight_specs,
        out_specs=out_specs,
        out_shape=out_shape,
        scratch_shapes=[
            pltpu.VMEM((rows, width), jnp.bfloat16),
            pltpu.VMEM((rows, width), jnp.float32),
            pltpu.VMEM((rows, width), jnp.float32),
        ],
        compiler_params=params(),
        cost_estimate=takes(13),
    )(x, attn, table, late, late, late)


def call_rear_back(keep, core, grad, x, branch, hidden, mlp, table, late):
    rows, width = x.shape
    steps, weight_specs = rear_weight_specs(late)
    column = pl.BlockSpec((rows, width), lambda j: (0, j))
    attn_grad = like(8, rows, 128)
    out_shape = [attn_grad, like(rows, width, dtype=jnp.float32)]
    out_specs = [whole_block(attn_grad), whole_block(x)]
    if keep:
        right = like(rows, (steps + 2) * width // 2)
        out_shape += [right, right]
        out_specs += [whole_block(right), whole_block(right)]
        out_shape += [like(*table.shape, dtype=jnp.float32)]
        out_specs += [whole_block(table)]
    return pl.pallas_call(
        functools.partial(rear_back_kernel, keep),
        grid=(steps,),
        in_specs=[
            SCALARS,
            whole_block(grad),
            whole_block(x),
            whole_block(branch),
            column,
            whole_block(mlp),
            whole_block(table),
        ]
        + weight_specs,
        out_specs=out_specs,
        out_shape=out_shape,
        scratch_shapes=[
            pltpu.VMEM((rows, width), jnp.bfloat16),
            pltpu.VMEM((rows, width), jnp.float32),
        ],
        compiler_params=params(),
        cost_estimate=takes(16),
    )(core, grad, x, branch, hidden, mlp, table, late, late, late)


def call_front_back(keep, core, grad_qkv, grad_middle, x, table, early):
    rows, width = x.shape
    out_shape, out_specs = [like(rows, width)], [whole_block(x)]
    if keep:
        out_shape += [like(*table.shape, dtype=jnp.float32)]
        out_specs += [whole_block(table)]
    return pl.pallas_call(
        functools.partial(front_back_kernel, keep),
        grid=(1,),
        in_specs=[SCALARS]
        + [whole_block(member) for member in (grad_qkv, grad_middle, x, table)]
        + early_specs(early),
        out_specs=out_specs,
        out_shape=out_shape,
        compiler_params=params(),
        cost_estimate=takes(7),
    )(core, grad_qkv, grad_middle, x, table, *early)


def call_mlp_weights(left, left_other, right, right_other, devices, owned):
    rows = left.shape[0]
    steps = owned // SLAB
    width, half = 1024, 512

    def column(size, at):
        return pl.BlockSpec((rows, size), lambda j: (0, at))

    by_step = [pl.BlockSpec((rows, size), lambda j: (0, j)) for size in (width, half)]
    out_shape = [like(devices, owned + SLAB, half), like(devices, owned, half)]
    return pl.pallas_call(
        mlp_weights_kernel,
        grid=(steps,),
        in_specs=[by_step[0]] * 2
        + [column(width, MLP_NORMED)] * 2
        + [column(width, ATTN_OUT)] * 2
        + [by_step[1]] * 2
        + [column(half, MLP_GRAD)] * 2
        + [column(half, BRANCH_GRAD)] * 2,
        out_specs=[
            whole_block(out_shape[0]),
            pl.BlockSpec((devices // steps, owned, half), lambda j: (j, 0, 0)),
        ],
        out_shape=out_shape,
        compiler_params=params(),
        cost_estimate=takes(9),
    )(*(left, left_other) * 3, *(right, right_other) * 3)


def call_attn_weights(parts, core, devices, left, left_other, grads, got, *small):
    column = pl.BlockSpec((left.shape[0], 1024), lambda i: (0, ATTN_NORMED))
    shape = like(devices, (len(parts) + len(small)) * SLAB, 512)
    return pl.pallas_call(
        functools.partial(attn_weights_kernel, parts),
        grid=(1,),
        in_specs=[SCALARS, column, column]
        + [whole_block(operand) for operand in (grads, got, *small)],
        out_specs=whole_block(shape),
        out_shape=shape,
        compiler_params=params(),
        cost_estimate=takes(3),
    )(core, left, left_other, grads, got, *small)


def small_slab(vectors, hidden_vector):
    lead = vectors.shape[:-2]
    row = jnp.concatenate([vectors.reshape(lead + (-1,)), hidden_vector], axis=-1)
    return jnp.pad(
        row[..., None, :], [(0, 0)] * len(lead) + [(0, SLAB - 1), (0, SMALL_WIDTH - row.shape[-1])]
    )


def table_of(slabs):
    row = slabs.astype(jnp.float32)
    vectors = row[:, : HIDDEN_ROW * SLAB].reshape(-1, HIDDEN_ROW, SLAB)
    vectors = vectors.transpose(1, 0, 2).reshape(HIDDEN_ROW, -1)
    start = HIDDEN_ROW * SLAB
    hidden = row[:, start : start + 64].reshape(-1, vectors.shape[1])
    return jnp.pad(
        jnp.concatenate([vectors, hidden]),
        [(0, TABLE_ROWS - HIDDEN_ROW - hidden.shape[0]), (0, 0)],
    )


def slabs_of(sums, devices):
    vectors = sums[:HIDDEN_ROW].reshape(HIDDEN_ROW, devices, SLAB).transpose(1, 0, 2)
    hidden = sums[HIDDEN_ROW : HIDDEN_ROW + 4].reshape(devices, -1)
    return small_slab(vectors, hidden).astype(jnp.bfloat16)


def column_slabs(rows):
    count = rows.shape[1] // 1024
    return rows.reshape(SLAB, count, 1024).transpose(1, 0, 2).reshape(count * SLAB, 1024)


def from_column_slabs(rows):
    count = rows.shape[0] // SLAB
    return rows.reshape(count, SLAB, 1024).transpose(1, 0, 2).reshape(SLAB, count * 1024)


def on_device(
    images,
    key_mask,
    image_order,
    attn_norm_gain,
    attn_norm_bias,
    qkv_weight,
    query_bias,
    value_bias,
    proj_weight,
    proj_bias,
    attn_scale,
    mlp_norm_gain,
    mlp_norm_bias,
    fc1_weight,
    fc1_bias,
    fc2_weight,
    fc2_bias,
    mlp_scale,
    cotangent,
):
    section_index = lax.axis_index("section")
    local_images, tokens_here, features = images.shape
    rows = local_images * tokens_here
    reversed_order = image_order[0] > image_order[1]
    core = (lax.axis_index("head") % 2).astype(jnp.int32).reshape(1)

    vectors = jnp.concatenate(
        [
            attn_norm_gain,
            attn_norm_bias,
            query_bias,
            value_bias,
            proj_bias,
            attn_scale,
            mlp_norm_gain,
            mlp_norm_bias,
            fc2_bias,
            mlp_scale,
        ]
    )
    late_shard = jnp.concatenate([fc2_weight[0], column_slabs(fc1_weight[0]), proj_weight[0]])
    late = lax.all_gather(late_shard, ("dp", "head"), axis=0)
    devices = late.shape[0]
    small_shard = jnp.pad(
        small_slab(vectors, fc1_bias[0]), [(0, 0), (0, features - SMALL_WIDTH)]
    )
    early_shard = jnp.concatenate([column_slabs(qkv_weight[0]), small_shard])
    ways = ("dp", "head")
    chip = spread_chip(early_shard)
    lanes = [
        spread_lane(chip[:, :, : 2 * SLAB], "dp"),
        spread_lane(chip[:, :, 2 * SLAB :], "head"),
    ]
    ends = [spread_ends(lane, way) for lane, way in zip(lanes, ways)]
    spread_parts = [spread_rest(*item) for item in zip(lanes, ends, ways)]
    early = [part[at] for at in range(2) for part in spread_parts]
    table = table_of(jnp.where(core == 0, early[1][:, SLAB], early[3][:, SLAB]))

    own_images = jnp.where(reversed_order, images[::-1], images).reshape(rows, features)
    counts = jnp.sum(key_mask, axis=1, dtype=jnp.int32)
    counts = jnp.where(reversed_order, counts[::-1], counts)

    def attention(x):
        heads = to_peers(call_front(core, x, table, early))
        attn, lse = call_attend(counts, heads)
        return heads, lse, to_peers(attn)

    (passed,) = call_rear(False, own_images, attention(own_images)[2], table, late)
    x = jnp.where(section_index == 0, own_images, shifted(passed, 1))
    heads, lse, attn = attention(x)
    result, *rear_state, left = call_rear(True, x, attn, table, late)
    left_other = swap(left, "head")

    own_grad = cotangent.reshape(rows, features)
    rear = call_rear_back(False, core, own_grad, x, *rear_state, table, late)
    grad_qkv = to_peers(call_attend_back(counts, to_peers(rear[0]), heads, lse))
    (passed_back,) = call_front_back(False, core, grad_qkv, rear[1], x, table, early)
    passed_back = after(passed_back, left_other)
    grad = jnp.where(section_index == 0, shifted(passed_back, -1), own_grad)

    rear = call_rear_back(True, core, grad, x, *rear_state, table, late)
    grad_attn, grad_middle, right, right_other, rear_sums = rear
    fc1_proj, fc2 = call_mlp_weights(
        left, left_other, right, swap(right_other, "head"), devices, 4 * SLAB
    )
    grad_heads = after(to_peers(grad_attn), fc2)
    mlp_terms = [by_chip(fc1_proj), by_chip(fc2)]
    mlp_halves = [ring_halves(terms, way) for terms, way in zip(mlp_terms, ways)]
    grad_qkv = call_attend_back(counts, grad_heads, heads, lse)
    grad_qkv = to_peers(after(grad_qkv, mlp_halves))
    mlp_ends = [ring_ends(*item) for item in zip(mlp_terms, mlp_halves, ways)]

    got = swap(lax.dynamic_slice_in_dim(grad_qkv, (1 - core[0]) * 4, 4), "head")
    query_key = call_attn_weights((0, 1), core, devices, left, left_other, grad_qkv, got)
    input_grad, front_sums = call_front_back(
        True, core, after(grad_qkv, query_key), grad_middle, x, table, early
    )
    small = slabs_of(rear_sums + front_sums, devices)
    value = call_attn_weights((2,), core, devices, left, left_other, grad_qkv, got, small)
    attn_terms = [by_chip(query_key), by_chip(value)]
    attn_halves = [ring_halves(terms, way) for terms, way in zip(attn_terms, ways)]
    mlp_ends = after(mlp_ends, attn_terms)
    mlp_terms = [ring_total(*item) for item in zip(mlp_terms, mlp_ends, ways)]
    attn_ends = [ring_ends(*item) for item in zip(attn_terms, attn_halves, ways)]
    mlp_terms = after(mlp_terms, attn_halves)
    attn_terms = [ring_total(*item) for item in zip(attn_terms, attn_ends, ways)]
    ring_sums = [
        second_ring(terms, way)
        for terms, way in zip(mlp_terms + attn_terms, ways + ways)
    ]
    shard_grad = collect_rest(jnp.concatenate(ring_sums, axis=2))
    fc1_grad, fc2_grad, proj_grad, qkv_grad, small_row = (
        shard_grad[start:stop]
        for start, stop in (
            (0, 4 * SLAB),
            (5 * SLAB, 9 * SLAB),
            (4 * SLAB, 5 * SLAB),
            (9 * SLAB, 12 * SLAB),
            (12 * SLAB, 12 * SLAB + 1),
        )
    )
    qkv_grad = from_column_slabs(qkv_grad)
    row = small_row[0, :SMALL_WIDTH] + small_row[0, SMALL_WIDTH:]
    small_grads = row[: HIDDEN_ROW * SLAB].reshape(HIDDEN_ROW, SLAB)
    fc1_bias_grad = row[HIDDEN_ROW * SLAB : HIDDEN_ROW * SLAB + 64]

    layer_out = result.reshape(images.shape)
    input_grad = input_grad.reshape(images.shape)
    input_grad = jnp.where(
        (section_index == 0) & reversed_order, input_grad[::-1], input_grad
    )
    outs = (
        layer_out,
        input_grad,
        small_grads[ATTN_GAIN],
        small_grads[ATTN_SHIFT],
        qkv_grad,
        small_grads[QUERY_ADD],
        small_grads[VALUE_ADD],
        proj_grad,
        small_grads[PROJ_ADD],
        small_grads[ATTN_LAYER],
        small_grads[MLP_GAIN],
        small_grads[MLP_SHIFT],
        from_column_slabs(fc1_grad),
        fc1_bias_grad,
        fc2_grad,
        small_grads[FC2_ADD],
        small_grads[MLP_LAYER],
    )
    return tuple(member[None] for member in outs)


def solution(mesh):
    tokens = P("dp", "head", None)
    vec = P("section", ("dp", "head"))
    mat = P("section", ("dp", "head"), None)
    in_specs = (
        (tokens, P("dp", None), P("dp"), vec, vec, mat, vec, vec, mat, vec, vec, vec, vec)
        + (mat, vec, mat, vec, vec, tokens)
    )
    out_tokens = P("section", "dp", "head", None)
    out_specs = (
        (out_tokens, out_tokens, vec, vec, mat, vec, vec, mat, vec, vec, vec, vec, mat, vec)
        + (mat, vec, vec)
    )
    return jax.shard_map(
        on_device, mesh=mesh, in_specs=in_specs, out_specs=out_specs, check_vma=False
    )
```

```python
import functools

import jax
import jax.numpy as jnp
from jax import lax
from jax.experimental import pallas as pl
from jax.experimental.pallas import tpu as pltpu
from jax.sharding import PartitionSpec as P

DH = 64
MASKED_SCORE = -1e30
NORM_EPSILON = 1e-06
ROOT_HALF = 0.7071067811865476
DENSITY_SCALE = 0.3989422804014327
SCORE_SCALE = DH ** (-0.5)
SLAB = 16
SMALL_WIDTH = 512
QUERY_ROWS = 512
BACK_ROWS = 128
PIECES = 1
VMEM_LIMIT = 60 * 1024 * 1024

(
    ATTN_GAIN,
    ATTN_SHIFT,
    QUERY_ADD,
    VALUE_ADD,
    PROJ_ADD,
    ATTN_LAYER,
    MLP_GAIN,
    MLP_SHIFT,
    FC2_ADD,
    MLP_LAYER,
) = range(10)
HIDDEN_ROW = 10
TABLE_ROWS = 16

MLP_NORMED, ATTN_NORMED, ATTN_OUT = 4, 5, 6
MLP_GRAD, BRANCH_GRAD = 4, 5


def hop(block, axis, places):
    size = lax.axis_size(axis)
    return lax.ppermute(block, axis, [(i, (i + 2 * places) % size) for i in range(size)])


def swap(block, axis):
    size = lax.axis_size(axis)
    return lax.ppermute(block, axis, [(i, i ^ 1) for i in range(size)])


def coordinates():
    dp_index, head_index = lax.axis_index("dp"), lax.axis_index("head")
    return dp_index // 2, dp_index % 2, head_index // 2, head_index % 2


def after(value, *others):
    return lax.optimization_barrier((value,) + others)[0]


def blank(shape, given):
    def kernel(given_ref, out_ref):
        pass

    anywhere = pl.BlockSpec(memory_space=pl.ANY)
    return pl.pallas_call(
        kernel,
        in_specs=[anywhere],
        out_specs=anywhere,
        out_shape=jax.ShapeDtypeStruct(shape, given.dtype),
    )(given)


def by_core(core, mine, other, axis):
    return jnp.where(
        core == 0,
        jnp.concatenate([mine, other], axis=axis),
        jnp.concatenate([other, mine], axis=axis),
    )


def spread_chip(shard):
    _, z_me, _, core_me = coordinates()
    half = shard.shape[1] // 2
    first, second = shard[:, :half], shard[:, half:]
    mine = jnp.where(core_me == 0, first, second)[None]
    cores = by_core(core_me, mine, swap(jnp.where(core_me == 0, second, first), "head")[None], 0)
    return by_core(z_me, cores[None], swap(cores, "dp")[None], 0)


def spread_lane(pair, last_axis):
    x_me, _, y_me, _ = coordinates()
    x_size, y_size = lax.axis_size("dp") // 2, lax.axis_size("head") // 2
    shape = pair.shape[1:]
    zeros = (0,) * len(shape)
    along_y = last_axis == "dp"
    axis, me, size = ("head", y_me, y_size) if along_y else ("dp", x_me, x_size)
    lane = blank(((2, size) if along_y else (size, 2)) + shape, pair)
    for places in range(size):
        came = pair if places == 0 else hop(pair, axis, places)
        source = (me - places) % size
        if along_y:
            lane = lax.dynamic_update_slice(lane, came[:, None], (0, source) + zeros)
        else:
            lane = lax.dynamic_update_slice(lane, came[None], (source, 0) + zeros)
    return lane


def spread_ends(lane, last_axis):
    return hop(lane, last_axis, 1), hop(lane, last_axis, -1)


def spread_rest(lane, ends, last_axis):
    x_me, _, y_me, _ = coordinates()
    x_size, y_size = lax.axis_size("dp") // 2, lax.axis_size("head") // 2
    along_x = last_axis == "dp"
    me, size = (x_me, x_size) if along_x else (y_me, y_size)
    low, high = ends
    half = lane.shape[0] // 2
    far = (hop(low[:half], last_axis, 1), hop(high[half:], last_axis, -1))
    shape = lane.shape[2:]
    zeros = (0,) * len(shape)
    near = blank((x_size, 2, y_size) + shape, lane)
    for places, at, block in (
        (0, 0, lane),
        (1, 0, low),
        (-1, 0, high),
        (2, 0, far[0]),
        (2, half, far[1]),
    ):
        source = (me - places) % size
        if along_x:
            near = lax.dynamic_update_slice(near, block[None], (source, at, 0) + zeros)
        else:
            near = lax.dynamic_update_slice(near, block[:, :, None], (at, 0, source) + zeros)
    near = near.reshape((-1,) + shape[1:])
    return near, swap(near, "head")


def piece(terms, at, dim):
    return lax.dynamic_index_in_dim(terms, at, dim, keepdims=False)


def by_chip(terms):
    x_size, y_size = lax.axis_size("dp") // 2, lax.axis_size("head") // 2
    return terms.reshape((x_size, 2, y_size, 2) + terms.shape[1:])


def ring_halves(terms, axis):
    x_me, _, y_me, _ = coordinates()
    dim, me, size = (0, x_me, 4) if axis == "dp" else (2, y_me, 4)
    far = piece(terms, (me + 2) % size, dim)
    half = far.shape[0] // 2
    return hop(far[:half], axis, 1), hop(far[half:], axis, -1)


def ring_ends(terms, passed, axis):
    x_me, _, y_me, _ = coordinates()
    dim, me, size = (0, x_me, 4) if axis == "dp" else (2, y_me, 4)
    low, high = (part.astype(jnp.float32) for part in passed)
    up = piece(terms, (me + 1) % size, dim).astype(jnp.float32)
    down = piece(terms, (me - 1) % size, dim).astype(jnp.float32)
    half = up.shape[0] // 2
    up = jnp.concatenate([up[:half] + low, up[half:]]).astype(jnp.bfloat16)
    down = jnp.concatenate([down[:half], down[half:] + high]).astype(jnp.bfloat16)
    return hop(up, axis, 1), hop(down, axis, -1)


def ring_total(terms, ends, axis):
    x_me, _, y_me, _ = coordinates()
    own = piece(terms, x_me, 0) if axis == "dp" else piece(terms, y_me, 2)
    total = sum((end.astype(jnp.float32) for end in ends), own.astype(jnp.float32))
    return total.astype(jnp.bfloat16)


def ring_direct(terms, axis, dim, me):
    own = piece(terms, me, dim).astype(jnp.float32)
    for places in (1, 2, 3):
        own = own + hop(piece(terms, (me + places) % 4, dim), axis, places).astype(jnp.float32)
    return own


def ring_first(terms, axis):
    x_me, _, y_me, _ = coordinates()
    dim, me = (0, x_me) if axis == "dp" else (2, y_me)
    return ring_direct(terms, axis, dim, me).astype(jnp.bfloat16)


def second_ring(terms, first_axis):
    x_me, _, y_me, _ = coordinates()
    if first_axis == "dp":
        return ring_direct(terms, "head", 1, y_me)
    return ring_direct(terms, "dp", 0, x_me)


def collect_rest(terms):
    _, z_me, _, core_me = coordinates()
    away = piece(terms, 1 - z_me, 0).astype(jnp.bfloat16)
    cores = piece(terms, z_me, 0) + swap(away, "dp").astype(jnp.float32)
    got = swap(piece(cores, 1 - core_me, 0).astype(jnp.bfloat16), "head").astype(jnp.float32)
    return by_core(core_me, piece(cores, core_me, 0), got, 1)


def to_peers(blocks):
    return lax.all_to_all(blocks, "head", split_axis=0, concat_axis=0, tiled=True)


def shifted(block, distance):
    size = lax.axis_size("section")
    route = [(i, i + distance) for i in range(size) if 0 <= i + distance < size]
    return lax.ppermute(block, "section", route)


def ahead(items, function):
    value = function(items[0])
    for at, item in enumerate(items):
        later = function(items[at + 1]) if at + 1 < len(items) else None
        yield item, value
        value = later


def norm_stats(rows):
    centre = rows - jnp.mean(rows, axis=-1, keepdims=True)
    inverse = lax.rsqrt(jnp.mean(centre * centre, axis=-1, keepdims=True) + NORM_EPSILON)
    return centre * inverse, inverse


def norm_back(grad_norm, scaled, inverse):
    first_mean = jnp.mean(grad_norm, axis=-1, keepdims=True)
    second_mean = jnp.mean(grad_norm * scaled, axis=-1, keepdims=True)
    return inverse * (grad_norm - first_mean - scaled * second_mean)


def product(left, right):
    return jnp.dot(left, right, preferred_element_type=jnp.float32)


def product_nt(left, right):
    return lax.dot_general(
        left, right, (((1,), (1,)), ((), ())), preferred_element_type=jnp.float32
    )


def product_tn(left, right):
    return lax.dot_general(
        left, right, (((0,), (0,)), ((), ())), preferred_element_type=jnp.float32
    )


def flat(block):
    return block.reshape(-1, block.shape[-1])


def column_sum(rows):
    return jnp.sum(rows, axis=0, keepdims=True)


def vector(table_ref, row):
    return table_ref[row : row + 1, :]


def side_by_side(blocks_ref, start=0, first=0, count=8):
    return jnp.concatenate(
        [blocks_ref[first + peer, :, start : start + 128] for peer in range(count)], axis=1
    )


def put_side_by_side(blocks_ref, rows, start=0, first=0):
    for peer in range(rows.shape[1] // 128):
        blocks_ref[first + peer, :, start : start + 128] = rows[
            :, peer * 128 : (peer + 1) * 128
        ].astype(blocks_ref.dtype)


def put_column(ref, at, rows):
    width = rows.shape[1]
    start = at * width if isinstance(at, int) else pl.multiple_of(at * width, width)
    ref[:, pl.ds(start, width)] = rows


def halves(core, rows):
    half = rows.shape[1] // 2
    first, second = rows[:, :half], rows[:, half:]
    return jnp.where(core == 0, first, second), jnp.where(core == 0, second, first)


def attn_normed(rows, table_ref):
    scaled, inverse = norm_stats(rows)
    normed = (scaled * vector(table_ref, ATTN_GAIN) + vector(table_ref, ATTN_SHIFT)).astype(
        jnp.bfloat16
    )
    return normed, scaled, inverse


def mlp_normed(middle, table_ref):
    scaled, inverse = norm_stats(middle)
    normed = (scaled * vector(table_ref, MLP_GAIN) + vector(table_ref, MLP_SHIFT)).astype(
        jnp.bfloat16
    )
    return normed, scaled, inverse


def cumulative(hidden):
    return 0.5 * (1.0 + lax.erf(hidden * ROOT_HALF))


def front_kernel(
    core_ref, x_ref, table_ref, qk_mine_ref, v_mine_ref, qk_other_ref, v_other_ref, out_ref
):
    core = core_ref[0]
    normed, _, _ = attn_normed(x_ref[...].astype(jnp.float32), table_ref)
    query_adds = halves(core, vector(table_ref, QUERY_ADD))
    value_adds = halves(core, vector(table_ref, VALUE_ADD))
    for at, (qk_ref, v_ref) in enumerate(
        ((qk_mine_ref, v_mine_ref), (qk_other_ref, v_other_ref))
    ):
        first = (core if at == 0 else 1 - core) * 4
        queries = product(normed, flat(qk_ref[:, :SLAB])) + query_adds[at]
        put_side_by_side(out_ref, queries, 0, first)
        put_side_by_side(out_ref, product(normed, flat(qk_ref[:, SLAB:])), 128, first)
        values = product(normed, flat(v_ref[...])) + value_adds[at]
        put_side_by_side(out_ref, values, 256, first)


def marked(rows, mark):
    first = lax.broadcasted_iota(jnp.int32, rows.shape, 1) == 0
    return jnp.concatenate([rows, jnp.where(first, mark, 0.0).astype(jnp.bfloat16)], axis=1)


def masked_keys(block, count, head):
    keys = block[:, 128 + head * DH : 128 + (head + 1) * DH]
    valid = lax.broadcasted_iota(jnp.int32, keys.shape, 0) < count
    return marked(keys, jnp.where(valid, 0.0, MASKED_SCORE))


def scaled_queries(block, start, count, head):
    queries = block[start : start + count, head * DH : (head + 1) * DH]
    return marked((queries.astype(jnp.float32) * SCORE_SCALE).astype(jnp.bfloat16), 1.0)


def attend_kernel(count_ref, heads_ref, out_ref, lse_ref):
    count = count_ref[pl.program_id(0)]
    block = flat(heads_ref[:, 0])
    seq_len = block.shape[0]
    keys = [masked_keys(block, count, head) for head in range(2)]
    values = [block[:, 256 + head * DH : 256 + (head + 1) * DH] for head in range(2)]
    values = [jnp.concatenate([part, jnp.ones_like(part)], axis=1) for part in values]
    outs = []

    def scores_of(item):
        start, head = item
        return product_nt(keys[head], scaled_queries(block, start, QUERY_ROWS, head))

    items = [(start, head) for start in range(0, seq_len, QUERY_ROWS) for head in range(2)]
    for (start, head), scores in ahead(items, scores_of):
        largest = jnp.max(scores, axis=0, keepdims=True)
        weights = jnp.exp(scores - largest)
        mixed = product_tn(values[head], weights.astype(jnp.bfloat16))
        total = mixed[DH : DH + 1]
        outs.append((mixed[:DH] / total).T)
        lse_ref[0, head : head + 1, start : start + QUERY_ROWS] = largest + jnp.log(total)
        if head == 1:
            rows = jnp.concatenate(outs[-2:], axis=1).astype(jnp.bfloat16)
            peers = QUERY_ROWS // 128
            out_ref[start // 128 : start // 128 + peers, 0] = rows.reshape(peers, 128, 128)


def attend_back_kernel(count_ref, grad_ref, heads_ref, lse_ref, out_ref):
    count = count_ref[pl.program_id(0)]
    block = flat(heads_ref[:, 0])
    grads = flat(grad_ref[:, 0])
    seq_len = block.shape[0]
    peers = BACK_ROWS // 128
    keys = [masked_keys(block, count, head) for head in range(2)]
    values = [block[:, 256 + head * DH : 256 + (head + 1) * DH] for head in range(2)]
    key_sums = [jnp.zeros((seq_len, DH), jnp.float32) for _ in range(2)]
    value_sums = [jnp.zeros((seq_len, DH), jnp.float32) for _ in range(2)]
    outs = []

    def products_of(item):
        start, head = item
        queries = scaled_queries(block, start, BACK_ROWS, head)
        grad_rows = grads[start : start + BACK_ROWS, head * DH : (head + 1) * DH]
        scores = product_nt(keys[head], queries)
        return queries, grad_rows, scores, product_nt(values[head], grad_rows)

    items = [(start, head) for start in range(0, seq_len, BACK_ROWS) for head in range(2)]
    for (start, head), members in ahead(items, products_of):
        queries, grad_rows, scores, grad_weights = members
        weights = jnp.exp(scores - lse_ref[0, head : head + 1, start : start + BACK_ROWS])
        shares = weights * grad_weights
        dots = jnp.sum(shares, axis=0, keepdims=True)
        grad_scores = (shares - weights * dots).astype(jnp.bfloat16)
        value_sums[head] += product(weights.astype(jnp.bfloat16), grad_rows)
        key_sums[head] += product(grad_scores, queries[:, :DH])
        outs.append((product_tn(keys[head][:, :DH], grad_scores) * SCORE_SCALE).T)
        if head == 1:
            rows = jnp.concatenate(outs[-2:], axis=1).astype(jnp.bfloat16)
            at = start // 128
            out_ref[at : at + peers, 0, :, :128] = rows.reshape(peers, 128, 128)
    key_rows = jnp.concatenate(key_sums, axis=1).astype(jnp.bfloat16)
    value_rows = jnp.concatenate(value_sums, axis=1).astype(jnp.bfloat16)
    out_ref[:, 0, :, 128:256] = key_rows.reshape(-1, 128, 128)
    out_ref[:, 0, :, 256:] = value_rows.reshape(-1, 128, 128)


def hidden_pieces(fc1_ref, fc2_ref):
    columns, owners = fc1_ref.shape[2] // PIECES, fc2_ref.shape[0] // PIECES
    return [
        (slice(at * columns, (at + 1) * columns), slice(at * owners, (at + 1) * owners))
        for at in range(PIECES)
    ]


def rear_kernel(keep, x_ref, attn_ref, table_ref, proj_ref, fc1_ref, fc2_ref, *rest):
    if keep:
        result_ref, branch_ref, hidden_ref, mlp_ref, left_ref, normed, middle, total = rest
    else:
        result_ref, normed, middle, total = rest
    step = pl.program_id(0)

    @pl.when(step == 0)
    def _():
        attn = side_by_side(attn_ref)
        branch = product(attn, flat(proj_ref[...])) + vector(table_ref, PROJ_ADD)
        rows = x_ref[...].astype(jnp.float32)
        middle[...] = rows + vector(table_ref, ATTN_LAYER) * branch
        normed[...] = mlp_normed(middle[...], table_ref)[0]
        if keep:
            branch_ref[...] = branch
            put_column(left_ref, MLP_NORMED, normed[...])
            put_column(left_ref, ATTN_NORMED, attn_normed(rows, table_ref)[0])
            put_column(left_ref, ATTN_OUT, attn)
        total[...] = jnp.broadcast_to(vector(table_ref, FC2_ADD), total.shape)

    adds = table_ref[pl.ds(HIDDEN_ROW + step, 1), :]
    actives, mixed = [], 0.0

    def hidden_of(item):
        return product(normed[...], flat(fc1_ref[:, :, item[0]])) + adds[:, item[0]]

    for (columns, owners), hidden in ahead(hidden_pieces(fc1_ref, fc2_ref), hidden_of):
        if keep:
            hidden_ref[:, columns] = hidden
        actives.append((hidden * cumulative(hidden)).astype(jnp.bfloat16))
        mixed += product(actives[-1], flat(fc2_ref[owners]))
    if keep:
        put_column(left_ref, step, jnp.concatenate(actives, axis=1))
    total[...] += mixed

    @pl.when(step == pl.num_programs(0) - 1)
    def _():
        if keep:
            mlp_ref[...] = total[...]
        result = middle[...] + vector(table_ref, MLP_LAYER) * total[...]
        result_ref[...] = result.astype(jnp.bfloat16)


def rear_back_kernel(
    keep,
    core_ref,
    grad_ref,
    x_ref,
    branch_ref,
    hidden_ref,
    mlp_ref,
    table_ref,
    proj_ref,
    fc1_ref,
    fc2_ref,
    attn_grad_ref,
    middle_grad_ref,
    *rest,
):
    if keep:
        mine_ref, other_ref, sums_ref = rest[:3]
    mlp_low, total = rest[-2:]
    step = pl.program_id(0)

    def put_right(at, rows):
        mine, other = halves(core_ref[0], rows)
        put_column(mine_ref, at, mine)
        put_column(other_ref, at, other)

    @pl.when(step == 0)
    def _():
        grad_mlp = vector(table_ref, MLP_LAYER) * grad_ref[...].astype(jnp.float32)
        mlp_low[...] = grad_mlp.astype(jnp.bfloat16)
        total[...] = jnp.zeros_like(total)
        if keep:
            sums_ref[...] = jnp.zeros_like(sums_ref)
            sums_ref[FC2_ADD : FC2_ADD + 1, :] = column_sum(grad_mlp)
            put_right(MLP_GRAD, mlp_low[...])

    lows, sums, mixed = [], [], 0.0

    def active_grad_of(item):
        return product_nt(mlp_low[...], flat(fc2_ref[item[1]]))

    for (columns, _), grad in ahead(hidden_pieces(fc1_ref, fc2_ref), active_grad_of):
        hidden = hidden_ref[:, columns]
        slope = cumulative(hidden) + hidden * (jnp.exp(-0.5 * hidden * hidden) * DENSITY_SCALE)
        grad_hidden = grad * slope
        lows.append(grad_hidden.astype(jnp.bfloat16))
        sums.append(column_sum(grad_hidden))
        mixed += product_nt(lows[-1], flat(fc1_ref[:, :, columns]))
    total[...] += mixed
    if keep:
        sums_ref[pl.ds(HIDDEN_ROW + step, 1), :] = jnp.concatenate(sums, axis=1)
        put_right(step, jnp.concatenate(lows, axis=1))

    @pl.when(step == pl.num_programs(0) - 1)
    def _():
        grad_rows = grad_ref[...].astype(jnp.float32)
        branch = branch_ref[...]
        middle = x_ref[...].astype(jnp.float32) + vector(table_ref, ATTN_LAYER) * branch
        _, scaled, inverse = mlp_normed(middle, table_ref)
        grad_normed = total[...]
        grad_middle = grad_rows + norm_back(
            grad_normed * vector(table_ref, MLP_GAIN), scaled, inverse
        )
        middle_grad_ref[...] = grad_middle
        grad_branch = vector(table_ref, ATTN_LAYER) * grad_middle
        branch_low = grad_branch.astype(jnp.bfloat16)
        put_side_by_side(attn_grad_ref, product_nt(branch_low, flat(proj_ref[...])))
        if keep:
            put_right(BRANCH_GRAD, branch_low)
            for row, rows in (
                (MLP_LAYER, grad_rows * mlp_ref[...]),
                (MLP_GAIN, grad_normed * scaled),
                (MLP_SHIFT, grad_normed),
                (ATTN_LAYER, grad_middle * branch),
                (PROJ_ADD, grad_branch),
            ):
                sums_ref[row : row + 1, :] = column_sum(rows)


def front_back_kernel(
    keep,
    core_ref,
    grad_ref,
    middle_grad_ref,
    x_ref,
    table_ref,
    qk_mine_ref,
    v_mine_ref,
    qk_other_ref,
    v_other_ref,
    *rest,
):
    if keep:
        out_ref, sums_ref = rest
    else:
        (out_ref,) = rest
    core = core_ref[0]
    grad_normed = 0.0
    for at, (qk_ref, v_ref) in enumerate(
        ((qk_mine_ref, v_mine_ref), (qk_other_ref, v_other_ref))
    ):
        first = (core if at == 0 else 1 - core) * 4
        queries, keys, values = (
            side_by_side(grad_ref, start, first, 4) for start in (0, 128, 256)
        )
        grad_normed += product_nt(queries, flat(qk_ref[:, :SLAB]))
        grad_normed += product_nt(keys, flat(qk_ref[:, SLAB:]))
        grad_normed += product_nt(values, flat(v_ref[...]))
    _, scaled, inverse = attn_normed(x_ref[...].astype(jnp.float32), table_ref)
    grad_input = middle_grad_ref[...] + norm_back(
        grad_normed * vector(table_ref, ATTN_GAIN), scaled, inverse
    )
    out_ref[...] = grad_input.astype(jnp.bfloat16)
    if keep:
        sums_ref[...] = jnp.zeros_like(sums_ref)
        for row, rows in (
            (ATTN_GAIN, grad_normed * scaled),
            (ATTN_SHIFT, grad_normed),
            (QUERY_ADD, side_by_side(grad_ref, 0).astype(jnp.float32)),
            (VALUE_ADD, side_by_side(grad_ref, 256).astype(jnp.float32)),
        ):
            sums_ref[row : row + 1, :] = column_sum(rows)


def both_products(left_ref, left_other_ref, right, right_other):
    grad = product_tn(left_ref[...], right) + product_tn(left_other_ref[...], right_other)
    return grad.astype(jnp.bfloat16)


def mlp_weights_kernel(
    active_ref,
    active_other_ref,
    normed_ref,
    normed_other_ref,
    attn_ref,
    attn_other_ref,
    hidden_ref,
    hidden_other_ref,
    mlp_ref,
    mlp_other_ref,
    branch_ref,
    branch_other_ref,
    fc1_proj_ref,
    fc2_ref,
):
    step = pl.program_id(0)
    devices, _, half = fc1_proj_ref.shape
    fc2 = both_products(active_ref, active_other_ref, mlp_ref[...], mlp_other_ref[...])
    fc2_ref[...] = fc2.reshape(fc2_ref.shape)
    fc1 = both_products(normed_ref, normed_other_ref, hidden_ref[...], hidden_other_ref[...])
    start = pl.multiple_of(step * SLAB, SLAB)
    fc1_proj_ref[:, pl.ds(start, SLAB)] = fc1.reshape(devices, SLAB, half)

    @pl.when(step == 0)
    def _():
        proj = both_products(attn_ref, attn_other_ref, branch_ref[...], branch_other_ref[...])
        start = pl.num_programs(0) * SLAB
        fc1_proj_ref[:, start:] = proj.reshape(devices, SLAB, half)


def attn_weights_kernel(
    core_ref, left_ref, left_other_ref, grad_ref, got_ref, small_ref, query_key_ref, value_ref
):
    devices, _, half = value_ref.shape
    for part, ref, start in ((0, query_key_ref, 0), (1, query_key_ref, SLAB), (2, value_ref, 0)):
        right = side_by_side(grad_ref, part * 128, core_ref[0] * 4, 4)
        right_other = side_by_side(got_ref, part * 128, 0, 4)
        grad = both_products(left_ref, left_other_ref, right, right_other)
        ref[:, start : start + SLAB] = grad.reshape(devices, SLAB, half)
    value_ref[:, SLAB:] = small_ref[...]


def like(*shape, dtype=jnp.bfloat16):
    return jax.ShapeDtypeStruct(shape, dtype)


def whole_block(array):
    ndim = len(array.shape)
    return pl.BlockSpec(array.shape, lambda *_: (0,) * ndim)


def params():
    return pltpu.CompilerParams(vmem_limit_bytes=VMEM_LIMIT)


def takes(microseconds):
    return pl.CostEstimate(
        flops=int(microseconds * 1.15e9), transcendentals=0, bytes_accessed=int(microseconds * 3e6)
    )


SCALARS = pl.BlockSpec(memory_space=pltpu.SMEM)


def early_specs(early):
    devices, _, half = early[0].shape
    values = pl.BlockSpec((devices, SLAB, half), lambda i: (0, 0, 0))
    return [whole_block(early[0]), values, whole_block(early[0]), values]


def call_front(core, x, table, early):
    rows, _ = x.shape
    return pl.pallas_call(
        front_kernel,
        grid=(1,),
        in_specs=[SCALARS, whole_block(x), whole_block(table)] + early_specs(early),
        out_specs=pl.BlockSpec((8, rows, 384), lambda i: (0, 0, 0)),
        out_shape=like(8, rows, 384),
        compiler_params=params(),
        cost_estimate=takes(6.5),
    )(core, x, table, *early)


def call_attend(counts, heads):
    images = counts.shape[0]
    heads = heads.reshape(8, images, -1, 384)
    tokens = heads.shape[2]
    out, lse = pl.pallas_call(
        attend_kernel,
        grid=(images,),
        in_specs=[SCALARS, pl.BlockSpec((8, 1, tokens, 384), lambda i: (0, i, 0, 0))],
        out_specs=[
            pl.BlockSpec((8, 1, tokens, 128), lambda i: (0, i, 0, 0)),
            pl.BlockSpec((1, 2, 8 * tokens), lambda i: (i, 0, 0)),
        ],
        out_shape=[
            like(8, images, tokens, 128),
            like(images, 2, 8 * tokens, dtype=jnp.float32),
        ],
        compiler_params=params(),
        cost_estimate=takes(14.3),
    )(counts, heads)
    return out.reshape(8, images * tokens, 128), lse


def call_attend_back(counts, grads, heads, lse):
    images = counts.shape[0]
    heads = heads.reshape(8, images, -1, 384)
    tokens = heads.shape[2]
    out = pl.pallas_call(
        attend_back_kernel,
        grid=(images,),
        in_specs=[
            SCALARS,
            pl.BlockSpec((8, 1, tokens, 128), lambda i: (0, i, 0, 0)),
            pl.BlockSpec((8, 1, tokens, 384), lambda i: (0, i, 0, 0)),
            pl.BlockSpec((1, 2, 8 * tokens), lambda i: (i, 0, 0)),
        ],
        out_specs=pl.BlockSpec((8, 1, tokens, 384), lambda i: (0, i, 0, 0)),
        out_shape=like(*heads.shape),
        compiler_params=params(),
        cost_estimate=takes(16.5),
    )(counts, grads.reshape(8, images, tokens, 128), heads, lse)
    return out.reshape(8, images * tokens, 384)


def rear_weight_specs(late):
    devices, owned, width = late.shape
    fc2_rows = (owned - SLAB) // 2
    steps = fc2_rows // SLAB
    return steps, [
        pl.BlockSpec((devices, SLAB, width), lambda j: (0, 2 * steps, 0)),
        pl.BlockSpec((devices, SLAB, width), lambda j: (0, steps + j, 0)),
        pl.BlockSpec((devices // steps, fc2_rows, width), lambda j: (j, 0, 0)),
    ]


def call_rear(keep, x, attn, table, late):
    rows, width = x.shape
    steps, weight_specs = rear_weight_specs(late)
    full = like(rows, width, dtype=jnp.float32)
    column = pl.BlockSpec((rows, width), lambda j: (0, j))
    out_shape, out_specs = [like(rows, width)], [whole_block(x)]
    if keep:
        left = like(rows, (steps + 3) * width)
        out_shape += [full, like(rows, steps * width, dtype=jnp.float32), full, left]
        out_specs += [whole_block(x), column, whole_block(x), whole_block(left)]
    return pl.pallas_call(
        functools.partial(rear_kernel, keep),
        grid=(steps,),
        in_specs=[whole_block(member) for member in (x, attn, table)] + weight_specs,
        out_specs=out_specs,
        out_shape=out_shape,
        scratch_shapes=[
            pltpu.VMEM((rows, width), jnp.bfloat16),
            pltpu.VMEM((rows, width), jnp.float32),
            pltpu.VMEM((rows, width), jnp.float32),
        ],
        compiler_params=params(),
        cost_estimate=takes(13),
    )(x, attn, table, late, late, late)


def call_rear_back(keep, core, grad, x, branch, hidden, mlp, table, late):
    rows, width = x.shape
    steps, weight_specs = rear_weight_specs(late)
    column = pl.BlockSpec((rows, width), lambda j: (0, j))
    attn_grad = like(8, rows, 128)
    out_shape = [attn_grad, like(rows, width, dtype=jnp.float32)]
    out_specs = [whole_block(attn_grad), whole_block(x)]
    if keep:
        right = like(rows, (steps + 2) * width // 2)
        out_shape += [right, right]
        out_specs += [whole_block(right), whole_block(right)]
        out_shape += [like(*table.shape, dtype=jnp.float32)]
        out_specs += [whole_block(table)]
    return pl.pallas_call(
        functools.partial(rear_back_kernel, keep),
        grid=(steps,),
        in_specs=[
            SCALARS,
            whole_block(grad),
            whole_block(x),
            whole_block(branch),
            column,
            whole_block(mlp),
            whole_block(table),
        ]
        + weight_specs,
        out_specs=out_specs,
        out_shape=out_shape,
        scratch_shapes=[
            pltpu.VMEM((rows, width), jnp.bfloat16),
            pltpu.VMEM((rows, width), jnp.float32),
        ],
        compiler_params=params(),
        cost_estimate=takes(16),
    )(core, grad, x, branch, hidden, mlp, table, late, late, late)


def call_front_back(keep, core, grad_qkv, grad_middle, x, table, early):
    rows, width = x.shape
    out_shape, out_specs = [like(rows, width)], [whole_block(x)]
    if keep:
        out_shape += [like(*table.shape, dtype=jnp.float32)]
        out_specs += [whole_block(table)]
    return pl.pallas_call(
        functools.partial(front_back_kernel, keep),
        grid=(1,),
        in_specs=[SCALARS]
        + [whole_block(member) for member in (grad_qkv, grad_middle, x, table)]
        + early_specs(early),
        out_specs=out_specs,
        out_shape=out_shape,
        compiler_params=params(),
        cost_estimate=takes(7),
    )(core, grad_qkv, grad_middle, x, table, *early)


def call_mlp_weights(left, left_other, right, right_other, devices, owned):
    rows = left.shape[0]
    steps = owned // SLAB
    width, half = 1024, 512

    def column(size, at):
        return pl.BlockSpec((rows, size), lambda j: (0, at))

    by_step = [pl.BlockSpec((rows, size), lambda j: (0, j)) for size in (width, half)]
    out_shape = [like(devices, owned + SLAB, half), like(devices, owned, half)]
    return pl.pallas_call(
        mlp_weights_kernel,
        grid=(steps,),
        in_specs=[by_step[0]] * 2
        + [column(width, MLP_NORMED)] * 2
        + [column(width, ATTN_OUT)] * 2
        + [by_step[1]] * 2
        + [column(half, MLP_GRAD)] * 2
        + [column(half, BRANCH_GRAD)] * 2,
        out_specs=[
            whole_block(out_shape[0]),
            pl.BlockSpec((devices // steps, owned, half), lambda j: (j, 0, 0)),
        ],
        out_shape=out_shape,
        compiler_params=params(),
        cost_estimate=takes(9),
    )(*(left, left_other) * 3, *(right, right_other) * 3)


def call_attn_weights(core, left, left_other, grads, got, small):
    column = pl.BlockSpec((left.shape[0], 1024), lambda i: (0, ATTN_NORMED))
    shape = like(small.shape[0], 2 * SLAB, 512)
    return pl.pallas_call(
        attn_weights_kernel,
        grid=(1,),
        in_specs=[SCALARS, column, column]
        + [whole_block(operand) for operand in (grads, got, small)],
        out_specs=[whole_block(shape), whole_block(shape)],
        out_shape=[shape, shape],
        compiler_params=params(),
        cost_estimate=takes(8),
    )(core, left, left_other, grads, got, small)


def small_slab(vectors, hidden_vector):
    lead = vectors.shape[:-2]
    row = jnp.concatenate([vectors.reshape(lead + (-1,)), hidden_vector], axis=-1)
    return jnp.pad(
        row[..., None, :], [(0, 0)] * len(lead) + [(0, SLAB - 1), (0, SMALL_WIDTH - row.shape[-1])]
    )


def table_of(slabs):
    row = slabs.astype(jnp.float32)
    vectors = row[:, : HIDDEN_ROW * SLAB].reshape(-1, HIDDEN_ROW, SLAB)
    vectors = vectors.transpose(1, 0, 2).reshape(HIDDEN_ROW, -1)
    start = HIDDEN_ROW * SLAB
    hidden = row[:, start : start + 64].reshape(-1, vectors.shape[1])
    return jnp.pad(
        jnp.concatenate([vectors, hidden]),
        [(0, TABLE_ROWS - HIDDEN_ROW - hidden.shape[0]), (0, 0)],
    )


def slabs_of(sums, devices):
    vectors = sums[:HIDDEN_ROW].reshape(HIDDEN_ROW, devices, SLAB).transpose(1, 0, 2)
    hidden = sums[HIDDEN_ROW : HIDDEN_ROW + 4].reshape(devices, -1)
    return small_slab(vectors, hidden).astype(jnp.bfloat16)


def column_slabs(rows):
    count = rows.shape[1] // 1024
    return rows.reshape(SLAB, count, 1024).transpose(1, 0, 2).reshape(count * SLAB, 1024)


def from_column_slabs(rows):
    count = rows.shape[0] // SLAB
    return rows.reshape(count, SLAB, 1024).transpose(1, 0, 2).reshape(SLAB, count * 1024)


def on_device(
    images,
    key_mask,
    image_order,
    attn_norm_gain,
    attn_norm_bias,
    qkv_weight,
    query_bias,
    value_bias,
    proj_weight,
    proj_bias,
    attn_scale,
    mlp_norm_gain,
    mlp_norm_bias,
    fc1_weight,
    fc1_bias,
    fc2_weight,
    fc2_bias,
    mlp_scale,
    cotangent,
):
    section_index = lax.axis_index("section")
    local_images, tokens_here, features = images.shape
    rows = local_images * tokens_here
    reversed_order = image_order[0] > image_order[1]
    core = (lax.axis_index("head") % 2).astype(jnp.int32).reshape(1)

    vectors = jnp.concatenate(
        [
            attn_norm_gain,
            attn_norm_bias,
            query_bias,
            value_bias,
            proj_bias,
            attn_scale,
            mlp_norm_gain,
            mlp_norm_bias,
            fc2_bias,
            mlp_scale,
        ]
    )
    late_shard = jnp.concatenate([fc2_weight[0], column_slabs(fc1_weight[0]), proj_weight[0]])
    late = lax.all_gather(late_shard, ("dp", "head"), axis=0)
    devices = late.shape[0]
    small_shard = jnp.pad(
        small_slab(vectors, fc1_bias[0]), [(0, 0), (0, features - SMALL_WIDTH)]
    )
    early_shard = jnp.concatenate([column_slabs(qkv_weight[0]), small_shard])
    ways = ("dp", "head")
    chip = spread_chip(early_shard)
    lanes = [
        spread_lane(chip[:, :, : 2 * SLAB], "dp"),
        spread_lane(chip[:, :, 2 * SLAB :], "head"),
    ]
    ends = [spread_ends(lane, way) for lane, way in zip(lanes, ways)]
    spread_parts = [spread_rest(*item) for item in zip(lanes, ends, ways)]
    early = [part[at] for at in range(2) for part in spread_parts]
    table = table_of(jnp.where(core == 0, early[1][:, SLAB], early[3][:, SLAB]))

    own_images = jnp.where(reversed_order, images[::-1], images).reshape(rows, features)
    counts = jnp.sum(key_mask, axis=1, dtype=jnp.int32)
    counts = jnp.where(reversed_order, counts[::-1], counts)

    def attention(x):
        heads = to_peers(call_front(core, x, table, early))
        attn, lse = call_attend(counts, heads)
        return heads, lse, to_peers(attn)

    (passed,) = call_rear(False, own_images, attention(own_images)[2], table, late)
    x = jnp.where(section_index == 0, own_images, shifted(passed, 1))
    heads, lse, attn = attention(x)
    result, *rear_state, left = call_rear(True, x, attn, table, late)
    left_other = swap(left, "head")

    own_grad = cotangent.reshape(rows, features)
    rear = call_rear_back(False, core, own_grad, x, *rear_state, table, late)
    grad_qkv = to_peers(call_attend_back(counts, to_peers(rear[0]), heads, lse))
    (passed_back,) = call_front_back(False, core, grad_qkv, rear[1], x, table, early)
    passed_back = after(passed_back, left_other)
    grad = jnp.where(section_index == 0, shifted(passed_back, -1), own_grad)

    rear = call_rear_back(True, core, grad, x, *rear_state, table, late)
    grad_attn, grad_middle, right, right_other, rear_sums = rear
    fc1_proj, fc2 = call_mlp_weights(
        left, left_other, right, swap(right_other, "head"), devices, 4 * SLAB
    )
    grad_heads = after(to_peers(grad_attn), fc2)
    mlp_terms = [by_chip(fc1_proj), by_chip(fc2)]
    mlp_halves = [ring_halves(terms, way) for terms, way in zip(mlp_terms, ways)]
    grad_qkv = call_attend_back(counts, grad_heads, heads, lse)
    grad_qkv = to_peers(after(grad_qkv, mlp_halves))
    mlp_ends = [ring_ends(*item) for item in zip(mlp_terms, mlp_halves, ways)]

    got = swap(lax.dynamic_slice_in_dim(grad_qkv, (1 - core[0]) * 4, 4), "head")
    input_grad, front_sums = call_front_back(
        True, core, grad_qkv, grad_middle, x, table, early
    )
    small = slabs_of(rear_sums + front_sums, devices)
    attn_terms = call_attn_weights(core, left, left_other, grad_qkv, got, small)
    attn_terms = [by_chip(terms) for terms in attn_terms]
    mlp_ends = after(mlp_ends, attn_terms)
    attn_totals = [ring_first(*item) for item in zip(attn_terms, ways)]
    mlp_totals = [ring_total(*item) for item in zip(mlp_terms, mlp_ends, ways)]
    ring_sums = [
        second_ring(jnp.concatenate(totals, axis=3), way)
        for *totals, way in zip(mlp_totals, attn_totals, ways)
    ]
    shard_grad = collect_rest(jnp.concatenate(ring_sums, axis=2))
    fc1_grad, proj_grad, query_key_grad, fc2_grad, value_grad, small_row = (
        shard_grad[start * SLAB : stop * SLAB]
        for start, stop in ((0, 4), (4, 5), (5, 7), (7, 11), (11, 12), (12, 13))
    )
    qkv_grad = from_column_slabs(jnp.concatenate([query_key_grad, value_grad]))
    row = small_row[0, :SMALL_WIDTH] + small_row[0, SMALL_WIDTH:]
    small_grads = row[: HIDDEN_ROW * SLAB].reshape(HIDDEN_ROW, SLAB)
    fc1_bias_grad = row[HIDDEN_ROW * SLAB : HIDDEN_ROW * SLAB + 64]

    layer_out = result.reshape(images.shape)
    input_grad = input_grad.reshape(images.shape)
    input_grad = jnp.where(
        (section_index == 0) & reversed_order, input_grad[::-1], input_grad
    )
    outs = (
        layer_out,
        input_grad,
        small_grads[ATTN_GAIN],
        small_grads[ATTN_SHIFT],
        qkv_grad,
        small_grads[QUERY_ADD],
        small_grads[VALUE_ADD],
        proj_grad,
        small_grads[PROJ_ADD],
        small_grads[ATTN_LAYER],
        small_grads[MLP_GAIN],
        small_grads[MLP_SHIFT],
        from_column_slabs(fc1_grad),
        fc1_bias_grad,
        fc2_grad,
        small_grads[FC2_ADD],
        small_grads[MLP_LAYER],
    )
    return tuple(member[None] for member in outs)


def solution(mesh):
    tokens = P("dp", "head", None)
    vec = P("section", ("dp", "head"))
    mat = P("section", ("dp", "head"), None)
    in_specs = (
        (tokens, P("dp", None), P("dp"), vec, vec, mat, vec, vec, mat, vec, vec, vec, vec)
        + (mat, vec, mat, vec, vec, tokens)
    )
    out_tokens = P("section", "dp", "head", None)
    out_specs = (
        (out_tokens, out_tokens, vec, vec, mat, vec, vec, mat, vec, vec, vec, vec, mat, vec)
        + (mat, vec, vec)
    )
    return jax.shard_map(
        on_device, mesh=mesh, in_specs=in_specs, out_specs=out_specs, check_vma=False
    )
```

```python
import functools

import jax
import jax.numpy as jnp
from jax import lax
from jax.experimental import pallas as pl
from jax.experimental.pallas import tpu as pltpu
from jax.sharding import PartitionSpec as P

DH = 64
MASKED_SCORE = -1e30
NORM_EPSILON = 1e-06
ROOT_HALF = 0.7071067811865476
DENSITY_SCALE = 0.3989422804014327
SCORE_SCALE = DH ** (-0.5)
SLAB = 16
SMALL_WIDTH = 512
QUERY_ROWS = 512
BACK_ROWS = 128
PIECES = 1
VMEM_LIMIT = 60 * 1024 * 1024

(
    ATTN_GAIN,
    ATTN_SHIFT,
    QUERY_ADD,
    VALUE_ADD,
    PROJ_ADD,
    ATTN_LAYER,
    MLP_GAIN,
    MLP_SHIFT,
    FC2_ADD,
    MLP_LAYER,
) = range(10)
HIDDEN_ROW = 10
TABLE_ROWS = 16

MLP_NORMED, ATTN_OUT = 4, 5
MLP_GRAD, BRANCH_GRAD = 4, 5


def hop(block, axis, places):
    size = lax.axis_size(axis)
    return lax.ppermute(block, axis, [(i, (i + 2 * places) % size) for i in range(size)])


def swap(block, axis):
    size = lax.axis_size(axis)
    return lax.ppermute(block, axis, [(i, i ^ 1) for i in range(size)])


def coordinates():
    dp_index, head_index = lax.axis_index("dp"), lax.axis_index("head")
    return dp_index // 2, dp_index % 2, head_index // 2, head_index % 2


def after(value, *others):
    return lax.optimization_barrier((value,) + others)[0]


def blank(shape, given):
    def kernel(given_ref, out_ref):
        pass

    anywhere = pl.BlockSpec(memory_space=pl.ANY)
    return pl.pallas_call(
        kernel,
        in_specs=[anywhere],
        out_specs=anywhere,
        out_shape=jax.ShapeDtypeStruct(shape, given.dtype),
    )(given)


def by_core(core, mine, other, axis):
    return jnp.where(
        core == 0,
        jnp.concatenate([mine, other], axis=axis),
        jnp.concatenate([other, mine], axis=axis),
    )


def spread_chip(shard):
    _, z_me, _, core_me = coordinates()
    half = shard.shape[1] // 2
    first, second = shard[:, :half], shard[:, half:]
    mine = jnp.where(core_me == 0, first, second)[None]
    cores = by_core(core_me, mine, swap(jnp.where(core_me == 0, second, first), "head")[None], 0)
    return by_core(z_me, cores[None], swap(cores, "dp")[None], 0)


def spread_lane(pair, last_axis):
    x_me, _, y_me, _ = coordinates()
    x_size, y_size = lax.axis_size("dp") // 2, lax.axis_size("head") // 2
    shape = pair.shape[1:]
    zeros = (0,) * len(shape)
    along_y = last_axis == "dp"
    axis, me, size = ("head", y_me, y_size) if along_y else ("dp", x_me, x_size)
    lane = blank(((2, size) if along_y else (size, 2)) + shape, pair)
    for places in range(size):
        came = pair if places == 0 else hop(pair, axis, places)
        source = (me - places) % size
        if along_y:
            lane = lax.dynamic_update_slice(lane, came[:, None], (0, source) + zeros)
        else:
            lane = lax.dynamic_update_slice(lane, came[None], (source, 0) + zeros)
    return lane


def spread_ends(lane, last_axis):
    return hop(lane, last_axis, 1), hop(lane, last_axis, -1)


def spread_rest(lane, ends, last_axis):
    x_me, _, y_me, _ = coordinates()
    x_size, y_size = lax.axis_size("dp") // 2, lax.axis_size("head") // 2
    along_x = last_axis == "dp"
    me, size = (x_me, x_size) if along_x else (y_me, y_size)
    low, high = ends
    half = lane.shape[0] // 2
    far = (hop(low[:half], last_axis, 1), hop(high[half:], last_axis, -1))
    shape = lane.shape[2:]
    zeros = (0,) * len(shape)
    near = blank((x_size, 2, y_size) + shape, lane)
    for places, at, block in (
        (0, 0, lane),
        (1, 0, low),
        (-1, 0, high),
        (2, 0, far[0]),
        (2, half, far[1]),
    ):
        source = (me - places) % size
        if along_x:
            near = lax.dynamic_update_slice(near, block[None], (source, at, 0) + zeros)
        else:
            near = lax.dynamic_update_slice(near, block[:, :, None], (at, 0, source) + zeros)
    near = near.reshape((-1,) + shape[1:])
    return near, swap(near, "head")


def piece(terms, at, dim):
    return lax.dynamic_index_in_dim(terms, at, dim, keepdims=False)


def by_chip(terms):
    x_size, y_size = lax.axis_size("dp") // 2, lax.axis_size("head") // 2
    return terms.reshape((x_size, 2, y_size, 2) + terms.shape[1:])


def ring_halves(terms, axis):
    x_me, _, y_me, _ = coordinates()
    dim, me, size = (0, x_me, 4) if axis == "dp" else (2, y_me, 4)
    far = piece(terms, (me + 2) % size, dim)
    half = far.shape[0] // 2
    return hop(far[:half], axis, 1), hop(far[half:], axis, -1)


def ring_ends(terms, passed, axis):
    x_me, _, y_me, _ = coordinates()
    dim, me, size = (0, x_me, 4) if axis == "dp" else (2, y_me, 4)
    low, high = (part.astype(jnp.float32) for part in passed)
    up = piece(terms, (me + 1) % size, dim).astype(jnp.float32)
    down = piece(terms, (me - 1) % size, dim).astype(jnp.float32)
    half = up.shape[0] // 2
    up = jnp.concatenate([up[:half] + low, up[half:]]).astype(jnp.bfloat16)
    down = jnp.concatenate([down[:half], down[half:] + high]).astype(jnp.bfloat16)
    return hop(up, axis, 1), hop(down, axis, -1)


def ring_total(terms, ends, axis):
    x_me, _, y_me, _ = coordinates()
    own = piece(terms, x_me, 0) if axis == "dp" else piece(terms, y_me, 2)
    total = sum((end.astype(jnp.float32) for end in ends), own.astype(jnp.float32))
    return total.astype(jnp.bfloat16)


def ring_direct(terms, axis, dim, me):
    own = piece(terms, me, dim).astype(jnp.float32)
    for places in (1, 2, 3):
        own = own + hop(piece(terms, (me + places) % 4, dim), axis, places).astype(jnp.float32)
    return own


def ring_first(terms, axis):
    x_me, _, y_me, _ = coordinates()
    dim, me = (0, x_me) if axis == "dp" else (2, y_me)
    return ring_direct(terms, axis, dim, me).astype(jnp.bfloat16)


def second_ring(terms, first_axis):
    x_me, _, y_me, _ = coordinates()
    if first_axis == "dp":
        return ring_direct(terms, "head", 1, y_me)
    return ring_direct(terms, "dp", 0, x_me)


def collect_rest(terms):
    _, z_me, _, core_me = coordinates()
    away = piece(terms, 1 - z_me, 0).astype(jnp.bfloat16)
    cores = piece(terms, z_me, 0) + swap(away, "dp").astype(jnp.float32)
    got = swap(piece(cores, 1 - core_me, 0).astype(jnp.bfloat16), "head").astype(jnp.float32)
    return by_core(core_me, piece(cores, core_me, 0), got, 1)


def collect_heads(terms):
    x_me, z_me, _, _ = coordinates()
    peers = lax.axis_size("head")
    blocks = terms.reshape(lax.axis_size("dp") // 2, 2, -1, terms.shape[1])
    blocks = ring_direct(blocks, "dp", 0, x_me)
    away = piece(blocks, 1 - z_me, 0).astype(jnp.bfloat16)
    total = piece(blocks, z_me, 0) + swap(away, "dp").astype(jnp.float32)
    parts = to_peers(total.astype(jnp.bfloat16).reshape(peers, -1, terms.shape[1]))
    rows = parts.shape[1]
    parts = parts.reshape(peers, rows, 3, -1).transpose(1, 2, 0, 3)
    return parts.reshape(rows, -1).astype(jnp.float32)


def to_peers(blocks):
    return lax.all_to_all(blocks, "head", split_axis=0, concat_axis=0, tiled=True)


def shifted(block, distance):
    size = lax.axis_size("section")
    route = [(i, i + distance) for i in range(size) if 0 <= i + distance < size]
    return lax.ppermute(block, "section", route)


def ahead(items, function):
    value = function(items[0])
    for at, item in enumerate(items):
        later = function(items[at + 1]) if at + 1 < len(items) else None
        yield item, value
        value = later


def norm_stats(rows):
    centre = rows - jnp.mean(rows, axis=-1, keepdims=True)
    inverse = lax.rsqrt(jnp.mean(centre * centre, axis=-1, keepdims=True) + NORM_EPSILON)
    return centre * inverse, inverse


def norm_back(grad_norm, scaled, inverse):
    first_mean = jnp.mean(grad_norm, axis=-1, keepdims=True)
    second_mean = jnp.mean(grad_norm * scaled, axis=-1, keepdims=True)
    return inverse * (grad_norm - first_mean - scaled * second_mean)


def product(left, right):
    return jnp.dot(left, right, preferred_element_type=jnp.float32)


def product_nt(left, right):
    return lax.dot_general(
        left, right, (((1,), (1,)), ((), ())), preferred_element_type=jnp.float32
    )


def product_tn(left, right):
    return lax.dot_general(
        left, right, (((0,), (0,)), ((), ())), preferred_element_type=jnp.float32
    )


def flat(block):
    return block.reshape(-1, block.shape[-1])


def column_sum(rows):
    return jnp.sum(rows, axis=0, keepdims=True)


def vector(table_ref, row):
    return table_ref[row : row + 1, :]


def side_by_side(blocks_ref, start=0, first=0, count=8):
    return jnp.concatenate(
        [blocks_ref[first + peer, :, start : start + 128] for peer in range(count)], axis=1
    )


def put_side_by_side(blocks_ref, rows, start=0, first=0):
    for peer in range(rows.shape[1] // 128):
        blocks_ref[first + peer, :, start : start + 128] = rows[
            :, peer * 128 : (peer + 1) * 128
        ].astype(blocks_ref.dtype)


def put_column(ref, at, rows):
    width = rows.shape[1]
    start = at * width if isinstance(at, int) else pl.multiple_of(at * width, width)
    ref[:, pl.ds(start, width)] = rows


def halves(core, rows):
    half = rows.shape[1] // 2
    first, second = rows[:, :half], rows[:, half:]
    return jnp.where(core == 0, first, second), jnp.where(core == 0, second, first)


def attn_normed(rows, table_ref):
    scaled, inverse = norm_stats(rows)
    normed = (scaled * vector(table_ref, ATTN_GAIN) + vector(table_ref, ATTN_SHIFT)).astype(
        jnp.bfloat16
    )
    return normed, scaled, inverse


def mlp_normed(middle, table_ref):
    scaled, inverse = norm_stats(middle)
    normed = (scaled * vector(table_ref, MLP_GAIN) + vector(table_ref, MLP_SHIFT)).astype(
        jnp.bfloat16
    )
    return normed, scaled, inverse


def cumulative(hidden):
    return 0.5 * (1.0 + lax.erf(hidden * ROOT_HALF))


def front_kernel(
    core_ref, x_ref, table_ref, qk_mine_ref, v_mine_ref, qk_other_ref, v_other_ref, out_ref, normed_ref
):
    core = core_ref[0]
    normed, _, _ = attn_normed(x_ref[...].astype(jnp.float32), table_ref)
    normed_ref[...] = normed
    query_adds = halves(core, vector(table_ref, QUERY_ADD))
    value_adds = halves(core, vector(table_ref, VALUE_ADD))
    for at, (qk_ref, v_ref) in enumerate(
        ((qk_mine_ref, v_mine_ref), (qk_other_ref, v_other_ref))
    ):
        first = (core if at == 0 else 1 - core) * 4
        queries = product(normed, flat(qk_ref[:, :SLAB])) + query_adds[at]
        put_side_by_side(out_ref, queries, 0, first)
        put_side_by_side(out_ref, product(normed, flat(qk_ref[:, SLAB:])), 128, first)
        values = product(normed, flat(v_ref[...])) + value_adds[at]
        put_side_by_side(out_ref, values, 256, first)


def marked(rows, mark):
    first = lax.broadcasted_iota(jnp.int32, rows.shape, 1) == 0
    return jnp.concatenate([rows, jnp.where(first, mark, 0.0).astype(jnp.bfloat16)], axis=1)


def masked_keys(block, count, head):
    keys = block[:, 128 + head * DH : 128 + (head + 1) * DH]
    valid = lax.broadcasted_iota(jnp.int32, keys.shape, 0) < count
    return marked(keys, jnp.where(valid, 0.0, MASKED_SCORE))


def scaled_queries(block, start, count, head):
    queries = block[start : start + count, head * DH : (head + 1) * DH]
    return marked((queries.astype(jnp.float32) * SCORE_SCALE).astype(jnp.bfloat16), 1.0)


def attend_kernel(count_ref, heads_ref, out_ref, lse_ref):
    count = count_ref[pl.program_id(0)]
    block = flat(heads_ref[:, 0])
    seq_len = block.shape[0]
    keys = [masked_keys(block, count, head) for head in range(2)]
    values = [block[:, 256 + head * DH : 256 + (head + 1) * DH] for head in range(2)]
    values = [jnp.concatenate([part, jnp.ones_like(part)], axis=1) for part in values]
    outs = []

    def scores_of(item):
        start, head = item
        return product_nt(keys[head], scaled_queries(block, start, QUERY_ROWS, head))

    items = [(start, head) for start in range(0, seq_len, QUERY_ROWS) for head in range(2)]
    for (start, head), scores in ahead(items, scores_of):
        largest = jnp.max(scores, axis=0, keepdims=True)
        weights = jnp.exp(scores - largest)
        mixed = product_tn(values[head], weights.astype(jnp.bfloat16))
        total = mixed[DH : DH + 1]
        outs.append((mixed[:DH] / total).T)
        lse_ref[0, head : head + 1, start : start + QUERY_ROWS] = largest + jnp.log(total)
        if head == 1:
            rows = jnp.concatenate(outs[-2:], axis=1).astype(jnp.bfloat16)
            peers = QUERY_ROWS // 128
            out_ref[start // 128 : start // 128 + peers, 0] = rows.reshape(peers, 128, 128)


def attend_back_kernel(count_ref, grad_ref, heads_ref, lse_ref, out_ref):
    count = count_ref[pl.program_id(0)]
    block = flat(heads_ref[:, 0])
    grads = flat(grad_ref[:, 0])
    seq_len = block.shape[0]
    peers = BACK_ROWS // 128
    keys = [masked_keys(block, count, head) for head in range(2)]
    values = [block[:, 256 + head * DH : 256 + (head + 1) * DH] for head in range(2)]
    key_sums = [jnp.zeros((seq_len, DH), jnp.float32) for _ in range(2)]
    value_sums = [jnp.zeros((seq_len, DH), jnp.float32) for _ in range(2)]
    outs = []

    def products_of(item):
        start, head = item
        queries = scaled_queries(block, start, BACK_ROWS, head)
        grad_rows = grads[start : start + BACK_ROWS, head * DH : (head + 1) * DH]
        scores = product_nt(keys[head], queries)
        return queries, grad_rows, scores, product_nt(values[head], grad_rows)

    items = [(start, head) for start in range(0, seq_len, BACK_ROWS) for head in range(2)]
    for (start, head), members in ahead(items, products_of):
        queries, grad_rows, scores, grad_weights = members
        weights = jnp.exp(scores - lse_ref[0, head : head + 1, start : start + BACK_ROWS])
        shares = weights * grad_weights
        dots = jnp.sum(shares, axis=0, keepdims=True)
        grad_scores = (shares - weights * dots).astype(jnp.bfloat16)
        value_sums[head] += product(weights.astype(jnp.bfloat16), grad_rows)
        key_sums[head] += product(grad_scores, queries[:, :DH])
        outs.append((product_tn(keys[head][:, :DH], grad_scores) * SCORE_SCALE).T)
        if head == 1:
            rows = jnp.concatenate(outs[-2:], axis=1).astype(jnp.bfloat16)
            at = start // 128
            out_ref[at : at + peers, 0, :, :128] = rows.reshape(peers, 128, 128)
    key_rows = jnp.concatenate(key_sums, axis=1).astype(jnp.bfloat16)
    value_rows = jnp.concatenate(value_sums, axis=1).astype(jnp.bfloat16)
    out_ref[:, 0, :, 128:256] = key_rows.reshape(-1, 128, 128)
    out_ref[:, 0, :, 256:] = value_rows.reshape(-1, 128, 128)


def hidden_pieces(fc1_ref, fc2_ref):
    columns, owners = fc1_ref.shape[2] // PIECES, fc2_ref.shape[0] // PIECES
    return [
        (slice(at * columns, (at + 1) * columns), slice(at * owners, (at + 1) * owners))
        for at in range(PIECES)
    ]


def rear_kernel(keep, x_ref, attn_ref, table_ref, proj_ref, fc1_ref, fc2_ref, *rest):
    if keep:
        result_ref, branch_ref, hidden_ref, mlp_ref, left_ref, normed, middle, total = rest
    else:
        result_ref, normed, middle, total = rest
    step = pl.program_id(0)

    @pl.when(step == 0)
    def _():
        attn = side_by_side(attn_ref)
        branch = product(attn, flat(proj_ref[...])) + vector(table_ref, PROJ_ADD)
        rows = x_ref[...].astype(jnp.float32)
        middle[...] = rows + vector(table_ref, ATTN_LAYER) * branch
        normed[...] = mlp_normed(middle[...], table_ref)[0]
        if keep:
            branch_ref[...] = branch
            put_column(left_ref, MLP_NORMED, normed[...])
            put_column(left_ref, ATTN_OUT, attn)
        total[...] = jnp.broadcast_to(vector(table_ref, FC2_ADD), total.shape)

    adds = table_ref[pl.ds(HIDDEN_ROW + step, 1), :]
    actives, mixed = [], 0.0

    def hidden_of(item):
        return product(normed[...], flat(fc1_ref[:, :, item[0]])) + adds[:, item[0]]

    for (columns, owners), hidden in ahead(hidden_pieces(fc1_ref, fc2_ref), hidden_of):
        if keep:
            hidden_ref[:, columns] = hidden
        actives.append((hidden * cumulative(hidden)).astype(jnp.bfloat16))
        mixed += product(actives[-1], flat(fc2_ref[owners]))
    if keep:
        put_column(left_ref, step, jnp.concatenate(actives, axis=1))
    total[...] += mixed

    @pl.when(step == pl.num_programs(0) - 1)
    def _():
        if keep:
            mlp_ref[...] = total[...]
        result = middle[...] + vector(table_ref, MLP_LAYER) * total[...]
        result_ref[...] = result.astype(jnp.bfloat16)


def rear_back_kernel(
    keep,
    core_ref,
    grad_ref,
    x_ref,
    branch_ref,
    hidden_ref,
    mlp_ref,
    table_ref,
    proj_ref,
    fc1_ref,
    fc2_ref,
    attn_grad_ref,
    middle_grad_ref,
    *rest,
):
    if keep:
        mine_ref, other_ref, sums_ref = rest[:3]
    mlp_low, total = rest[-2:]
    step = pl.program_id(0)

    def put_right(at, rows):
        mine, other = halves(core_ref[0], rows)
        put_column(mine_ref, at, mine)
        put_column(other_ref, at, other)

    @pl.when(step == 0)
    def _():
        grad_mlp = vector(table_ref, MLP_LAYER) * grad_ref[...].astype(jnp.float32)
        mlp_low[...] = grad_mlp.astype(jnp.bfloat16)
        total[...] = jnp.zeros_like(total)
        if keep:
            sums_ref[...] = jnp.zeros_like(sums_ref)
            sums_ref[FC2_ADD : FC2_ADD + 1, :] = column_sum(grad_mlp)
            put_right(MLP_GRAD, mlp_low[...])

    lows, sums, mixed = [], [], 0.0

    def active_grad_of(item):
        return product_nt(mlp_low[...], flat(fc2_ref[item[1]]))

    for (columns, _), grad in ahead(hidden_pieces(fc1_ref, fc2_ref), active_grad_of):
        hidden = hidden_ref[:, columns]
        slope = cumulative(hidden) + hidden * (jnp.exp(-0.5 * hidden * hidden) * DENSITY_SCALE)
        grad_hidden = grad * slope
        lows.append(grad_hidden.astype(jnp.bfloat16))
        sums.append(column_sum(grad_hidden))
        mixed += product_nt(lows[-1], flat(fc1_ref[:, :, columns]))
    total[...] += mixed
    if keep:
        sums_ref[pl.ds(HIDDEN_ROW + step, 1), :] = jnp.concatenate(sums, axis=1)
        put_right(step, jnp.concatenate(lows, axis=1))

    @pl.when(step == pl.num_programs(0) - 1)
    def _():
        grad_rows = grad_ref[...].astype(jnp.float32)
        branch = branch_ref[...]
        middle = x_ref[...].astype(jnp.float32) + vector(table_ref, ATTN_LAYER) * branch
        _, scaled, inverse = mlp_normed(middle, table_ref)
        grad_normed = total[...]
        grad_middle = grad_rows + norm_back(
            grad_normed * vector(table_ref, MLP_GAIN), scaled, inverse
        )
        middle_grad_ref[...] = grad_middle
        grad_branch = vector(table_ref, ATTN_LAYER) * grad_middle
        branch_low = grad_branch.astype(jnp.bfloat16)
        put_side_by_side(attn_grad_ref, product_nt(branch_low, flat(proj_ref[...])))
        if keep:
            put_right(BRANCH_GRAD, branch_low)
            for row, rows in (
                (MLP_LAYER, grad_rows * mlp_ref[...]),
                (MLP_GAIN, grad_normed * scaled),
                (MLP_SHIFT, grad_normed),
                (ATTN_LAYER, grad_middle * branch),
                (PROJ_ADD, grad_branch),
            ):
                sums_ref[row : row + 1, :] = column_sum(rows)


def front_back_kernel(
    keep,
    core_ref,
    grad_ref,
    middle_grad_ref,
    x_ref,
    table_ref,
    qk_mine_ref,
    v_mine_ref,
    qk_other_ref,
    v_other_ref,
    *rest,
):
    if keep:
        out_ref, sums_ref = rest
    else:
        (out_ref,) = rest
    core = core_ref[0]
    grad_normed = 0.0
    for at, (qk_ref, v_ref) in enumerate(
        ((qk_mine_ref, v_mine_ref), (qk_other_ref, v_other_ref))
    ):
        first = (core if at == 0 else 1 - core) * 4
        queries, keys, values = (
            side_by_side(grad_ref, start, first, 4) for start in (0, 128, 256)
        )
        grad_normed += product_nt(queries, flat(qk_ref[:, :SLAB]))
        grad_normed += product_nt(keys, flat(qk_ref[:, SLAB:]))
        grad_normed += product_nt(values, flat(v_ref[...]))
    _, scaled, inverse = attn_normed(x_ref[...].astype(jnp.float32), table_ref)
    grad_input = middle_grad_ref[...] + norm_back(
        grad_normed * vector(table_ref, ATTN_GAIN), scaled, inverse
    )
    out_ref[...] = grad_input.astype(jnp.bfloat16)
    if keep:
        sums_ref[...] = jnp.zeros_like(sums_ref)
        for row, rows in (
            (ATTN_GAIN, grad_normed * scaled),
            (ATTN_SHIFT, grad_normed),
            (QUERY_ADD, side_by_side(grad_ref, 0).astype(jnp.float32)),
            (VALUE_ADD, side_by_side(grad_ref, 256).astype(jnp.float32)),
        ):
            sums_ref[row : row + 1, :] = column_sum(rows)


def both_products(left_ref, left_other_ref, right, right_other):
    grad = product_tn(left_ref[...], right) + product_tn(left_other_ref[...], right_other)
    return grad.astype(jnp.bfloat16)


def mlp_weights_kernel(
    active_ref,
    active_other_ref,
    normed_ref,
    normed_other_ref,
    attn_ref,
    attn_other_ref,
    hidden_ref,
    hidden_other_ref,
    mlp_ref,
    mlp_other_ref,
    branch_ref,
    branch_other_ref,
    fc1_proj_ref,
    fc2_ref,
):
    step = pl.program_id(0)
    devices, _, half = fc1_proj_ref.shape
    fc2 = both_products(active_ref, active_other_ref, mlp_ref[...], mlp_other_ref[...])
    fc2_ref[...] = fc2.reshape(fc2_ref.shape)
    fc1 = both_products(normed_ref, normed_other_ref, hidden_ref[...], hidden_other_ref[...])
    start = pl.multiple_of(step * SLAB, SLAB)
    fc1_proj_ref[:, pl.ds(start, SLAB)] = fc1.reshape(devices, SLAB, half)

    @pl.when(step == 0)
    def _():
        proj = both_products(attn_ref, attn_other_ref, branch_ref[...], branch_other_ref[...])
        start = pl.num_programs(0) * SLAB
        fc1_proj_ref[:, start:] = proj.reshape(devices, SLAB, half)


def attn_weights_kernel(normed_ref, grad_ref, out_ref):
    out_ref[...] = product_tn(flat(normed_ref[...]), flat(grad_ref[...])).astype(jnp.bfloat16)


def like(*shape, dtype=jnp.bfloat16):
    return jax.ShapeDtypeStruct(shape, dtype)


def whole_block(array):
    ndim = len(array.shape)
    return pl.BlockSpec(array.shape, lambda *_: (0,) * ndim)


def params():
    return pltpu.CompilerParams(vmem_limit_bytes=VMEM_LIMIT)


def takes(microseconds):
    return pl.CostEstimate(
        flops=int(microseconds * 1.15e9), transcendentals=0, bytes_accessed=int(microseconds * 3e6)
    )


SCALARS = pl.BlockSpec(memory_space=pltpu.SMEM)


def early_specs(early):
    devices, _, half = early[0].shape
    values = pl.BlockSpec((devices, SLAB, half), lambda i: (0, 0, 0))
    return [whole_block(early[0]), values, whole_block(early[0]), values]


def call_front(core, x, table, early):
    rows, _ = x.shape
    return pl.pallas_call(
        front_kernel,
        grid=(1,),
        in_specs=[SCALARS, whole_block(x), whole_block(table)] + early_specs(early),
        out_specs=[pl.BlockSpec((8, rows, 384), lambda i: (0, 0, 0)), whole_block(x)],
        out_shape=[like(8, rows, 384), like(*x.shape)],
        compiler_params=params(),
        cost_estimate=takes(6.5),
    )(core, x, table, *early)


def call_attend(counts, heads):
    images = counts.shape[0]
    heads = heads.reshape(8, images, -1, 384)
    tokens = heads.shape[2]
    out, lse = pl.pallas_call(
        attend_kernel,
        grid=(images,),
        in_specs=[SCALARS, pl.BlockSpec((8, 1, tokens, 384), lambda i: (0, i, 0, 0))],
        out_specs=[
            pl.BlockSpec((8, 1, tokens, 128), lambda i: (0, i, 0, 0)),
            pl.BlockSpec((1, 2, 8 * tokens), lambda i: (i, 0, 0)),
        ],
        out_shape=[
            like(8, images, tokens, 128),
            like(images, 2, 8 * tokens, dtype=jnp.float32),
        ],
        compiler_params=params(),
        cost_estimate=takes(14.3),
    )(counts, heads)
    return out.reshape(8, images * tokens, 128), lse


def call_attend_back(counts, grads, heads, lse):
    images = counts.shape[0]
    heads = heads.reshape(8, images, -1, 384)
    tokens = heads.shape[2]
    out = pl.pallas_call(
        attend_back_kernel,
        grid=(images,),
        in_specs=[
            SCALARS,
            pl.BlockSpec((8, 1, tokens, 128), lambda i: (0, i, 0, 0)),
            pl.BlockSpec((8, 1, tokens, 384), lambda i: (0, i, 0, 0)),
            pl.BlockSpec((1, 2, 8 * tokens), lambda i: (i, 0, 0)),
        ],
        out_specs=pl.BlockSpec((8, 1, tokens, 384), lambda i: (0, i, 0, 0)),
        out_shape=like(*heads.shape),
        compiler_params=params(),
        cost_estimate=takes(16.5),
    )(counts, grads.reshape(8, images, tokens, 128), heads, lse)
    return out.reshape(8, images * tokens, 384)


def rear_weight_specs(late):
    devices, owned, width = late.shape
    fc2_rows = (owned - SLAB) // 2
    steps = fc2_rows // SLAB
    return steps, [
        pl.BlockSpec((devices, SLAB, width), lambda j: (0, 2 * steps, 0)),
        pl.BlockSpec((devices, SLAB, width), lambda j: (0, steps + j, 0)),
        pl.BlockSpec((devices // steps, fc2_rows, width), lambda j: (j, 0, 0)),
    ]


def call_rear(keep, x, attn, table, late):
    rows, width = x.shape
    steps, weight_specs = rear_weight_specs(late)
    full = like(rows, width, dtype=jnp.float32)
    column = pl.BlockSpec((rows, width), lambda j: (0, j))
    out_shape, out_specs = [like(rows, width)], [whole_block(x)]
    if keep:
        left = like(rows, (steps + 2) * width)
        out_shape += [full, like(rows, steps * width, dtype=jnp.float32), full, left]
        out_specs += [whole_block(x), column, whole_block(x), whole_block(left)]
    return pl.pallas_call(
        functools.partial(rear_kernel, keep),
        grid=(steps,),
        in_specs=[whole_block(member) for member in (x, attn, table)] + weight_specs,
        out_specs=out_specs,
        out_shape=out_shape,
        scratch_shapes=[
            pltpu.VMEM((rows, width), jnp.bfloat16),
            pltpu.VMEM((rows, width), jnp.float32),
            pltpu.VMEM((rows, width), jnp.float32),
        ],
        compiler_params=params(),
        cost_estimate=takes(13),
    )(x, attn, table, late, late, late)


def call_rear_back(keep, core, grad, x, branch, hidden, mlp, table, late):
    rows, width = x.shape
    steps, weight_specs = rear_weight_specs(late)
    column = pl.BlockSpec((rows, width), lambda j: (0, j))
    attn_grad = like(8, rows, 128)
    out_shape = [attn_grad, like(rows, width, dtype=jnp.float32)]
    out_specs = [whole_block(attn_grad), whole_block(x)]
    if keep:
        right = like(rows, (steps + 2) * width // 2)
        out_shape += [right, right]
        out_specs += [whole_block(right), whole_block(right)]
        out_shape += [like(*table.shape, dtype=jnp.float32)]
        out_specs += [whole_block(table)]
    return pl.pallas_call(
        functools.partial(rear_back_kernel, keep),
        grid=(steps,),
        in_specs=[
            SCALARS,
            whole_block(grad),
            whole_block(x),
            whole_block(branch),
            column,
            whole_block(mlp),
            whole_block(table),
        ]
        + weight_specs,
        out_specs=out_specs,
        out_shape=out_shape,
        scratch_shapes=[
            pltpu.VMEM((rows, width), jnp.bfloat16),
            pltpu.VMEM((rows, width), jnp.float32),
        ],
        compiler_params=params(),
        cost_estimate=takes(16),
    )(core, grad, x, branch, hidden, mlp, table, late, late, late)


def call_front_back(keep, core, grad_qkv, grad_middle, x, table, early):
    rows, width = x.shape
    out_shape, out_specs = [like(rows, width)], [whole_block(x)]
    if keep:
        out_shape += [like(*table.shape, dtype=jnp.float32)]
        out_specs += [whole_block(table)]
    return pl.pallas_call(
        functools.partial(front_back_kernel, keep),
        grid=(1,),
        in_specs=[SCALARS]
        + [whole_block(member) for member in (grad_qkv, grad_middle, x, table)]
        + early_specs(early),
        out_specs=out_specs,
        out_shape=out_shape,
        compiler_params=params(),
        cost_estimate=takes(7),
    )(core, grad_qkv, grad_middle, x, table, *early)


def call_mlp_weights(left, left_other, right, right_other, devices, owned):
    rows = left.shape[0]
    steps = owned // SLAB
    width, half = 1024, 512

    def column(size, at):
        return pl.BlockSpec((rows, size), lambda j: (0, at))

    by_step = [pl.BlockSpec((rows, size), lambda j: (0, j)) for size in (width, half)]
    out_shape = [like(devices, owned + SLAB, half), like(devices, owned, half)]
    return pl.pallas_call(
        mlp_weights_kernel,
        grid=(steps,),
        in_specs=[by_step[0]] * 2
        + [column(width, MLP_NORMED)] * 2
        + [column(width, ATTN_OUT)] * 2
        + [by_step[1]] * 2
        + [column(half, MLP_GRAD)] * 2
        + [column(half, BRANCH_GRAD)] * 2,
        out_specs=[
            whole_block(out_shape[0]),
            pl.BlockSpec((devices // steps, owned, half), lambda j: (j, 0, 0)),
        ],
        out_shape=out_shape,
        compiler_params=params(),
        cost_estimate=takes(9),
    )(*(left, left_other) * 3, *(right, right_other) * 3)


def call_attn_weights(normed, grads):
    width, columns = normed.shape[2], grads.shape[2]
    return pl.pallas_call(
        attn_weights_kernel,
        grid=(1,),
        in_specs=[whole_block(normed), whole_block(grads)],
        out_specs=pl.BlockSpec((width, columns), lambda i: (0, 0)),
        out_shape=like(width, columns),
        compiler_params=params(),
        cost_estimate=takes(6),
    )(normed, grads)


def small_slab(vectors, hidden_vector):
    lead = vectors.shape[:-2]
    row = jnp.concatenate([vectors.reshape(lead + (-1,)), hidden_vector], axis=-1)
    return jnp.pad(
        row[..., None, :], [(0, 0)] * len(lead) + [(0, SLAB - 1), (0, SMALL_WIDTH - row.shape[-1])]
    )


def table_of(slabs):
    row = slabs.astype(jnp.float32)
    vectors = row[:, : HIDDEN_ROW * SLAB].reshape(-1, HIDDEN_ROW, SLAB)
    vectors = vectors.transpose(1, 0, 2).reshape(HIDDEN_ROW, -1)
    start = HIDDEN_ROW * SLAB
    hidden = row[:, start : start + 64].reshape(-1, vectors.shape[1])
    return jnp.pad(
        jnp.concatenate([vectors, hidden]),
        [(0, TABLE_ROWS - HIDDEN_ROW - hidden.shape[0]), (0, 0)],
    )


def slabs_of(sums, devices):
    vectors = sums[:HIDDEN_ROW].reshape(HIDDEN_ROW, devices, SLAB).transpose(1, 0, 2)
    hidden = sums[HIDDEN_ROW : HIDDEN_ROW + 4].reshape(devices, -1)
    return small_slab(vectors, hidden).astype(jnp.bfloat16)


def column_slabs(rows):
    count = rows.shape[1] // 1024
    return rows.reshape(SLAB, count, 1024).transpose(1, 0, 2).reshape(count * SLAB, 1024)


def from_column_slabs(rows):
    count = rows.shape[0] // SLAB
    return rows.reshape(count, SLAB, 1024).transpose(1, 0, 2).reshape(SLAB, count * 1024)


def on_device(
    images,
    key_mask,
    image_order,
    attn_norm_gain,
    attn_norm_bias,
    qkv_weight,
    query_bias,
    value_bias,
    proj_weight,
    proj_bias,
    attn_scale,
    mlp_norm_gain,
    mlp_norm_bias,
    fc1_weight,
    fc1_bias,
    fc2_weight,
    fc2_bias,
    mlp_scale,
    cotangent,
):
    section_index = lax.axis_index("section")
    local_images, tokens_here, features = images.shape
    rows = local_images * tokens_here
    reversed_order = image_order[0] > image_order[1]
    core = (lax.axis_index("head") % 2).astype(jnp.int32).reshape(1)

    vectors = jnp.concatenate(
        [
            attn_norm_gain,
            attn_norm_bias,
            query_bias,
            value_bias,
            proj_bias,
            attn_scale,
            mlp_norm_gain,
            mlp_norm_bias,
            fc2_bias,
            mlp_scale,
        ]
    )
    late_shard = jnp.concatenate([fc2_weight[0], column_slabs(fc1_weight[0]), proj_weight[0]])
    late = lax.all_gather(late_shard, ("dp", "head"), axis=0)
    devices = late.shape[0]
    small_shard = jnp.pad(
        small_slab(vectors, fc1_bias[0]), [(0, 0), (0, features - SMALL_WIDTH)]
    )
    early_shard = jnp.concatenate([column_slabs(qkv_weight[0]), small_shard])
    ways = ("dp", "head")
    chip = spread_chip(early_shard)
    lanes = [
        spread_lane(chip[:, :, : 2 * SLAB], "dp"),
        spread_lane(chip[:, :, 2 * SLAB :], "head"),
    ]
    ends = [spread_ends(lane, way) for lane, way in zip(lanes, ways)]
    spread_parts = [spread_rest(*item) for item in zip(lanes, ends, ways)]
    early = [part[at] for at in range(2) for part in spread_parts]
    table = table_of(jnp.where(core == 0, early[1][:, SLAB], early[3][:, SLAB]))

    own_images = jnp.where(reversed_order, images[::-1], images).reshape(rows, features)
    counts = jnp.sum(key_mask, axis=1, dtype=jnp.int32)
    counts = jnp.where(reversed_order, counts[::-1], counts)

    def attention(x):
        heads, normed = call_front(core, x, table, early)
        heads = to_peers(heads)
        attn, lse = call_attend(counts, heads)
        return heads, lse, to_peers(attn), normed

    (passed,) = call_rear(False, own_images, attention(own_images)[2], table, late)
    x = jnp.where(section_index == 0, own_images, shifted(passed, 1))
    heads, lse, attn, normed = attention(x)
    normed = lax.all_gather(after(normed, attn), "head", axis=0)
    result, *rear_state, left = call_rear(True, x, attn, table, late)
    left_other = swap(left, "head")

    own_grad = cotangent.reshape(rows, features)
    rear = call_rear_back(False, core, own_grad, x, *rear_state, table, late)
    grad_qkv = to_peers(call_attend_back(counts, to_peers(rear[0]), heads, lse))
    (passed_back,) = call_front_back(False, core, grad_qkv, rear[1], x, table, early)
    passed_back = after(passed_back, left_other)
    grad = jnp.where(section_index == 0, shifted(passed_back, -1), own_grad)

    rear = call_rear_back(True, core, grad, x, *rear_state, table, late)
    grad_attn, grad_middle, right, right_other, rear_sums = rear
    fc1_proj, fc2 = call_mlp_weights(
        left, left_other, right, swap(right_other, "head"), devices, 4 * SLAB
    )
    grad_heads = after(to_peers(grad_attn), fc2)
    mlp_terms = [by_chip(fc1_proj), by_chip(fc2)]
    mlp_halves = [ring_halves(terms, way) for terms, way in zip(mlp_terms, ways)]
    grad_own_heads = call_attend_back(counts, grad_heads, heads, lse)
    grad_qkv = to_peers(after(grad_own_heads, mlp_halves))
    mlp_ends = [ring_ends(*item) for item in zip(mlp_terms, mlp_halves, ways)]
    qkv_terms = call_attn_weights(normed, grad_own_heads)
    qkv_grad = collect_heads(qkv_terms)

    input_grad, front_sums = call_front_back(
        True, core, after(grad_qkv, qkv_terms), grad_middle, x, table, early
    )
    small = ring_first(by_chip(slabs_of(rear_sums + front_sums, devices)), "dp")
    mlp_totals = [ring_total(*item) for item in zip(mlp_terms, mlp_ends, ways)]
    ring_sums = [
        second_ring(jnp.concatenate([mlp_totals[0], small], axis=3), "dp"),
        second_ring(mlp_totals[1], "head"),
    ]
    shard_grad = collect_rest(jnp.concatenate(ring_sums, axis=2))
    fc1_grad, proj_grad, small_row, fc2_grad = (
        shard_grad[start * SLAB : stop * SLAB] for start, stop in ((0, 4), (4, 5), (5, 6), (6, 10))
    )
    row = small_row[0, :SMALL_WIDTH] + small_row[0, SMALL_WIDTH:]
    small_grads = row[: HIDDEN_ROW * SLAB].reshape(HIDDEN_ROW, SLAB)
    fc1_bias_grad = row[HIDDEN_ROW * SLAB : HIDDEN_ROW * SLAB + 64]

    layer_out = result.reshape(images.shape)
    input_grad = input_grad.reshape(images.shape)
    input_grad = jnp.where(
        (section_index == 0) & reversed_order, input_grad[::-1], input_grad
    )
    outs = (
        layer_out,
        input_grad,
        small_grads[ATTN_GAIN],
        small_grads[ATTN_SHIFT],
        qkv_grad,
        small_grads[QUERY_ADD],
        small_grads[VALUE_ADD],
        proj_grad,
        small_grads[PROJ_ADD],
        small_grads[ATTN_LAYER],
        small_grads[MLP_GAIN],
        small_grads[MLP_SHIFT],
        from_column_slabs(fc1_grad),
        fc1_bias_grad,
        fc2_grad,
        small_grads[FC2_ADD],
        small_grads[MLP_LAYER],
    )
    return tuple(member[None] for member in outs)


def solution(mesh):
    tokens = P("dp", "head", None)
    vec = P("section", ("dp", "head"))
    mat = P("section", ("dp", "head"), None)
    in_specs = (
        (tokens, P("dp", None), P("dp"), vec, vec, mat, vec, vec, mat, vec, vec, vec, vec)
        + (mat, vec, mat, vec, vec, tokens)
    )
    out_tokens = P("section", "dp", "head", None)
    out_specs = (
        (out_tokens, out_tokens, vec, vec, mat, vec, vec, mat, vec, vec, vec, vec, mat, vec)
        + (mat, vec, vec)
    )
    return jax.shard_map(
        on_device, mesh=mesh, in_specs=in_specs, out_specs=out_specs, check_vma=False
    )
```

```python
import functools

import jax
import jax.numpy as jnp
from jax import lax
from jax.experimental import pallas as pl
from jax.experimental.pallas import tpu as pltpu
from jax.sharding import PartitionSpec as P

DH = 64
MASKED_SCORE = -1e30
NORM_EPSILON = 1e-06
ROOT_HALF = 0.7071067811865476
DENSITY_SCALE = 0.3989422804014327
SCORE_SCALE = DH ** (-0.5)
SLAB = 16
SMALL_WIDTH = 512
QUERY_ROWS = 512
BACK_ROWS = 128
PIECES = 1
VMEM_LIMIT = 60 * 1024 * 1024

(
    ATTN_GAIN,
    ATTN_SHIFT,
    QUERY_ADD,
    VALUE_ADD,
    PROJ_ADD,
    ATTN_LAYER,
    MLP_GAIN,
    MLP_SHIFT,
    FC2_ADD,
    MLP_LAYER,
) = range(10)
HIDDEN_ROW = 10
TABLE_ROWS = 16

MLP_NORMED, ATTN_OUT = 4, 5
MLP_GRAD, BRANCH_GRAD = 4, 5


def hop(block, axis, places):
    size = lax.axis_size(axis)
    return lax.ppermute(block, axis, [(i, (i + 2 * places) % size) for i in range(size)])


def swap(block, axis):
    size = lax.axis_size(axis)
    return lax.ppermute(block, axis, [(i, i ^ 1) for i in range(size)])


def coordinates():
    dp_index, head_index = lax.axis_index("dp"), lax.axis_index("head")
    return dp_index // 2, dp_index % 2, head_index // 2, head_index % 2


def after(value, *others):
    return lax.optimization_barrier((value,) + others)[0]


def blank(shape, given):
    def kernel(given_ref, out_ref):
        pass

    anywhere = pl.BlockSpec(memory_space=pl.ANY)
    return pl.pallas_call(
        kernel,
        in_specs=[anywhere],
        out_specs=anywhere,
        out_shape=jax.ShapeDtypeStruct(shape, given.dtype),
    )(given)


def by_core(core, mine, other, axis):
    return jnp.where(
        core == 0,
        jnp.concatenate([mine, other], axis=axis),
        jnp.concatenate([other, mine], axis=axis),
    )


def spread_chip(shard):
    _, z_me, _, core_me = coordinates()
    half = shard.shape[1] // 2
    first, second = shard[:, :half], shard[:, half:]
    mine = jnp.where(core_me == 0, first, second)[None]
    cores = by_core(core_me, mine, swap(jnp.where(core_me == 0, second, first), "head")[None], 0)
    return by_core(z_me, cores[None], swap(cores, "dp")[None], 0)


def spread_lane(pair, last_axis):
    x_me, _, y_me, _ = coordinates()
    x_size, y_size = lax.axis_size("dp") // 2, lax.axis_size("head") // 2
    shape = pair.shape[1:]
    zeros = (0,) * len(shape)
    along_y = last_axis == "dp"
    axis, me, size = ("head", y_me, y_size) if along_y else ("dp", x_me, x_size)
    lane = blank(((2, size) if along_y else (size, 2)) + shape, pair)
    for places in range(size):
        came = pair if places == 0 else hop(pair, axis, places)
        source = (me - places) % size
        if along_y:
            lane = lax.dynamic_update_slice(lane, came[:, None], (0, source) + zeros)
        else:
            lane = lax.dynamic_update_slice(lane, came[None], (source, 0) + zeros)
    return lane


def spread_ends(lane, last_axis):
    return hop(lane, last_axis, 1), hop(lane, last_axis, -1)


def spread_rest(lane, ends, last_axis):
    x_me, _, y_me, _ = coordinates()
    x_size, y_size = lax.axis_size("dp") // 2, lax.axis_size("head") // 2
    along_x = last_axis == "dp"
    me, size = (x_me, x_size) if along_x else (y_me, y_size)
    low, high = ends
    half = lane.shape[0] // 2
    far = (hop(low[:half], last_axis, 1), hop(high[half:], last_axis, -1))
    shape = lane.shape[2:]
    zeros = (0,) * len(shape)
    near = blank((x_size, 2, y_size) + shape, lane)
    for places, at, block in (
        (0, 0, lane),
        (1, 0, low),
        (-1, 0, high),
        (2, 0, far[0]),
        (2, half, far[1]),
    ):
        source = (me - places) % size
        if along_x:
            near = lax.dynamic_update_slice(near, block[None], (source, at, 0) + zeros)
        else:
            near = lax.dynamic_update_slice(near, block[:, :, None], (at, 0, source) + zeros)
    near = near.reshape((-1,) + shape[1:])
    return near, swap(near, "head")


def piece(terms, at, dim):
    return lax.dynamic_index_in_dim(terms, at, dim, keepdims=False)


def by_chip(terms):
    x_size, y_size = lax.axis_size("dp") // 2, lax.axis_size("head") // 2
    return terms.reshape((x_size, 2, y_size, 2) + terms.shape[1:])


def ring_halves(terms, axis):
    x_me, _, y_me, _ = coordinates()
    dim, me, size = (0, x_me, 4) if axis == "dp" else (2, y_me, 4)
    far = piece(terms, (me + 2) % size, dim)
    half = far.shape[0] // 2
    return hop(far[:half], axis, 1), hop(far[half:], axis, -1)


def ring_ends(terms, passed, axis):
    x_me, _, y_me, _ = coordinates()
    dim, me, size = (0, x_me, 4) if axis == "dp" else (2, y_me, 4)
    low, high = (part.astype(jnp.float32) for part in passed)
    up = piece(terms, (me + 1) % size, dim).astype(jnp.float32)
    down = piece(terms, (me - 1) % size, dim).astype(jnp.float32)
    half = up.shape[0] // 2
    up = jnp.concatenate([up[:half] + low, up[half:]]).astype(jnp.bfloat16)
    down = jnp.concatenate([down[:half], down[half:] + high]).astype(jnp.bfloat16)
    return hop(up, axis, 1), hop(down, axis, -1)


def ring_total(terms, ends, axis):
    x_me, _, y_me, _ = coordinates()
    own = piece(terms, x_me, 0) if axis == "dp" else piece(terms, y_me, 2)
    total = sum((end.astype(jnp.float32) for end in ends), own.astype(jnp.float32))
    return total.astype(jnp.bfloat16)


def ring_direct(terms, axis, dim, me):
    own = piece(terms, me, dim).astype(jnp.float32)
    for places in (1, 2, 3):
        own = own + hop(piece(terms, (me + places) % 4, dim), axis, places).astype(jnp.float32)
    return own


def ring_first(terms, axis):
    x_me, _, y_me, _ = coordinates()
    dim, me = (0, x_me) if axis == "dp" else (2, y_me)
    return ring_direct(terms, axis, dim, me).astype(jnp.bfloat16)


def second_ring(terms, first_axis):
    x_me, _, y_me, _ = coordinates()
    if first_axis == "dp":
        return ring_direct(terms, "head", 1, y_me)
    return ring_direct(terms, "dp", 0, x_me)


def collect_rest(terms):
    _, z_me, _, core_me = coordinates()
    away = piece(terms, 1 - z_me, 0).astype(jnp.bfloat16)
    cores = piece(terms, z_me, 0) + swap(away, "dp").astype(jnp.float32)
    got = swap(piece(cores, 1 - core_me, 0).astype(jnp.bfloat16), "head").astype(jnp.float32)
    return by_core(core_me, piece(cores, core_me, 0), got, 1)


def collect_heads(terms):
    x_me, z_me, _, _ = coordinates()
    peers = lax.axis_size("head")
    blocks = terms.reshape(lax.axis_size("dp") // 2, 2, -1, terms.shape[1])
    blocks = ring_direct(blocks, "dp", 0, x_me)
    away = piece(blocks, 1 - z_me, 0).astype(jnp.bfloat16)
    total = piece(blocks, z_me, 0) + swap(away, "dp").astype(jnp.float32)
    parts = to_peers(total.astype(jnp.bfloat16).reshape(peers, -1, terms.shape[1]))
    rows = parts.shape[1]
    parts = parts.reshape(peers, rows, 3, -1).transpose(1, 2, 0, 3)
    return parts.reshape(rows, -1).astype(jnp.float32)


def to_peers(blocks):
    return lax.all_to_all(blocks, "head", split_axis=0, concat_axis=0, tiled=True)


def shifted(block, distance):
    size = lax.axis_size("section")
    route = [(i, i + distance) for i in range(size) if 0 <= i + distance < size]
    return lax.ppermute(block, "section", route)


def ahead(items, function):
    value = function(items[0])
    for at, item in enumerate(items):
        later = function(items[at + 1]) if at + 1 < len(items) else None
        yield item, value
        value = later


def norm_stats(rows):
    centre = rows - jnp.mean(rows, axis=-1, keepdims=True)
    inverse = lax.rsqrt(jnp.mean(centre * centre, axis=-1, keepdims=True) + NORM_EPSILON)
    return centre * inverse, inverse


def norm_back(grad_norm, scaled, inverse):
    first_mean = jnp.mean(grad_norm, axis=-1, keepdims=True)
    second_mean = jnp.mean(grad_norm * scaled, axis=-1, keepdims=True)
    return inverse * (grad_norm - first_mean - scaled * second_mean)


def product(left, right):
    return jnp.dot(left, right, preferred_element_type=jnp.float32)


def product_nt(left, right):
    return lax.dot_general(
        left, right, (((1,), (1,)), ((), ())), preferred_element_type=jnp.float32
    )


def product_tn(left, right):
    return lax.dot_general(
        left, right, (((0,), (0,)), ((), ())), preferred_element_type=jnp.float32
    )


def flat(block):
    return block.reshape(-1, block.shape[-1])


def column_sum(rows):
    return jnp.sum(rows, axis=0, keepdims=True)


def vector(table_ref, row):
    return table_ref[row : row + 1, :]


def side_by_side(blocks_ref, start=0, first=0, count=8):
    return jnp.concatenate(
        [blocks_ref[first + peer, :, start : start + 128] for peer in range(count)], axis=1
    )


def put_side_by_side(blocks_ref, rows, start=0, first=0):
    for peer in range(rows.shape[1] // 128):
        blocks_ref[first + peer, :, start : start + 128] = rows[
            :, peer * 128 : (peer + 1) * 128
        ].astype(blocks_ref.dtype)


def put_column(ref, at, rows):
    width = rows.shape[1]
    start = at * width if isinstance(at, int) else pl.multiple_of(at * width, width)
    ref[:, pl.ds(start, width)] = rows


def halves(core, rows):
    half = rows.shape[1] // 2
    first, second = rows[:, :half], rows[:, half:]
    return jnp.where(core == 0, first, second), jnp.where(core == 0, second, first)


def attn_normed(rows, table_ref):
    scaled, inverse = norm_stats(rows)
    normed = (scaled * vector(table_ref, ATTN_GAIN) + vector(table_ref, ATTN_SHIFT)).astype(
        jnp.bfloat16
    )
    return normed, scaled, inverse


def mlp_normed(middle, table_ref):
    scaled, inverse = norm_stats(middle)
    normed = (scaled * vector(table_ref, MLP_GAIN) + vector(table_ref, MLP_SHIFT)).astype(
        jnp.bfloat16
    )
    return normed, scaled, inverse


def cumulative(hidden):
    return 0.5 * (1.0 + lax.erf(hidden * ROOT_HALF))


def front_kernel(
    core_ref, x_ref, table_ref, qk_mine_ref, v_mine_ref, qk_other_ref, v_other_ref, out_ref, normed_ref
):
    core = core_ref[0]
    normed, _, _ = attn_normed(x_ref[...].astype(jnp.float32), table_ref)
    normed_ref[...] = normed
    query_adds = halves(core, vector(table_ref, QUERY_ADD))
    value_adds = halves(core, vector(table_ref, VALUE_ADD))
    for at, (qk_ref, v_ref) in enumerate(
        ((qk_mine_ref, v_mine_ref), (qk_other_ref, v_other_ref))
    ):
        first = (core if at == 0 else 1 - core) * 4
        queries = product(normed, flat(qk_ref[:, :SLAB])) + query_adds[at]
        put_side_by_side(out_ref, queries, 0, first)
        put_side_by_side(out_ref, product(normed, flat(qk_ref[:, SLAB:])), 128, first)
        values = product(normed, flat(v_ref[...])) + value_adds[at]
        put_side_by_side(out_ref, values, 256, first)


def marked(rows, mark):
    first = lax.broadcasted_iota(jnp.int32, rows.shape, 1) == 0
    return jnp.concatenate([rows, jnp.where(first, mark, 0.0).astype(jnp.bfloat16)], axis=1)


def masked_keys(block, count, head):
    keys = block[:, 128 + head * DH : 128 + (head + 1) * DH]
    valid = lax.broadcasted_iota(jnp.int32, keys.shape, 0) < count
    return marked(keys, jnp.where(valid, 0.0, MASKED_SCORE))


def scaled_queries(block, start, count, head):
    queries = block[start : start + count, head * DH : (head + 1) * DH]
    return marked((queries.astype(jnp.float32) * SCORE_SCALE).astype(jnp.bfloat16), 1.0)


def attend_kernel(count_ref, heads_ref, out_ref, lse_ref):
    count = count_ref[pl.program_id(0)]
    block = flat(heads_ref[:, 0])
    seq_len = block.shape[0]
    keys = [masked_keys(block, count, head) for head in range(2)]
    values = [block[:, 256 + head * DH : 256 + (head + 1) * DH] for head in range(2)]
    values = [jnp.concatenate([part, jnp.ones_like(part)], axis=1) for part in values]
    outs = []

    def scores_of(item):
        start, head = item
        return product_nt(keys[head], scaled_queries(block, start, QUERY_ROWS, head))

    items = [(start, head) for start in range(0, seq_len, QUERY_ROWS) for head in range(2)]
    for (start, head), scores in ahead(items, scores_of):
        largest = jnp.max(scores, axis=0, keepdims=True)
        weights = jnp.exp(scores - largest)
        mixed = product_tn(values[head], weights.astype(jnp.bfloat16))
        total = mixed[DH : DH + 1]
        outs.append((mixed[:DH] / total).T)
        lse_ref[0, head : head + 1, start : start + QUERY_ROWS] = largest + jnp.log(total)
        if head == 1:
            rows = jnp.concatenate(outs[-2:], axis=1).astype(jnp.bfloat16)
            peers = QUERY_ROWS // 128
            out_ref[start // 128 : start // 128 + peers, 0] = rows.reshape(peers, 128, 128)


def attend_back_kernel(count_ref, grad_ref, heads_ref, lse_ref, out_ref):
    count = count_ref[pl.program_id(0)]
    block = flat(heads_ref[:, 0])
    grads = flat(grad_ref[:, 0])
    seq_len = block.shape[0]
    peers = BACK_ROWS // 128
    keys = [masked_keys(block, count, head) for head in range(2)]
    values = [block[:, 256 + head * DH : 256 + (head + 1) * DH] for head in range(2)]
    key_sums = [jnp.zeros((seq_len, DH), jnp.float32) for _ in range(2)]
    value_sums = [jnp.zeros((seq_len, DH), jnp.float32) for _ in range(2)]
    outs = []

    def products_of(item):
        start, head = item
        queries = scaled_queries(block, start, BACK_ROWS, head)
        grad_rows = grads[start : start + BACK_ROWS, head * DH : (head + 1) * DH]
        scores = product_nt(keys[head], queries)
        return queries, grad_rows, scores, product_nt(values[head], grad_rows)

    items = [(start, head) for start in range(0, seq_len, BACK_ROWS) for head in range(2)]
    for (start, head), members in ahead(items, products_of):
        queries, grad_rows, scores, grad_weights = members
        weights = jnp.exp(scores - lse_ref[0, head : head + 1, start : start + BACK_ROWS])
        shares = weights * grad_weights
        dots = jnp.sum(shares, axis=0, keepdims=True)
        grad_scores = (shares - weights * dots).astype(jnp.bfloat16)
        value_sums[head] += product(weights.astype(jnp.bfloat16), grad_rows)
        key_sums[head] += product(grad_scores, queries[:, :DH])
        outs.append((product_tn(keys[head][:, :DH], grad_scores) * SCORE_SCALE).T)
        if head == 1:
            rows = jnp.concatenate(outs[-2:], axis=1).astype(jnp.bfloat16)
            at = start // 128
            out_ref[at : at + peers, 0, :, :128] = rows.reshape(peers, 128, 128)
    key_rows = jnp.concatenate(key_sums, axis=1).astype(jnp.bfloat16)
    value_rows = jnp.concatenate(value_sums, axis=1).astype(jnp.bfloat16)
    out_ref[:, 0, :, 128:256] = key_rows.reshape(-1, 128, 128)
    out_ref[:, 0, :, 256:] = value_rows.reshape(-1, 128, 128)


def hidden_pieces(fc1_ref, fc2_ref):
    columns, owners = fc1_ref.shape[2] // PIECES, fc2_ref.shape[0] // PIECES
    return [
        (slice(at * columns, (at + 1) * columns), slice(at * owners, (at + 1) * owners))
        for at in range(PIECES)
    ]


def rear_kernel(keep, x_ref, attn_ref, table_ref, proj_ref, fc1_ref, fc2_ref, *rest):
    if keep:
        result_ref, branch_ref, hidden_ref, mlp_ref, left_ref, normed, middle, total = rest
    else:
        result_ref, normed, middle, total = rest
    step = pl.program_id(0)

    @pl.when(step == 0)
    def _():
        attn = side_by_side(attn_ref)
        branch = product(attn, flat(proj_ref[...])) + vector(table_ref, PROJ_ADD)
        rows = x_ref[...].astype(jnp.float32)
        middle[...] = rows + vector(table_ref, ATTN_LAYER) * branch
        normed[...] = mlp_normed(middle[...], table_ref)[0]
        if keep:
            branch_ref[...] = branch
            put_column(left_ref, MLP_NORMED, normed[...])
            put_column(left_ref, ATTN_OUT, attn)
        total[...] = jnp.broadcast_to(vector(table_ref, FC2_ADD), total.shape)

    adds = table_ref[pl.ds(HIDDEN_ROW + step, 1), :]
    actives, mixed = [], 0.0

    def hidden_of(item):
        return product(normed[...], flat(fc1_ref[:, :, item[0]])) + adds[:, item[0]]

    for (columns, owners), hidden in ahead(hidden_pieces(fc1_ref, fc2_ref), hidden_of):
        if keep:
            hidden_ref[:, columns] = hidden
        actives.append((hidden * cumulative(hidden)).astype(jnp.bfloat16))
        mixed += product(actives[-1], flat(fc2_ref[owners]))
    if keep:
        put_column(left_ref, step, jnp.concatenate(actives, axis=1))
    total[...] += mixed

    @pl.when(step == pl.num_programs(0) - 1)
    def _():
        if keep:
            mlp_ref[...] = total[...]
        result = middle[...] + vector(table_ref, MLP_LAYER) * total[...]
        result_ref[...] = result.astype(jnp.bfloat16)


def rear_back_kernel(
    keep,
    core_ref,
    grad_ref,
    x_ref,
    branch_ref,
    hidden_ref,
    mlp_ref,
    table_ref,
    proj_ref,
    fc1_ref,
    fc2_ref,
    attn_grad_ref,
    middle_grad_ref,
    *rest,
):
    if keep:
        mine_ref, other_ref, sums_ref = rest[:3]
    mlp_low, total = rest[-2:]
    step = pl.program_id(0)

    def put_right(at, rows):
        mine, other = halves(core_ref[0], rows)
        put_column(mine_ref, at, mine)
        put_column(other_ref, at, other)

    @pl.when(step == 0)
    def _():
        grad_mlp = vector(table_ref, MLP_LAYER) * grad_ref[...].astype(jnp.float32)
        mlp_low[...] = grad_mlp.astype(jnp.bfloat16)
        total[...] = jnp.zeros_like(total)
        if keep:
            sums_ref[...] = jnp.zeros_like(sums_ref)
            sums_ref[FC2_ADD : FC2_ADD + 1, :] = column_sum(grad_mlp)
            put_right(MLP_GRAD, mlp_low[...])

    lows, sums, mixed = [], [], 0.0

    def active_grad_of(item):
        return product_nt(mlp_low[...], flat(fc2_ref[item[1]]))

    for (columns, _), grad in ahead(hidden_pieces(fc1_ref, fc2_ref), active_grad_of):
        hidden = hidden_ref[:, columns]
        slope = cumulative(hidden) + hidden * (jnp.exp(-0.5 * hidden * hidden) * DENSITY_SCALE)
        grad_hidden = grad * slope
        lows.append(grad_hidden.astype(jnp.bfloat16))
        sums.append(column_sum(grad_hidden))
        mixed += product_nt(lows[-1], flat(fc1_ref[:, :, columns]))
    total[...] += mixed
    if keep:
        sums_ref[pl.ds(HIDDEN_ROW + step, 1), :] = jnp.concatenate(sums, axis=1)
        put_right(step, jnp.concatenate(lows, axis=1))

    @pl.when(step == pl.num_programs(0) - 1)
    def _():
        grad_rows = grad_ref[...].astype(jnp.float32)
        branch = branch_ref[...]
        middle = x_ref[...].astype(jnp.float32) + vector(table_ref, ATTN_LAYER) * branch
        _, scaled, inverse = mlp_normed(middle, table_ref)
        grad_normed = total[...]
        grad_middle = grad_rows + norm_back(
            grad_normed * vector(table_ref, MLP_GAIN), scaled, inverse
        )
        middle_grad_ref[...] = grad_middle
        grad_branch = vector(table_ref, ATTN_LAYER) * grad_middle
        branch_low = grad_branch.astype(jnp.bfloat16)
        put_side_by_side(attn_grad_ref, product_nt(branch_low, flat(proj_ref[...])))
        if keep:
            put_right(BRANCH_GRAD, branch_low)
            for row, rows in (
                (MLP_LAYER, grad_rows * mlp_ref[...]),
                (MLP_GAIN, grad_normed * scaled),
                (MLP_SHIFT, grad_normed),
                (ATTN_LAYER, grad_middle * branch),
                (PROJ_ADD, grad_branch),
            ):
                sums_ref[row : row + 1, :] = column_sum(rows)


def front_back_kernel(
    keep,
    core_ref,
    grad_ref,
    middle_grad_ref,
    x_ref,
    table_ref,
    qk_mine_ref,
    v_mine_ref,
    qk_other_ref,
    v_other_ref,
    *rest,
):
    if keep:
        out_ref, sums_ref = rest
    else:
        (out_ref,) = rest
    core = core_ref[0]
    grad_normed = 0.0
    for at, (qk_ref, v_ref) in enumerate(
        ((qk_mine_ref, v_mine_ref), (qk_other_ref, v_other_ref))
    ):
        first = (core if at == 0 else 1 - core) * 4
        queries, keys, values = (
            side_by_side(grad_ref, start, first, 4) for start in (0, 128, 256)
        )
        grad_normed += product_nt(queries, flat(qk_ref[:, :SLAB]))
        grad_normed += product_nt(keys, flat(qk_ref[:, SLAB:]))
        grad_normed += product_nt(values, flat(v_ref[...]))
    _, scaled, inverse = attn_normed(x_ref[...].astype(jnp.float32), table_ref)
    grad_input = middle_grad_ref[...] + norm_back(
        grad_normed * vector(table_ref, ATTN_GAIN), scaled, inverse
    )
    out_ref[...] = grad_input.astype(jnp.bfloat16)
    if keep:
        sums_ref[...] = jnp.zeros_like(sums_ref)
        for row, rows in (
            (ATTN_GAIN, grad_normed * scaled),
            (ATTN_SHIFT, grad_normed),
            (QUERY_ADD, side_by_side(grad_ref, 0).astype(jnp.float32)),
            (VALUE_ADD, side_by_side(grad_ref, 256).astype(jnp.float32)),
        ):
            sums_ref[row : row + 1, :] = column_sum(rows)


def both_products(left_ref, left_other_ref, right, right_other):
    grad = product_tn(left_ref[...], right) + product_tn(left_other_ref[...], right_other)
    return grad.astype(jnp.bfloat16)


def mlp_weights_kernel(
    active_ref,
    active_other_ref,
    normed_ref,
    normed_other_ref,
    attn_ref,
    attn_other_ref,
    hidden_ref,
    hidden_other_ref,
    mlp_ref,
    mlp_other_ref,
    branch_ref,
    branch_other_ref,
    fc1_proj_ref,
    fc2_ref,
):
    step = pl.program_id(0)
    devices, _, half = fc1_proj_ref.shape
    fc2 = both_products(active_ref, active_other_ref, mlp_ref[...], mlp_other_ref[...])
    fc2_ref[...] = fc2.reshape(fc2_ref.shape)
    fc1 = both_products(normed_ref, normed_other_ref, hidden_ref[...], hidden_other_ref[...])
    start = pl.multiple_of(step * SLAB, SLAB)
    fc1_proj_ref[:, pl.ds(start, SLAB)] = fc1.reshape(devices, SLAB, half)

    @pl.when(step == 0)
    def _():
        proj = both_products(attn_ref, attn_other_ref, branch_ref[...], branch_other_ref[...])
        start = pl.num_programs(0) * SLAB
        fc1_proj_ref[:, start:] = proj.reshape(devices, SLAB, half)


def attn_weights_kernel(normed_ref, grad_ref, out_ref):
    out_ref[...] = product_tn(flat(normed_ref[...]), flat(grad_ref[...])).astype(jnp.bfloat16)


def like(*shape, dtype=jnp.bfloat16):
    return jax.ShapeDtypeStruct(shape, dtype)


def whole_block(array):
    ndim = len(array.shape)
    return pl.BlockSpec(array.shape, lambda *_: (0,) * ndim)


def params():
    return pltpu.CompilerParams(vmem_limit_bytes=VMEM_LIMIT)


def takes(microseconds):
    return pl.CostEstimate(
        flops=int(microseconds * 1.15e9), transcendentals=0, bytes_accessed=int(microseconds * 3e6)
    )


SCALARS = pl.BlockSpec(memory_space=pltpu.SMEM)


def early_specs(early):
    devices, _, half = early[0].shape
    values = pl.BlockSpec((devices, SLAB, half), lambda i: (0, 0, 0))
    return [whole_block(early[0]), values, whole_block(early[0]), values]


def call_front(core, x, table, early):
    rows, _ = x.shape
    return pl.pallas_call(
        front_kernel,
        grid=(1,),
        in_specs=[SCALARS, whole_block(x), whole_block(table)] + early_specs(early),
        out_specs=[pl.BlockSpec((8, rows, 384), lambda i: (0, 0, 0)), whole_block(x)],
        out_shape=[like(8, rows, 384), like(*x.shape)],
        compiler_params=params(),
        cost_estimate=takes(6.5),
    )(core, x, table, *early)


def call_attend(counts, heads):
    images = counts.shape[0]
    heads = heads.reshape(8, images, -1, 384)
    tokens = heads.shape[2]
    out, lse = pl.pallas_call(
        attend_kernel,
        grid=(images,),
        in_specs=[SCALARS, pl.BlockSpec((8, 1, tokens, 384), lambda i: (0, i, 0, 0))],
        out_specs=[
            pl.BlockSpec((8, 1, tokens, 128), lambda i: (0, i, 0, 0)),
            pl.BlockSpec((1, 2, 8 * tokens), lambda i: (i, 0, 0)),
        ],
        out_shape=[
            like(8, images, tokens, 128),
            like(images, 2, 8 * tokens, dtype=jnp.float32),
        ],
        compiler_params=params(),
        cost_estimate=takes(14.3),
    )(counts, heads)
    return out.reshape(8, images * tokens, 128), lse


def call_attend_back(counts, grads, heads, lse):
    images = counts.shape[0]
    heads = heads.reshape(8, images, -1, 384)
    tokens = heads.shape[2]
    out = pl.pallas_call(
        attend_back_kernel,
        grid=(images,),
        in_specs=[
            SCALARS,
            pl.BlockSpec((8, 1, tokens, 128), lambda i: (0, i, 0, 0)),
            pl.BlockSpec((8, 1, tokens, 384), lambda i: (0, i, 0, 0)),
            pl.BlockSpec((1, 2, 8 * tokens), lambda i: (i, 0, 0)),
        ],
        out_specs=pl.BlockSpec((8, 1, tokens, 384), lambda i: (0, i, 0, 0)),
        out_shape=like(*heads.shape),
        compiler_params=params(),
        cost_estimate=takes(16.5),
    )(counts, grads.reshape(8, images, tokens, 128), heads, lse)
    return out.reshape(8, images * tokens, 384)


def rear_weight_specs(late):
    devices, owned, width = late.shape
    fc2_rows = (owned - SLAB) // 2
    steps = fc2_rows // SLAB
    return steps, [
        pl.BlockSpec((devices, SLAB, width), lambda j: (0, 2 * steps, 0)),
        pl.BlockSpec((devices, SLAB, width), lambda j: (0, steps + j, 0)),
        pl.BlockSpec((devices // steps, fc2_rows, width), lambda j: (j, 0, 0)),
    ]


def call_rear(keep, x, attn, table, late):
    rows, width = x.shape
    steps, weight_specs = rear_weight_specs(late)
    full = like(rows, width, dtype=jnp.float32)
    column = pl.BlockSpec((rows, width), lambda j: (0, j))
    out_shape, out_specs = [like(rows, width)], [whole_block(x)]
    if keep:
        left = like(rows, (steps + 2) * width)
        out_shape += [full, like(rows, steps * width, dtype=jnp.float32), full, left]
        out_specs += [whole_block(x), column, whole_block(x), whole_block(left)]
    return pl.pallas_call(
        functools.partial(rear_kernel, keep),
        grid=(steps,),
        in_specs=[whole_block(member) for member in (x, attn, table)] + weight_specs,
        out_specs=out_specs,
        out_shape=out_shape,
        scratch_shapes=[
            pltpu.VMEM((rows, width), jnp.bfloat16),
            pltpu.VMEM((rows, width), jnp.float32),
            pltpu.VMEM((rows, width), jnp.float32),
        ],
        compiler_params=params(),
        cost_estimate=takes(13),
    )(x, attn, table, late, late, late)


def call_rear_back(keep, core, grad, x, branch, hidden, mlp, table, late):
    rows, width = x.shape
    steps, weight_specs = rear_weight_specs(late)
    column = pl.BlockSpec((rows, width), lambda j: (0, j))
    attn_grad = like(8, rows, 128)
    out_shape = [attn_grad, like(rows, width, dtype=jnp.float32)]
    out_specs = [whole_block(attn_grad), whole_block(x)]
    if keep:
        right = like(rows, (steps + 2) * width // 2)
        out_shape += [right, right]
        out_specs += [whole_block(right), whole_block(right)]
        out_shape += [like(*table.shape, dtype=jnp.float32)]
        out_specs += [whole_block(table)]
    return pl.pallas_call(
        functools.partial(rear_back_kernel, keep),
        grid=(steps,),
        in_specs=[
            SCALARS,
            whole_block(grad),
            whole_block(x),
            whole_block(branch),
            column,
            whole_block(mlp),
            whole_block(table),
        ]
        + weight_specs,
        out_specs=out_specs,
        out_shape=out_shape,
        scratch_shapes=[
            pltpu.VMEM((rows, width), jnp.bfloat16),
            pltpu.VMEM((rows, width), jnp.float32),
        ],
        compiler_params=params(),
        cost_estimate=takes(16),
    )(core, grad, x, branch, hidden, mlp, table, late, late, late)


def call_front_back(keep, core, grad_qkv, grad_middle, x, table, early):
    rows, width = x.shape
    out_shape, out_specs = [like(rows, width)], [whole_block(x)]
    if keep:
        out_shape += [like(*table.shape, dtype=jnp.float32)]
        out_specs += [whole_block(table)]
    return pl.pallas_call(
        functools.partial(front_back_kernel, keep),
        grid=(1,),
        in_specs=[SCALARS]
        + [whole_block(member) for member in (grad_qkv, grad_middle, x, table)]
        + early_specs(early),
        out_specs=out_specs,
        out_shape=out_shape,
        compiler_params=params(),
        cost_estimate=takes(7),
    )(core, grad_qkv, grad_middle, x, table, *early)


def call_mlp_weights(left, left_other, right, right_other, devices, owned):
    rows = left.shape[0]
    steps = owned // SLAB
    width, half = 1024, 512

    def column(size, at):
        return pl.BlockSpec((rows, size), lambda j: (0, at))

    by_step = [pl.BlockSpec((rows, size), lambda j: (0, j)) for size in (width, half)]
    out_shape = [like(devices, owned + SLAB, half), like(devices, owned, half)]
    return pl.pallas_call(
        mlp_weights_kernel,
        grid=(steps,),
        in_specs=[by_step[0]] * 2
        + [column(width, MLP_NORMED)] * 2
        + [column(width, ATTN_OUT)] * 2
        + [by_step[1]] * 2
        + [column(half, MLP_GRAD)] * 2
        + [column(half, BRANCH_GRAD)] * 2,
        out_specs=[
            whole_block(out_shape[0]),
            pl.BlockSpec((devices // steps, owned, half), lambda j: (j, 0, 0)),
        ],
        out_shape=out_shape,
        compiler_params=params(),
        cost_estimate=takes(9),
    )(*(left, left_other) * 3, *(right, right_other) * 3)


def call_attn_weights(normed, grads):
    width, columns = normed.shape[2], grads.shape[2]
    return pl.pallas_call(
        attn_weights_kernel,
        grid=(1,),
        in_specs=[whole_block(normed), whole_block(grads)],
        out_specs=pl.BlockSpec((width, columns), lambda i: (0, 0)),
        out_shape=like(width, columns),
        compiler_params=params(),
        cost_estimate=takes(6),
    )(normed, grads)


def small_slab(vectors, hidden_vector):
    lead = vectors.shape[:-2]
    row = jnp.concatenate([vectors.reshape(lead + (-1,)), hidden_vector], axis=-1)
    return jnp.pad(
        row[..., None, :], [(0, 0)] * len(lead) + [(0, SLAB - 1), (0, SMALL_WIDTH - row.shape[-1])]
    )


def table_of(slabs):
    row = slabs.astype(jnp.float32)
    vectors = row[:, : HIDDEN_ROW * SLAB].reshape(-1, HIDDEN_ROW, SLAB)
    vectors = vectors.transpose(1, 0, 2).reshape(HIDDEN_ROW, -1)
    start = HIDDEN_ROW * SLAB
    hidden = row[:, start : start + 64].reshape(-1, vectors.shape[1])
    return jnp.pad(
        jnp.concatenate([vectors, hidden]),
        [(0, TABLE_ROWS - HIDDEN_ROW - hidden.shape[0]), (0, 0)],
    )


def slabs_of(sums, devices):
    vectors = sums[:HIDDEN_ROW].reshape(HIDDEN_ROW, devices, SLAB).transpose(1, 0, 2)
    hidden = sums[HIDDEN_ROW : HIDDEN_ROW + 4].reshape(devices, -1)
    return small_slab(vectors, hidden).astype(jnp.bfloat16)


def column_slabs(rows):
    count = rows.shape[1] // 1024
    return rows.reshape(SLAB, count, 1024).transpose(1, 0, 2).reshape(count * SLAB, 1024)


def from_column_slabs(rows):
    count = rows.shape[0] // SLAB
    return rows.reshape(count, SLAB, 1024).transpose(1, 0, 2).reshape(SLAB, count * 1024)


def on_device(
    images,
    key_mask,
    image_order,
    attn_norm_gain,
    attn_norm_bias,
    qkv_weight,
    query_bias,
    value_bias,
    proj_weight,
    proj_bias,
    attn_scale,
    mlp_norm_gain,
    mlp_norm_bias,
    fc1_weight,
    fc1_bias,
    fc2_weight,
    fc2_bias,
    mlp_scale,
    cotangent,
):
    section_index = lax.axis_index("section")
    local_images, tokens_here, features = images.shape
    rows = local_images * tokens_here
    reversed_order = image_order[0] > image_order[1]
    core = (lax.axis_index("head") % 2).astype(jnp.int32).reshape(1)

    vectors = jnp.concatenate(
        [
            attn_norm_gain,
            attn_norm_bias,
            query_bias,
            value_bias,
            proj_bias,
            attn_scale,
            mlp_norm_gain,
            mlp_norm_bias,
            fc2_bias,
            mlp_scale,
        ]
    )
    late_shard = jnp.concatenate([fc2_weight[0], column_slabs(fc1_weight[0]), proj_weight[0]])
    late = lax.all_gather(late_shard, ("dp", "head"), axis=0)
    devices = late.shape[0]
    small_shard = jnp.pad(
        small_slab(vectors, fc1_bias[0]), [(0, 0), (0, features - SMALL_WIDTH)]
    )
    early_shard = jnp.concatenate([column_slabs(qkv_weight[0]), small_shard])
    ways = ("dp", "head")
    chip = spread_chip(early_shard)
    lanes = [
        spread_lane(chip[:, :, : 2 * SLAB], "dp"),
        spread_lane(chip[:, :, 2 * SLAB :], "head"),
    ]
    ends = [spread_ends(lane, way) for lane, way in zip(lanes, ways)]
    spread_parts = [spread_rest(*item) for item in zip(lanes, ends, ways)]
    early = [part[at] for at in range(2) for part in spread_parts]
    table = table_of(jnp.where(core == 0, early[1][:, SLAB], early[3][:, SLAB]))

    own_images = jnp.where(reversed_order, images[::-1], images).reshape(rows, features)
    counts = jnp.sum(key_mask, axis=1, dtype=jnp.int32)
    counts = jnp.where(reversed_order, counts[::-1], counts)

    def attention(x):
        heads, normed = call_front(core, x, table, early)
        heads = to_peers(heads)
        attn, lse = call_attend(counts, heads)
        return heads, lse, to_peers(attn), normed

    (passed,) = call_rear(False, own_images, attention(own_images)[2], table, late)
    x = jnp.where(section_index == 0, own_images, shifted(passed, 1))
    heads, lse, attn, normed = attention(x)
    normed = lax.all_gather(after(normed, attn), "head", axis=0)
    result, *rear_state, left = call_rear(True, x, attn, table, late)
    left_other = swap(left, "head")

    own_grad = cotangent.reshape(rows, features)
    rear = call_rear_back(False, core, own_grad, x, *rear_state, table, late)
    grad_qkv = to_peers(call_attend_back(counts, to_peers(rear[0]), heads, lse))
    (passed_back,) = call_front_back(False, core, grad_qkv, rear[1], x, table, early)
    passed_back = after(passed_back, left_other)
    grad = jnp.where(section_index == 0, shifted(passed_back, -1), own_grad)

    rear = call_rear_back(True, core, grad, x, *rear_state, table, late)
    grad_attn, grad_middle, right, right_other, rear_sums = rear
    fc1_proj, fc2 = call_mlp_weights(
        left, left_other, right, swap(right_other, "head"), devices, 4 * SLAB
    )
    grad_heads = after(to_peers(grad_attn), fc2)
    mlp_terms = [by_chip(fc1_proj), by_chip(fc2)]
    mlp_halves = [ring_halves(terms, way) for terms, way in zip(mlp_terms, ways)]
    grad_own_heads = call_attend_back(counts, grad_heads, heads, lse)
    mlp_halves = after(mlp_halves, grad_own_heads)
    grad_qkv = to_peers(after(grad_own_heads, mlp_halves))
    mlp_ends = [ring_ends(*item) for item in zip(mlp_terms, mlp_halves, ways)]
    qkv_terms = call_attn_weights(normed, grad_own_heads)
    qkv_grad = collect_heads(qkv_terms)

    input_grad, front_sums = call_front_back(
        True, core, after(grad_qkv, qkv_terms), grad_middle, x, table, early
    )
    small = ring_first(by_chip(slabs_of(rear_sums + front_sums, devices)), "dp")
    mlp_totals = [ring_total(*item) for item in zip(mlp_terms, mlp_ends, ways)]
    ring_sums = [
        second_ring(jnp.concatenate([mlp_totals[0], small], axis=3), "dp"),
        second_ring(mlp_totals[1], "head"),
    ]
    ring_sums = after(ring_sums, qkv_grad)
    shard_grad = collect_rest(jnp.concatenate(ring_sums, axis=2))
    fc1_grad, proj_grad, small_row, fc2_grad = (
        shard_grad[start * SLAB : stop * SLAB] for start, stop in ((0, 4), (4, 5), (5, 6), (6, 10))
    )
    row = small_row[0, :SMALL_WIDTH] + small_row[0, SMALL_WIDTH:]
    small_grads = row[: HIDDEN_ROW * SLAB].reshape(HIDDEN_ROW, SLAB)
    fc1_bias_grad = row[HIDDEN_ROW * SLAB : HIDDEN_ROW * SLAB + 64]

    layer_out = result.reshape(images.shape)
    input_grad = input_grad.reshape(images.shape)
    input_grad = jnp.where(
        (section_index == 0) & reversed_order, input_grad[::-1], input_grad
    )
    outs = (
        layer_out,
        input_grad,
        small_grads[ATTN_GAIN],
        small_grads[ATTN_SHIFT],
        qkv_grad,
        small_grads[QUERY_ADD],
        small_grads[VALUE_ADD],
        proj_grad,
        small_grads[PROJ_ADD],
        small_grads[ATTN_LAYER],
        small_grads[MLP_GAIN],
        small_grads[MLP_SHIFT],
        from_column_slabs(fc1_grad),
        fc1_bias_grad,
        fc2_grad,
        small_grads[FC2_ADD],
        small_grads[MLP_LAYER],
    )
    return tuple(member[None] for member in outs)


def solution(mesh):
    tokens = P("dp", "head", None)
    vec = P("section", ("dp", "head"))
    mat = P("section", ("dp", "head"), None)
    in_specs = (
        (tokens, P("dp", None), P("dp"), vec, vec, mat, vec, vec, mat, vec, vec, vec, vec)
        + (mat, vec, mat, vec, vec, tokens)
    )
    out_tokens = P("section", "dp", "head", None)
    out_specs = (
        (out_tokens, out_tokens, vec, vec, mat, vec, vec, mat, vec, vec, vec, vec, mat, vec)
        + (mat, vec, vec)
    )
    return jax.shard_map(
        on_device, mesh=mesh, in_specs=in_specs, out_specs=out_specs, check_vma=False
    )
```
